32 devices in a mesh: uv: 4 (over z), chan: 8 (over y, x, core).
Axes of the slice: x: 2, y: 2, z: 4, core: 2. Of those that a mesh axis runs over, the one named last changes fastest.
Arguments:
- visibility: bfloat16 [2, 512, 32, 4096], P(None, 'chan', 'uv'), may hold values from -6 to 6
- eigen_basis: bfloat16 [512, 512], P('chan'), may hold values from -0.25 to 0.25
- eigenvalues: float32 [512], replicated, may hold values from 0.01 to 100
- noise_power: float32 [32], P('uv'), may hold values from 0.1 to 10
Outputs:
- image_cube: bfloat16 [2, 512, 32, 4096], P(None, ('uv', 'chan'))
The draws below stay inside these ranges and needn't reach their ends.
All inputs are finite; a program needn't handle non-finite values.
Results may differ from the reference program's by a relative error of at most 0.019.
Values may be sent and summed in bfloat16 or wider, within the bound.
No kernel may reach another device: no remote copies, remote signals or barrier semaphores. Data moves between devices by JAX's collectives and lax.ppermute only.
A program may use at most 128 MiB of HBM per device.

```python
import math
import jax
import jax.numpy as jnp
from jax import lax

NCH = 512
NV = 4096
ROWS = 32


def level_of(key, dims, cuts, low, largest):
    gain = 1.0
    for axis_at, blocks in cuts:
        steps = jax.random.uniform(jax.random.fold_in(jax.random.fold_in(key, 6), axis_at), (blocks,), jnp.float32, low / len(cuts), largest / len(cuts))
        gain = gain * jnp.repeat(jnp.exp(steps), dims[axis_at] // blocks).reshape((-1,) + (1,) * (len(dims) - 1 - axis_at))
    return gain


def normal_values(stream_key, dims, width, limit, split=(), kind=jnp.bfloat16):
    factor_of = level_of(stream_key, dims, split, -0.22, 0.18) if split else 1.0
    result = jax.random.normal(stream_key, dims, jnp.float32) * width * factor_of
    return jnp.minimum(jnp.maximum(result, -limit), limit).astype(kind)


def setup_inputs(seed: int = 0) -> dict:
    key_list = jax.random.split(jax.random.key(seed), 5)
    return {
        "visibility": normal_values(key_list[0], (2, NCH, ROWS, NV), 1.0, 6.0, ((1, 8), (2, 4))),
        "eigen_basis": normal_values(key_list[1], (NCH, NCH), NCH ** -0.5, 0.25, ((0, 8),)),
        "eigenvalues": jnp.clip(jnp.exp(jax.random.uniform(key_list[2], (NCH,), jnp.float32, math.log(0.01), math.log(100.0))), 0.01, 100.0),
        "noise_power": jnp.clip(jnp.exp(math.log(10.0) - 4.6051702 * jax.random.uniform(key_list[3], (ROWS,), jnp.float32) ** level_of(key_list[3], (ROWS,), ((0, 4),), -0.2, 0.2)), 0.1, 10.0),
    }


def reference(visibility, eigen_basis, eigenvalues, noise_power):
    broad_basis = eigen_basis.astype(jnp.float32)

    def clean_row(row_index):
        slab_line_row = lax.dynamic_index_in_dim(visibility, row_index, 2, keepdims=False)
        noise_level = lax.dynamic_index_in_dim(noise_power, row_index, 0, keepdims=False)
        mode_amplitudes = jnp.einsum("wj,lwr->ljr", broad_basis, slab_line_row.astype(jnp.float32)).astype(jnp.bfloat16)
        mode_filter_gain = eigenvalues / (eigenvalues + noise_level)
        foreground_signal = (mode_filter_gain[None, :, None] * mode_amplitudes.astype(jnp.float32)).astype(jnp.bfloat16)
        rearranged_slab = jnp.einsum("fq,tqj->tfj", broad_basis, foreground_signal.astype(jnp.float32))
        return (slab_line_row.astype(jnp.float32) - rearranged_slab).astype(jnp.bfloat16)

    cleaned = lax.map(clean_row, jnp.arange(visibility.shape[2], dtype=jnp.int32))

    def image_plane(chan_index):
        one_plane = lax.dynamic_index_in_dim(cleaned, chan_index, 2, keepdims=False)
        complex_plane = lax.complex(one_plane[:, 0].astype(jnp.float32), one_plane[:, 1].astype(jnp.float32))
        imaged = jnp.fft.ifft2(complex_plane, norm="ortho")
        return jnp.stack([jnp.real(imaged), jnp.imag(imaged)]).astype(jnp.bfloat16)

    planes = lax.map(image_plane, jnp.arange(visibility.shape[1], dtype=jnp.int32))
    return jnp.transpose(planes, (1, 0, 2, 3))
```

```python
import functools
import math

import jax
import jax.numpy as jnp
import numpy as np
from jax import lax
from jax.experimental import pallas as pl
from jax.experimental.pallas import tpu as pltpu
from jax.sharding import PartitionSpec as P

LANES = 128
RADIX = 8
VMEM_BYTES = 56 * 1024 * 1024


def params():
    return pltpu.CompilerParams(vmem_limit_bytes=VMEM_BYTES)


def inner_table(size):
    position = np.arange(size)
    phase = 2.0 * np.pi * (np.outer(position, position) % size) / size
    cosine, sine = np.cos(phase), np.sin(phase)
    return np.block([[cosine, sine], [-sine, cosine]]).astype(jnp.bfloat16)


def twiddle_table(length):
    inner = length // RADIX
    phase = 2.0 * np.pi * np.outer(np.arange(RADIX), np.arange(inner)) / length
    return np.stack([np.cos(phase), np.sin(phase)], axis=1).astype(np.float32)


def lane_tables(length):
    span = LANES // RADIX
    table = np.zeros((RADIX, LANES, LANES), np.float32)
    for t in range(RADIX):
        for group in range(RADIX):
            y_lo = (group - t) % RADIX
            for h in range(span):
                table[t, group * span + h, h * RADIX + y_lo] = 1.0
    return table.astype(jnp.bfloat16)


def swap_table(major, minor):
    table = np.zeros((major * minor, major * minor), np.float32)
    for a in range(major):
        for b in range(minor):
            table[b * major + a, a * minor + b] = 1.0
    return table.astype(jnp.bfloat16)


def row_table(rows_dev, uv_count, group):
    total = rows_dev * uv_count
    position = np.arange(total)
    phase = 2.0 * np.pi * (np.outer(position, position) % total) / total
    cosine, sine = np.cos(phase), np.sin(phase)
    parts = np.array([[cosine, -sine], [sine, cosine]])
    parts = parts.reshape(2, 2, total, uv_count, rows_dev)
    eye = np.eye(group)
    table = np.einsum("tsxzu,cd->tcxzsdu", parts, eye)
    return table.reshape(2 * group * total, 2 * group * total).astype(jnp.bfloat16)


def butterfly8(re, im):
    def dft2(ar, ai, br, bi):
        return ar + br, ai + bi, ar - br, ai - bi

    def dft4(r, i):
        s0r, s0i, d0r, d0i = dft2(r[0], i[0], r[2], i[2])
        s1r, s1i, d1r, d1i = dft2(r[1], i[1], r[3], i[3])
        return (
            [s0r + s1r, d0r - d1i, s0r - s1r, d0r + d1i],
            [s0i + s1i, d0i + d1r, s0i - s1i, d0i - d1r],
        )

    er, ei = dft4(re[0::2], im[0::2])
    orr, oi = dft4(re[1::2], im[1::2])
    half = math.sqrt(0.5)
    turned_r = [orr[0], (orr[1] - oi[1]) * half, -oi[2], (-orr[3] - oi[3]) * half]
    turned_i = [oi[0], (orr[1] + oi[1]) * half, orr[2], (orr[3] - oi[3]) * half]
    out_r = [er[k] + turned_r[k] for k in range(4)] + [er[k] - turned_r[k] for k in range(4)]
    out_i = [ei[k] + turned_i[k] for k in range(4)] + [ei[k] - turned_i[k] for k in range(4)]
    return out_r, out_i


def column_kernel(x_ref, twiddle_ref, table_ref, out_ref, mid, wide):
    rows, length = x_ref.shape[1:]
    inner = length // RADIX
    width = out_ref.shape[3]
    step = 16

    def first(i, carry):
        at = pl.ds(pl.multiple_of(i * step, step), step)
        for block in range(inner // LANES):
            re, im = [], []
            for a in range(RADIX):
                lanes = slice(a * inner + block * LANES, a * inner + (block + 1) * LANES)
                re.append(x_ref[0, at, lanes].astype(jnp.float32))
                im.append(x_ref[1, at, lanes].astype(jnp.float32))
            re, im = butterfly8(re, im)
            lanes = slice(block * LANES, (block + 1) * LANES)
            for y_lo in range(RADIX):
                if y_lo == 0:
                    tr, ti = re[0], im[0]
                else:
                    cosine = twiddle_ref[y_lo, 0:1, lanes]
                    sine = twiddle_ref[y_lo, 1:2, lanes]
                    tr = re[y_lo] * cosine - im[y_lo] * sine
                    ti = re[y_lo] * sine + im[y_lo] * cosine
                mid[y_lo, at, lanes] = tr.astype(jnp.bfloat16)
                mid[y_lo, at, slice(inner + block * LANES, inner + (block + 1) * LANES)] = ti.astype(
                    jnp.bfloat16
                )
        return carry

    lax.fori_loop(0, rows // step, first, 0)
    for y_lo in range(RADIX):
        wide[y_lo] = jnp.dot(mid[y_lo], table_ref[...], preferred_element_type=jnp.float32)

    span = LANES // RADIX
    group_of = lax.broadcasted_iota(jnp.int32, (step, LANES), 1) // span

    def last(i, carry):
        at = pl.ds(pl.multiple_of(i * step, step), step)
        for part in range(2):
            for block in range(inner // LANES):
                lanes = slice(part * inner + block * LANES, part * inner + (block + 1) * LANES)
                tiles = []
                for y_lo in range(RADIX):
                    tile = wide[y_lo, at, lanes]
                    tiles.append(pltpu.roll(tile, y_lo * span, 1) if y_lo else tile)
                for t in range(RADIX):
                    value = tiles[(0 - t) % RADIX]
                    for group in range(1, RADIX):
                        value = jnp.where(group_of == group, tiles[(group - t) % RADIX], value)
                    start = (block * RADIX + t) * LANES
                    piece, lane = divmod(start, width)
                    out_ref[piece, part, at, lane : lane + LANES] = value.astype(jnp.bfloat16)
        return carry

    lax.fori_loop(0, rows // step, last, 0)


def column_transform(x, pieces):
    _, rows, length = x.shape
    inner = length // RADIX
    width = length // pieces
    block = math.gcd(rows, 64)
    return pl.pallas_call(
        column_kernel,
        grid=(rows // block,),
        in_specs=[
            pl.BlockSpec((2, block, length), lambda i: (0, i, 0)),
            pl.BlockSpec((RADIX, 2, inner), lambda i: (0, 0, 0)),
            pl.BlockSpec((2 * inner, 2 * inner), lambda i: (0, 0)),
        ],
        out_specs=pl.BlockSpec((pieces, 2, block, width), lambda i: (0, 0, i, 0)),
        out_shape=jax.ShapeDtypeStruct((pieces, 2, rows, width), jnp.bfloat16),
        scratch_shapes=[
            pltpu.VMEM((RADIX, block, 2 * inner), jnp.bfloat16),
            pltpu.VMEM((RADIX, block, 2 * inner), jnp.float32),
        ],
        compiler_params=params(),
        name="column_transform",
    )(x, jnp.asarray(twiddle_table(length)), jnp.asarray(inner_table(inner)))


def clean_kernel(group, x_ref, basis_ref, basis_t_ref, gain_ref, swap_ref, back_ref, lane_ref, out_ref, slab):
    sources, _, rows, width = x_ref.shape
    rows_dev, chans, _ = slab.shape
    tall = group * rows_dev
    for b in range(chans // group):
        if rows % tall == 0:
            source, row = divmod(b * tall, rows)
            tile = x_ref[source, 0, row : row + tall, :]
        else:
            take = tall // rows
            tile = x_ref[b * take : (b + 1) * take, 0].reshape(tall, width)
        turned = jnp.dot(swap_ref[...], tile, preferred_element_type=jnp.float32)
        slab[:, b * group : (b + 1) * group, :] = turned.astype(jnp.bfloat16).reshape(
            rows_dev, group, width
        )
    for u in range(rows_dev):
        line = slab[u]
        amps = jnp.dot(basis_t_ref[...], line, preferred_element_type=jnp.float32)
        amps = amps.astype(jnp.bfloat16).astype(jnp.float32)
        front = (gain_ref[:, u : u + 1] * amps).astype(jnp.bfloat16)
        drop = jnp.dot(basis_ref[...], front, preferred_element_type=jnp.float32)
        slab[u] = (line.astype(jnp.float32) - drop).astype(jnp.bfloat16)
    out_rows = out_ref.shape[2]
    for b in range(chans // group):
        tile = slab[:, b * group : (b + 1) * group, :].reshape(tall, width)
        turned = jnp.dot(back_ref[...], tile, preferred_element_type=jnp.float32).astype(jnp.bfloat16)
        for k in range(width // LANES):
            lanes = slice(k * LANES, (k + 1) * LANES)
            value = jnp.dot(turned[:, lanes], lane_ref[k], preferred_element_type=jnp.float32)
            if out_rows % tall == 0:
                target, row = divmod(b * tall, out_rows)
                out_ref[target, 0, row : row + tall, lanes] = value.astype(jnp.bfloat16)
            else:
                take = tall // out_rows
                out_ref[b * take : (b + 1) * take, 0, :, lanes] = value.reshape(
                    take, out_rows, LANES
                ).astype(jnp.bfloat16)


def clean(x, basis, gain, lane_table, targets, rows_dev):
    sources, _, rows, width = x.shape
    chans = basis.shape[0]
    group = 256 // rows_dev
    tile = min(width, 256)
    out_rows = chans * rows_dev // targets
    swap = swap_table(group, rows_dev)
    per_tile = tile // LANES
    return pl.pallas_call(
        functools.partial(clean_kernel, group),
        grid=(2, width // tile),
        in_specs=[
            pl.BlockSpec((sources, 1, rows, tile), lambda s, i: (0, s, 0, i)),
            pl.BlockSpec(basis.shape, lambda s, i: (0, 0)),
            pl.BlockSpec(basis.shape, lambda s, i: (0, 0)),
            pl.BlockSpec(gain.shape, lambda s, i: (0, 0)),
            pl.BlockSpec(swap.shape, lambda s, i: (0, 0)),
            pl.BlockSpec(swap.shape, lambda s, i: (0, 0)),
            pl.BlockSpec((per_tile, LANES, LANES), lambda s, i: (i, 0, 0)),
        ],
        out_specs=pl.BlockSpec((targets, 1, out_rows, tile), lambda s, i: (0, s, 0, i)),
        out_shape=jax.ShapeDtypeStruct((targets, 2, out_rows, width), jnp.bfloat16),
        scratch_shapes=[pltpu.VMEM((rows_dev, chans, tile), jnp.bfloat16)],
        compiler_params=params(),
        name="clean",
    )(x, basis, basis.T, gain, jnp.asarray(swap), jnp.asarray(np.ascontiguousarray(swap.T)), lane_table)


def row_kernel(scale, x_ref, table_ref, out_ref):
    z, _, parts, rows, width = x_ref.shape
    tall = z * parts * rows
    if rows % 16 == 0:
        tile = x_ref[:, 0].reshape(tall, width)
    else:
        tile = x_ref[:, 0].astype(jnp.float32).reshape(tall, width).astype(jnp.bfloat16)
    value = jnp.dot(table_ref[...], tile, preferred_element_type=jnp.float32) * scale
    out_ref[...] = value.reshape(out_ref.shape).astype(jnp.bfloat16)


def row_transform(x, chans, rows_dev):
    z, pieces, parts, rows, width = x.shape
    total = z * rows_dev
    length = pieces * width
    group = min(chans, max(1, 256 // (2 * total)))
    table = row_table(rows_dev, z, group)
    scale = 1.0 / math.sqrt(total * length)
    return pl.pallas_call(
        functools.partial(row_kernel, scale),
        grid=(chans // group, pieces),
        in_specs=[
            pl.BlockSpec((z, 1, 2, group * rows_dev, width), lambda c, j: (0, j, 0, c, 0)),
            pl.BlockSpec(table.shape, lambda c, j: (0, 0)),
        ],
        out_specs=pl.BlockSpec((2, group, total, width), lambda c, j: (0, c, 0, j)),
        out_shape=jax.ShapeDtypeStruct((2, chans, total, length), jnp.bfloat16),
        compiler_params=params(),
        name="row_transform",
    )(x, jnp.asarray(table))


def shards(visibility, eigen_basis, eigenvalues, noise_power):
    uv_count = lax.axis_size("uv")
    chan_count = lax.axis_size("chan")
    _, chans, rows_dev, length = visibility.shape
    width = length // chan_count
    out_chans = chans // uv_count
    flat = visibility.reshape(2, chans * rows_dev, length)
    pieces = column_transform(flat, chan_count)
    cells = lax.all_to_all(pieces, "chan", split_axis=0, concat_axis=0, tiled=True)
    basis = lax.all_gather(eigen_basis, "chan", axis=0, tiled=True)
    gain = eigenvalues[:, None] / (eigenvalues[:, None] + noise_power[None, :])
    per_piece = width // LANES
    first_tile = lax.rem(lax.axis_index("chan") * per_piece, RADIX)
    lanes = jnp.concatenate([jnp.asarray(lane_tables(length))] * 2, axis=0)
    lane_table = lax.dynamic_slice_in_dim(lanes, first_tile, per_piece, axis=0)
    cleaned = clean(cells, basis, gain, lane_table, uv_count * chan_count, rows_dev)
    planes = lax.all_to_all(cleaned, ("uv", "chan"), split_axis=0, concat_axis=0, tiled=True)
    planes = planes.reshape(uv_count, chan_count, 2, out_chans * rows_dev, width)
    return row_transform(planes, out_chans, rows_dev)


def solution(mesh):
    in_specs = (P(None, "chan", "uv", None), P("chan", None), P(), P("uv"))
    out_specs = P(None, ("uv", "chan"), None, None)
    return jax.shard_map(shards, mesh=mesh, in_specs=in_specs, out_specs=out_specs, check_vma=False)
```

```python
import functools
import math

import jax
import jax.numpy as jnp
import numpy as np
from jax import lax
from jax.experimental import pallas as pl
from jax.experimental.pallas import tpu as pltpu
from jax.sharding import PartitionSpec as P

LANES = 128
RADIX = 8
VMEM_BYTES = 56 * 1024 * 1024


def params():
    return pltpu.CompilerParams(vmem_limit_bytes=VMEM_BYTES)


def inner_table(size):
    position = np.arange(size)
    phase = 2.0 * np.pi * (np.outer(position, position) % size) / size
    cosine, sine = np.cos(phase), np.sin(phase)
    return np.block([[cosine, sine], [-sine, cosine]]).astype(jnp.bfloat16)


def twiddle_table(length):
    inner = length // RADIX
    phase = 2.0 * np.pi * np.outer(np.arange(RADIX), np.arange(inner)) / length
    return np.stack([np.cos(phase), np.sin(phase)], axis=1).astype(np.float32)


def lane_tables(length):
    span = LANES // RADIX
    table = np.zeros((RADIX, LANES, LANES), np.float32)
    for t in range(RADIX):
        for group in range(RADIX):
            y_lo = (group - t) % RADIX
            for h in range(span):
                table[t, group * span + h, h * RADIX + y_lo] = 1.0
    return table.astype(jnp.bfloat16)


def swap_table(major, minor):
    table = np.zeros((major * minor, major * minor), np.float32)
    for a in range(major):
        for b in range(minor):
            table[b * major + a, a * minor + b] = 1.0
    return table.astype(jnp.bfloat16)


def row_tables(rows_dev, uv_count, group):
    total = rows_dev * uv_count
    position = np.arange(total)
    phase = 2.0 * np.pi * (np.outer(position, position) % total) / total
    cosine, sine = np.cos(phase), np.sin(phase)
    parts = np.array([[cosine, -sine], [sine, cosine]])
    parts = parts.reshape(2, 2, total, uv_count, rows_dev)
    eye = np.eye(group)
    size = 2 * group * total
    tables = []
    for at in range(uv_count):
        order = (at - np.arange(uv_count)) % uv_count
        table = np.einsum("tsxzu,cd->tcxzsdu", parts[:, :, :, order], eye)
        tables.append(table.reshape(size, size).astype(jnp.bfloat16))
    return np.stack(tables)


def butterfly8(re, im):
    def dft2(ar, ai, br, bi):
        return ar + br, ai + bi, ar - br, ai - bi

    def dft4(r, i):
        s0r, s0i, d0r, d0i = dft2(r[0], i[0], r[2], i[2])
        s1r, s1i, d1r, d1i = dft2(r[1], i[1], r[3], i[3])
        return (
            [s0r + s1r, d0r - d1i, s0r - s1r, d0r + d1i],
            [s0i + s1i, d0i + d1r, s0i - s1i, d0i - d1r],
        )

    er, ei = dft4(re[0::2], im[0::2])
    orr, oi = dft4(re[1::2], im[1::2])
    half = math.sqrt(0.5)
    turned_r = [orr[0], (orr[1] - oi[1]) * half, -oi[2], (-orr[3] - oi[3]) * half]
    turned_i = [oi[0], (orr[1] + oi[1]) * half, orr[2], (orr[3] - oi[3]) * half]
    out_r = [er[k] + turned_r[k] for k in range(4)] + [er[k] - turned_r[k] for k in range(4)]
    out_i = [ei[k] + turned_i[k] for k in range(4)] + [ei[k] - turned_i[k] for k in range(4)]
    return out_r, out_i


def column_kernel(x_ref, twiddle_ref, table_ref, *refs):
    *out_refs, mid, wide = refs
    rows, length = x_ref.shape[1:]
    inner = length // RADIX
    per_piece = len(out_refs)
    step = 16

    def first(i, carry):
        at = pl.ds(pl.multiple_of(i * step, step), step)
        for block in range(inner // LANES):
            re, im = [], []
            for a in range(RADIX):
                lanes = slice(a * inner + block * LANES, a * inner + (block + 1) * LANES)
                re.append(x_ref[0, at, lanes].astype(jnp.float32))
                im.append(x_ref[1, at, lanes].astype(jnp.float32))
            re, im = butterfly8(re, im)
            lanes = slice(block * LANES, (block + 1) * LANES)
            other = slice(inner + block * LANES, inner + (block + 1) * LANES)
            for y_lo in range(RADIX):
                if y_lo == 0:
                    tr, ti = re[0], im[0]
                else:
                    cosine = twiddle_ref[y_lo, 0:1, lanes]
                    sine = twiddle_ref[y_lo, 1:2, lanes]
                    tr = re[y_lo] * cosine - im[y_lo] * sine
                    ti = re[y_lo] * sine + im[y_lo] * cosine
                mid[y_lo, at, lanes] = tr.astype(jnp.bfloat16)
                mid[y_lo, at, other] = ti.astype(jnp.bfloat16)
        return carry

    lax.fori_loop(0, rows // step, first, 0)
    wide[...] = jnp.dot(
        mid[...].reshape(RADIX * rows, 2 * inner), table_ref[...], preferred_element_type=jnp.float32
    ).reshape(wide.shape)

    span = LANES // RADIX
    group_of = lax.broadcasted_iota(jnp.int32, (step, LANES), 1) // span

    def last(i, carry):
        at = pl.ds(pl.multiple_of(i * step, step), step)
        for part in range(2):
            for block in range(inner // LANES):
                lanes = slice(part * inner + block * LANES, part * inner + (block + 1) * LANES)
                tiles = []
                for y_lo in range(RADIX):
                    tile = wide[y_lo, at, lanes]
                    tiles.append(pltpu.roll(tile, y_lo * span, 1) if y_lo else tile)
                for t in range(RADIX):
                    value = tiles[(0 - t) % RADIX]
                    for group in range(1, RADIX):
                        value = jnp.where(group_of == group, tiles[(group - t) % RADIX], value)
                    piece, chunk = divmod(block * RADIX + t, per_piece)
                    out_refs[chunk][piece, part, at, :] = value.astype(jnp.bfloat16)
        return carry

    lax.fori_loop(0, rows // step, last, 0)


def column_transform(x, pieces):
    _, rows, length = x.shape
    inner = length // RADIX
    per_piece = length // pieces // LANES
    block = math.gcd(rows, 64)
    return pl.pallas_call(
        column_kernel,
        grid=(rows // block,),
        in_specs=[
            pl.BlockSpec((2, block, length), lambda i: (0, i, 0)),
            pl.BlockSpec((RADIX, 2, inner), lambda i: (0, 0, 0)),
            pl.BlockSpec((2 * inner, 2 * inner), lambda i: (0, 0)),
        ],
        out_specs=[pl.BlockSpec((pieces, 2, block, LANES), lambda i: (0, 0, i, 0))] * per_piece,
        out_shape=[jax.ShapeDtypeStruct((pieces, 2, rows, LANES), jnp.bfloat16)] * per_piece,
        scratch_shapes=[
            pltpu.VMEM((RADIX, block, 2 * inner), jnp.bfloat16),
            pltpu.VMEM((RADIX, block, 2 * inner), jnp.float32),
        ],
        compiler_params=params(),
        cost_estimate=pl.CostEstimate(
            flops=16 * rows * length * inner, bytes_accessed=8 * rows * length, transcendentals=0
        ),
        name="column_transform",
    )(x, jnp.asarray(twiddle_table(length)), jnp.asarray(inner_table(inner)))


def clean_kernel(group, at_ref, x_ref, basis_ref, basis_t_ref, gain_ref, swap_ref, back_ref, lane_ref, *refs):
    *out_refs, slab = refs
    sources, _, rows, _ = x_ref.shape
    chans = slab.shape[0]
    rows_dev = slab.shape[1] // LANES
    tall = group * rows_dev
    for b in range(chans // group):
        if rows % tall == 0:
            source, row = divmod(b * tall, rows)
            tile = x_ref[source, 0, row : row + tall, :]
        else:
            take = tall // rows
            tile = x_ref[b * take : (b + 1) * take, 0].reshape(tall, LANES)
        tile = jnp.dot(tile, lane_ref[...], preferred_element_type=jnp.float32).astype(jnp.bfloat16)
        turned = jnp.dot(swap_ref[...], tile, preferred_element_type=jnp.float32).astype(jnp.bfloat16)
        for u in range(rows_dev):
            slab[b * group : (b + 1) * group, u * LANES : (u + 1) * LANES] = turned[
                u * group : (u + 1) * group
            ]
    pair = math.gcd(rows_dev, 2)
    for first in range(0, rows_dev, pair):
        lanes = slice(first * LANES, (first + pair) * LANES)
        line = slab[:, lanes]
        amps = jnp.dot(basis_t_ref[...], line, preferred_element_type=jnp.float32)
        amps = amps.astype(jnp.bfloat16).astype(jnp.float32)
        front = jnp.concatenate(
            [
                gain_ref[:, first + k : first + k + 1] * amps[:, k * LANES : (k + 1) * LANES]
                for k in range(pair)
            ],
            axis=1,
        ).astype(jnp.bfloat16)
        drop = jnp.dot(basis_ref[...], front, preferred_element_type=jnp.float32)
        slab[:, lanes] = (line.astype(jnp.float32) - drop).astype(jnp.bfloat16)
    steps = len(out_refs)
    share = chans // steps
    out_rows = out_refs[0].shape[2]
    for step, out_ref in enumerate(out_refs):
        start = lax.rem(at_ref[0] + step, steps) * share
        for b in range(share // group):
            channels = pl.ds(pl.multiple_of(start + b * group, group), group)
            tile = jnp.concatenate(
                [slab[channels, u * LANES : (u + 1) * LANES] for u in range(rows_dev)], axis=0
            )
            value = jnp.dot(back_ref[...], tile, preferred_element_type=jnp.float32)
            if out_rows % tall == 0:
                target, row = divmod(b * tall, out_rows)
                out_ref[target, 0, row : row + tall, :] = value.astype(jnp.bfloat16)
            else:
                take = tall // out_rows
                out_ref[b * take : (b + 1) * take, 0] = value.reshape(
                    take, out_rows, LANES
                ).astype(jnp.bfloat16)


def clean(at, x, basis, gain, lane_table, steps, targets, rows_dev):
    sources, _, rows, _ = x.shape
    chans = basis.shape[0]
    group = 256 // rows_dev
    out_rows = chans * rows_dev // (targets * steps)
    swap = swap_table(group, rows_dev)
    whole = lambda s, at: (0, 0)
    return pl.pallas_call(
        functools.partial(clean_kernel, group),
        grid_spec=pltpu.PrefetchScalarGridSpec(
            num_scalar_prefetch=1,
            grid=(2,),
            in_specs=[
                pl.BlockSpec((sources, 1, rows, LANES), lambda s, at: (0, s, 0, 0)),
                pl.BlockSpec(basis.shape, whole),
                pl.BlockSpec(basis.shape, whole),
                pl.BlockSpec(gain.shape, whole),
                pl.BlockSpec(swap.shape, whole),
                pl.BlockSpec(swap.shape, whole),
                pl.BlockSpec((LANES, LANES), whole),
            ],
            out_specs=[
                pl.BlockSpec((targets, 1, out_rows, LANES), lambda s, at: (0, s, 0, 0))
            ] * steps,
            scratch_shapes=[pltpu.VMEM((chans, rows_dev * LANES), jnp.bfloat16)],
        ),
        out_shape=[jax.ShapeDtypeStruct((targets, 2, out_rows, LANES), jnp.bfloat16)] * steps,
        compiler_params=params(),
        cost_estimate=pl.CostEstimate(
            flops=12 * chans * chans * rows_dev * LANES,
            bytes_accessed=8 * chans * rows_dev * LANES,
            transcendentals=0,
        ),
        name="clean",
    )(at, x, basis, basis.T, gain, jnp.asarray(swap), jnp.asarray(np.ascontiguousarray(swap.T)), lane_table)


def row_kernel(scale, group, *refs):
    *x_refs, table_ref, out_ref = refs
    targets, _, chans, total, _ = out_ref.shape
    rows_dev = x_refs[0].shape[2] // chans
    tall = group * rows_dev
    for target in range(targets):
        for c in range(chans // group):
            rows = slice(c * tall, (c + 1) * tall)
            parts = [x_ref[target, s, rows, :] for x_ref in x_refs for s in range(2)]
            if tall % 16:
                parts = [part.astype(jnp.float32) for part in parts]
            tile = jnp.concatenate(parts, axis=0).astype(jnp.bfloat16)
            value = jnp.dot(table_ref[...], tile, preferred_element_type=jnp.float32) * scale
            out_ref[target, :, c * group : (c + 1) * group] = value.reshape(
                2, group, total, LANES
            ).astype(jnp.bfloat16)


def row_transform(pieces, at, chans, rows_dev, length):
    steps = len(pieces)
    targets, _, rows, _ = pieces[0].shape
    total = steps * rows_dev
    group = min(chans, max(1, 256 // (2 * total)))
    tables = jnp.asarray(row_tables(rows_dev, steps, group))
    table = lax.dynamic_index_in_dim(tables, at[0], 0, keepdims=False)
    scale = 1.0 / math.sqrt(total * length)
    block = math.gcd(targets, 2)
    return pl.pallas_call(
        functools.partial(row_kernel, scale, group),
        grid=(targets // block,),
        in_specs=[pl.BlockSpec((block, 2, rows, LANES), lambda j: (j, 0, 0, 0))] * steps
        + [pl.BlockSpec(table.shape, lambda j: (0, 0))],
        out_specs=pl.BlockSpec((block, 2, chans, total, LANES), lambda j: (j, 0, 0, 0, 0)),
        out_shape=jax.ShapeDtypeStruct((targets, 2, chans, total, LANES), jnp.bfloat16),
        compiler_params=params(),
        cost_estimate=pl.CostEstimate(
            flops=1024 * targets * chans * total * LANES,
            bytes_accessed=8 * targets * chans * total * LANES,
            transcendentals=0,
        ),
        name="row_transform",
    )(*pieces, table)


def place_kernel(x_ref, *refs):
    refs[-1][...] = x_ref[0]


def place(x, chunk, per_piece, held):
    pieces, _, chans, total, _ = x.shape
    shape = jax.ShapeDtypeStruct((2, chans, total, pieces * per_piece * LANES), jnp.bfloat16)
    return pl.pallas_call(
        place_kernel,
        grid=(pieces,),
        in_specs=[pl.BlockSpec((1, 2, chans, total, LANES), lambda j: (j, 0, 0, 0, 0))]
        + [pl.BlockSpec(memory_space=pl.ANY)] * len(held),
        out_specs=pl.BlockSpec((2, chans, total, LANES), lambda j: (0, 0, 0, j * per_piece + chunk)),
        out_shape=shape,
        input_output_aliases={1: 0} if held else {},
        compiler_params=params(),
        cost_estimate=pl.CostEstimate(
            flops=0, bytes_accessed=8 * pieces * chans * total * LANES, transcendentals=0
        ),
        name="place",
    )(x, *held)


def shards(visibility, eigen_basis, eigenvalues, noise_power):
    uv_count = lax.axis_size("uv")
    chan_count = lax.axis_size("chan")
    _, chans, rows_dev, length = visibility.shape
    per_piece = length // chan_count // LANES
    out_chans = chans // uv_count
    at = lax.axis_index("uv").astype(jnp.int32).reshape(1)
    basis = lax.all_gather(eigen_basis, "chan", axis=0, tiled=True)
    gain = eigenvalues[:, None] / (eigenvalues[:, None] + noise_power[None, :])
    lane_table = jnp.asarray(lane_tables(length))
    chunks = column_transform(visibility.reshape(2, chans * rows_dev, length), chan_count)
    cells = [
        lax.all_to_all(chunk, "chan", split_axis=0, concat_axis=0, tiled=True) for chunk in chunks
    ]
    held = []
    for k in range(per_piece):
        tile = lax.rem(lax.axis_index("chan") * per_piece + k, RADIX)
        lanes = lax.dynamic_index_in_dim(lane_table, tile, 0, keepdims=False)
        cleaned = clean(at, cells[k], basis, gain, lanes, uv_count, chan_count, rows_dev)
        pieces = [cleaned[0]] + [
            lax.ppermute(
                cleaned[step], "uv", [(z, (z + step) % uv_count) for z in range(uv_count)]
            )
            for step in range(1, uv_count)
        ]
        lines = row_transform(pieces, at, out_chans, rows_dev, length)
        returned = lax.all_to_all(lines, "chan", split_axis=0, concat_axis=0, tiled=True)
        held = [place(returned, k, per_piece, held)]
    return held[0]


def solution(mesh):
    in_specs = (P(None, "chan", "uv", None), P("chan", None), P(), P("uv"))
    out_specs = P(None, ("uv", "chan"), None, None)
    return jax.shard_map(shards, mesh=mesh, in_specs=in_specs, out_specs=out_specs, check_vma=False)
```

```python
import functools
import math

import jax
import jax.numpy as jnp
import numpy as np
from jax import lax
from jax.experimental import pallas as pl
from jax.experimental.pallas import tpu as pltpu
from jax.sharding import PartitionSpec as P

LANES = 128
RADIX = 8
VMEM_BYTES = 56 * 1024 * 1024


def params():
    return pltpu.CompilerParams(vmem_limit_bytes=VMEM_BYTES)


def inner_table(size):
    position = np.arange(size)
    phase = 2.0 * np.pi * (np.outer(position, position) % size) / size
    cosine, sine = np.cos(phase), np.sin(phase)
    return np.block([[cosine, sine], [-sine, cosine]]).astype(jnp.bfloat16)


def twiddle_table(length):
    inner = length // RADIX
    phase = 2.0 * np.pi * np.outer(np.arange(RADIX), np.arange(inner)) / length
    return np.stack([np.cos(phase), np.sin(phase)], axis=1).astype(np.float32)


def lane_tables(length):
    span = LANES // RADIX
    table = np.zeros((RADIX, LANES, LANES), np.float32)
    for t in range(RADIX):
        for group in range(RADIX):
            y_lo = (group - t) % RADIX
            for h in range(span):
                table[t, group * span + h, h * RADIX + y_lo] = 1.0
    return table.astype(jnp.bfloat16)


def swap_table(major, minor):
    table = np.zeros((major * minor, major * minor), np.float32)
    for a in range(major):
        for b in range(minor):
            table[b * major + a, a * minor + b] = 1.0
    return table.astype(jnp.bfloat16)


def row_tables(rows_dev, uv_count, group):
    total = rows_dev * uv_count
    position = np.arange(total)
    phase = 2.0 * np.pi * (np.outer(position, position) % total) / total
    cosine, sine = np.cos(phase), np.sin(phase)
    parts = np.array([[cosine, -sine], [sine, cosine]])
    parts = parts.reshape(2, 2, total, uv_count, rows_dev)
    eye = np.eye(group)
    size = 2 * group * total
    tables = []
    for at in range(uv_count):
        order = (at - np.arange(uv_count)) % uv_count
        table = np.einsum("tsxzu,cd->tcxzsdu", parts[:, :, :, order], eye)
        tables.append(table.reshape(size, size).astype(jnp.bfloat16))
    return np.stack(tables)


def butterfly8(re, im):
    def dft2(ar, ai, br, bi):
        return ar + br, ai + bi, ar - br, ai - bi

    def dft4(r, i):
        s0r, s0i, d0r, d0i = dft2(r[0], i[0], r[2], i[2])
        s1r, s1i, d1r, d1i = dft2(r[1], i[1], r[3], i[3])
        return (
            [s0r + s1r, d0r - d1i, s0r - s1r, d0r + d1i],
            [s0i + s1i, d0i + d1r, s0i - s1i, d0i - d1r],
        )

    er, ei = dft4(re[0::2], im[0::2])
    orr, oi = dft4(re[1::2], im[1::2])
    half = math.sqrt(0.5)
    turned_r = [orr[0], (orr[1] - oi[1]) * half, -oi[2], (-orr[3] - oi[3]) * half]
    turned_i = [oi[0], (orr[1] + oi[1]) * half, orr[2], (orr[3] - oi[3]) * half]
    out_r = [er[k] + turned_r[k] for k in range(4)] + [er[k] - turned_r[k] for k in range(4)]
    out_i = [ei[k] + turned_i[k] for k in range(4)] + [ei[k] - turned_i[k] for k in range(4)]
    return out_r, out_i


def column_kernel(x_ref, twiddle_ref, table_ref, *refs):
    *out_refs, mid, wide = refs
    rows, length = x_ref.shape[1:]
    inner = length // RADIX
    per_piece = len(out_refs)
    step = 16

    def first(i, carry):
        at = pl.ds(pl.multiple_of(i * step, step), step)
        for block in range(inner // LANES):
            re, im = [], []
            for a in range(RADIX):
                lanes = slice(a * inner + block * LANES, a * inner + (block + 1) * LANES)
                re.append(x_ref[0, at, lanes].astype(jnp.float32))
                im.append(x_ref[1, at, lanes].astype(jnp.float32))
            re, im = butterfly8(re, im)
            lanes = slice(block * LANES, (block + 1) * LANES)
            other = slice(inner + block * LANES, inner + (block + 1) * LANES)
            for y_lo in range(RADIX):
                if y_lo == 0:
                    tr, ti = re[0], im[0]
                else:
                    cosine = twiddle_ref[y_lo, 0:1, lanes]
                    sine = twiddle_ref[y_lo, 1:2, lanes]
                    tr = re[y_lo] * cosine - im[y_lo] * sine
                    ti = re[y_lo] * sine + im[y_lo] * cosine
                mid[y_lo, at, lanes] = tr.astype(jnp.bfloat16)
                mid[y_lo, at, other] = ti.astype(jnp.bfloat16)
        return carry

    lax.fori_loop(0, rows // step, first, 0)
    wide[...] = jnp.dot(
        mid[...].reshape(RADIX * rows, 2 * inner), table_ref[...], preferred_element_type=jnp.float32
    ).reshape(wide.shape)

    span = LANES // RADIX
    group_of = lax.broadcasted_iota(jnp.int32, (step, LANES), 1) // span

    def last(i, carry):
        at = pl.ds(pl.multiple_of(i * step, step), step)
        for part in range(2):
            for block in range(inner // LANES):
                lanes = slice(part * inner + block * LANES, part * inner + (block + 1) * LANES)
                tiles = []
                for y_lo in range(RADIX):
                    tile = wide[y_lo, at, lanes]
                    tiles.append(pltpu.roll(tile, y_lo * span, 1) if y_lo else tile)
                for t in range(RADIX):
                    value = tiles[(0 - t) % RADIX]
                    for group in range(1, RADIX):
                        value = jnp.where(group_of == group, tiles[(group - t) % RADIX], value)
                    piece, chunk = divmod(block * RADIX + t, per_piece)
                    out_refs[chunk][piece, part, at, :] = value.astype(jnp.bfloat16)
        return carry

    lax.fori_loop(0, rows // step, last, 0)


def column_transform(x, pieces):
    _, rows, length = x.shape
    inner = length // RADIX
    per_piece = length // pieces // LANES
    block = math.gcd(rows, 64)
    return pl.pallas_call(
        column_kernel,
        grid=(rows // block,),
        in_specs=[
            pl.BlockSpec((2, block, length), lambda i: (0, i, 0)),
            pl.BlockSpec((RADIX, 2, inner), lambda i: (0, 0, 0)),
            pl.BlockSpec((2 * inner, 2 * inner), lambda i: (0, 0)),
        ],
        out_specs=[pl.BlockSpec((pieces, 2, block, LANES), lambda i: (0, 0, i, 0))] * per_piece,
        out_shape=[jax.ShapeDtypeStruct((pieces, 2, rows, LANES), jnp.bfloat16)] * per_piece,
        scratch_shapes=[
            pltpu.VMEM((RADIX, block, 2 * inner), jnp.bfloat16),
            pltpu.VMEM((RADIX, block, 2 * inner), jnp.float32),
        ],
        compiler_params=params(),
        cost_estimate=pl.CostEstimate(
            flops=16 * rows * length * inner, bytes_accessed=8 * rows * length, transcendentals=0
        ),
        name="column_transform",
    )(x, jnp.asarray(twiddle_table(length)), jnp.asarray(inner_table(inner)))


def clean_kernel(
    group, later, at_ref, x_ref, basis_ref, basis_t_ref, gain_ref, swap_ref, back_ref, lane_ref, *refs
):
    *out_refs, slab = refs[later:]
    out_refs = out_refs[: len(out_refs) - later]
    sources, _, rows, _ = x_ref.shape
    chans = slab.shape[0]
    rows_dev = slab.shape[1] // LANES
    tall = group * rows_dev
    for b in range(chans // group):
        if rows % tall == 0:
            source, row = divmod(b * tall, rows)
            tile = x_ref[source, 0, row : row + tall, :]
        else:
            take = tall // rows
            tile = x_ref[b * take : (b + 1) * take, 0].reshape(tall, LANES)
        tile = jnp.dot(tile, lane_ref[...], preferred_element_type=jnp.float32).astype(jnp.bfloat16)
        turned = jnp.dot(swap_ref[...], tile, preferred_element_type=jnp.float32).astype(jnp.bfloat16)
        for u in range(rows_dev):
            slab[b * group : (b + 1) * group, u * LANES : (u + 1) * LANES] = turned[
                u * group : (u + 1) * group
            ]
    pair = math.gcd(rows_dev, 2)
    for first in range(0, rows_dev, pair):
        lanes = slice(first * LANES, (first + pair) * LANES)
        line = slab[:, lanes]
        amps = jnp.dot(basis_t_ref[...], line, preferred_element_type=jnp.float32)
        amps = amps.astype(jnp.bfloat16).astype(jnp.float32)
        front = jnp.concatenate(
            [
                gain_ref[:, first + k : first + k + 1] * amps[:, k * LANES : (k + 1) * LANES]
                for k in range(pair)
            ],
            axis=1,
        ).astype(jnp.bfloat16)
        drop = jnp.dot(basis_ref[...], front, preferred_element_type=jnp.float32)
        slab[:, lanes] = (line.astype(jnp.float32) - drop).astype(jnp.bfloat16)
    steps = len(out_refs)
    share = chans // steps
    out_rows = out_refs[0].shape[2]
    for step, out_ref in enumerate(out_refs):
        start = lax.rem(at_ref[0] + step, steps) * share
        for b in range(share // group):
            channels = pl.ds(pl.multiple_of(start + b * group, group), group)
            tile = jnp.concatenate(
                [slab[channels, u * LANES : (u + 1) * LANES] for u in range(rows_dev)], axis=0
            )
            value = jnp.dot(back_ref[...], tile, preferred_element_type=jnp.float32)
            if out_rows % tall == 0:
                target, row = divmod(b * tall, out_rows)
                out_ref[target, 0, row : row + tall, :] = value.astype(jnp.bfloat16)
            else:
                take = tall // out_rows
                out_ref[b * take : (b + 1) * take, 0] = value.reshape(
                    take, out_rows, LANES
                ).astype(jnp.bfloat16)


def clean(at, x, basis, basis_t, gain, lane_table, steps, targets, rows_dev, later):
    sources, _, rows, _ = x.shape
    chans = basis.shape[0]
    group = 256 // rows_dev
    out_rows = chans * rows_dev // (targets * steps)
    swap = swap_table(group, rows_dev)
    whole = lambda s, at: (0, 0)
    return pl.pallas_call(
        functools.partial(clean_kernel, group, len(later)),
        grid_spec=pltpu.PrefetchScalarGridSpec(
            num_scalar_prefetch=1,
            grid=(2,),
            in_specs=[
                pl.BlockSpec((sources, 1, rows, LANES), lambda s, at: (0, s, 0, 0)),
                pl.BlockSpec(basis.shape, whole),
                pl.BlockSpec(basis.shape, whole),
                pl.BlockSpec(gain.shape, whole),
                pl.BlockSpec(swap.shape, whole),
                pl.BlockSpec(swap.shape, whole),
                pl.BlockSpec((LANES, LANES), whole),
            ]
            + [pl.BlockSpec(memory_space=pl.ANY)] * len(later),
            out_specs=[
                pl.BlockSpec((targets, 1, out_rows, LANES), lambda s, at: (0, s, 0, 0))
            ] * steps
            + [pl.BlockSpec(memory_space=pl.ANY)] * len(later),
            scratch_shapes=[pltpu.VMEM((chans, rows_dev * LANES), jnp.bfloat16)],
        ),
        out_shape=[jax.ShapeDtypeStruct((targets, 2, out_rows, LANES), jnp.bfloat16)] * steps
        + [jax.ShapeDtypeStruct(a.shape, a.dtype) for a in later],
        input_output_aliases={8 + i: steps + i for i in range(len(later))},
        compiler_params=params(),
        cost_estimate=pl.CostEstimate(
            flops=12 * chans * chans * rows_dev * LANES,
            bytes_accessed=8 * chans * rows_dev * LANES,
            transcendentals=0,
        ),
        name="clean",
    )(
        at,
        x,
        basis,
        basis_t,
        gain,
        jnp.asarray(swap),
        jnp.asarray(np.ascontiguousarray(swap.T)),
        lane_table,
        *later,
    )


def row_kernel(scale, group, steps, *refs):
    x_refs, table_ref, out_ref = refs[:steps], refs[steps], refs[-1]
    targets, _, chans, total, _ = out_ref.shape
    rows_dev = x_refs[0].shape[2] // chans
    tall = group * rows_dev
    for target in range(targets):
        for c in range(chans // group):
            rows = slice(c * tall, (c + 1) * tall)
            parts = [x_ref[target, s, rows, :] for x_ref in x_refs for s in range(2)]
            if tall % 16:
                parts = [part.astype(jnp.float32) for part in parts]
            tile = jnp.concatenate(parts, axis=0).astype(jnp.bfloat16)
            value = jnp.dot(table_ref[...], tile, preferred_element_type=jnp.float32) * scale
            out_ref[target, :, c * group : (c + 1) * group] = value.reshape(
                2, group, total, LANES
            ).astype(jnp.bfloat16)


def row_transform(pieces, at, chans, rows_dev, length, after):
    steps = len(pieces)
    targets, _, rows, _ = pieces[0].shape
    total = steps * rows_dev
    group = min(chans, max(1, 256 // (2 * total)))
    tables = jnp.asarray(row_tables(rows_dev, steps, group))
    table = lax.dynamic_index_in_dim(tables, at[0], 0, keepdims=False)
    scale = 1.0 / math.sqrt(total * length)
    block = math.gcd(targets, 2)
    return pl.pallas_call(
        functools.partial(row_kernel, scale, group, steps),
        grid=(targets // block,),
        in_specs=[pl.BlockSpec((block, 2, rows, LANES), lambda j: (j, 0, 0, 0))] * steps
        + [pl.BlockSpec(table.shape, lambda j: (0, 0))]
        + [pl.BlockSpec(memory_space=pl.ANY)] * len(after),
        out_specs=pl.BlockSpec((block, 2, chans, total, LANES), lambda j: (j, 0, 0, 0, 0)),
        out_shape=jax.ShapeDtypeStruct((targets, 2, chans, total, LANES), jnp.bfloat16),
        compiler_params=params(),
        cost_estimate=pl.CostEstimate(
            flops=1024 * targets * chans * total * LANES,
            bytes_accessed=8 * targets * chans * total * LANES,
            transcendentals=0,
        ),
        name="row_transform",
    )(*pieces, table, *after)


def place_kernel(x_ref, *refs):
    refs[-1][...] = x_ref[0]


def place(x, chunk, per_piece, held):
    pieces, _, chans, total, _ = x.shape
    shape = jax.ShapeDtypeStruct((2, chans, total, pieces * per_piece * LANES), jnp.bfloat16)
    return pl.pallas_call(
        place_kernel,
        grid=(pieces,),
        in_specs=[pl.BlockSpec((1, 2, chans, total, LANES), lambda j: (j, 0, 0, 0, 0))]
        + [pl.BlockSpec(memory_space=pl.ANY)] * len(held),
        out_specs=pl.BlockSpec((2, chans, total, LANES), lambda j: (0, 0, 0, j * per_piece + chunk)),
        out_shape=shape,
        input_output_aliases={1: 0} if held else {},
        compiler_params=params(),
        cost_estimate=pl.CostEstimate(
            flops=0, bytes_accessed=8 * pieces * chans * total * LANES, transcendentals=0
        ),
        name="place",
    )(x, *held)


def turn_kernel(basis_ref, _, out_ref, __):
    out_ref[...] = basis_ref[...].T


def turn(basis, later):
    return pl.pallas_call(
        turn_kernel,
        in_specs=[pl.BlockSpec(memory_space=pltpu.VMEM), pl.BlockSpec(memory_space=pl.ANY)],
        out_specs=[pl.BlockSpec(memory_space=pltpu.VMEM), pl.BlockSpec(memory_space=pl.ANY)],
        out_shape=[
            jax.ShapeDtypeStruct(basis.shape, basis.dtype),
            jax.ShapeDtypeStruct(later.shape, later.dtype),
        ],
        input_output_aliases={1: 1},
        compiler_params=params(),
        name="turn",
    )(basis, later)


def exchange(x):
    return lax.all_to_all(x, "chan", split_axis=0, concat_axis=0, tiled=True)


def shards(visibility, eigen_basis, eigenvalues, noise_power):
    uv_count = lax.axis_size("uv")
    chan_count = lax.axis_size("chan")
    _, chans, rows_dev, length = visibility.shape
    count = length // chan_count // LANES
    out_chans = chans // uv_count
    at = lax.axis_index("uv").astype(jnp.int32).reshape(1)
    basis = exchange(jnp.broadcast_to(eigen_basis, (chan_count,) + eigen_basis.shape))
    basis = basis.reshape(chan_count * chans, -1)
    gain = eigenvalues[:, None] / (eigenvalues[:, None] + noise_power[None, :])
    lane_table = jnp.asarray(lane_tables(length))
    chunks = list(column_transform(visibility.reshape(2, chans * rows_dev, length), chan_count))
    basis_t, chunks[0] = turn(basis, chunks[0])
    cells, cleaned, held = [], [], []
    for k in range(min(2, count)):
        cells.append(exchange(chunks[k]))
    for k in range(count):
        tile = lax.rem(lax.axis_index("chan") * count + k, RADIX)
        lanes = lax.dynamic_index_in_dim(lane_table, tile, 0, keepdims=False)
        result = clean(
            at, cells[k], basis, basis_t, gain, lanes, uv_count, chan_count, rows_dev, chunks[k + 2 : k + 3]
        )
        cleaned.append(result[:uv_count])
        if k + 2 < count:
            cells.append(exchange(result[uv_count]))
    for k in range(count):
        pieces = [cleaned[k][0]] + [
            lax.ppermute(
                cleaned[k][step], "uv", [(z, (z + step) % uv_count) for z in range(uv_count)]
            )
            for step in range(1, uv_count)
        ]
        after = [parts[0] for parts in cleaned[k + 2 : k + 3]] + cells[k + 3 : k + 4]
        lines = row_transform(pieces, at, out_chans, rows_dev, length, after)
        held = [place(exchange(lines), k, count, held)]
    return held[0]


def solution(mesh):
    in_specs = (P(None, "chan", "uv", None), P("chan", None), P(), P("uv"))
    out_specs = P(None, ("uv", "chan"), None, None)
    return jax.shard_map(shards, mesh=mesh, in_specs=in_specs, out_specs=out_specs, check_vma=False)
```

```python
import functools
import math

import jax
import jax.numpy as jnp
import numpy as np
from jax import lax
from jax.experimental import pallas as pl
from jax.experimental.pallas import tpu as pltpu
from jax.sharding import PartitionSpec as P

LANES = 128
RADIX = 8
PARTS = 2
VMEM_BYTES = 56 * 1024 * 1024


def params():
    return pltpu.CompilerParams(vmem_limit_bytes=VMEM_BYTES)


def inner_table(size):
    position = np.arange(size)
    phase = 2.0 * np.pi * (np.outer(position, position) % size) / size
    cosine, sine = np.cos(phase), np.sin(phase)
    return np.block([[cosine, sine], [-sine, cosine]]).astype(jnp.bfloat16)


def twiddle_table(length):
    inner = length // RADIX
    phase = 2.0 * np.pi * np.outer(np.arange(RADIX), np.arange(inner)) / length
    return np.stack([np.cos(phase), np.sin(phase)], axis=1).astype(np.float32)


def order_table():
    table = np.zeros((RADIX, LANES, LANES, RADIX), np.float32)
    for y_lo in range(RADIX):
        for y_hi in range(LANES):
            table[y_lo, y_hi, y_hi, y_lo] = 1.0
    return table.reshape(RADIX * LANES, RADIX * LANES).astype(jnp.bfloat16)


def swap_table(major, minor):
    table = np.zeros((major * minor, major * minor), np.float32)
    for a in range(major):
        for b in range(minor):
            table[b * major + a, a * minor + b] = 1.0
    return table.astype(jnp.bfloat16)


def row_tables(rows_dev, uv_count, group):
    total = rows_dev * uv_count
    position = np.arange(total)
    phase = 2.0 * np.pi * (np.outer(position, position) % total) / total
    cosine, sine = np.cos(phase), np.sin(phase)
    parts = np.array([[cosine, -sine], [sine, cosine]])
    parts = parts.reshape(2, 2, total, uv_count, rows_dev)
    eye = np.eye(group)
    size = 2 * group * total
    tables = []
    for at in range(uv_count):
        order = (at - np.arange(uv_count)) % uv_count
        table = np.einsum("tsxzu,cd->tcxzsdu", parts[:, :, :, order], eye)
        tables.append(table.reshape(size, size).astype(jnp.bfloat16))
    return np.stack(tables)


def butterfly8(re, im):
    def dft2(ar, ai, br, bi):
        return ar + br, ai + bi, ar - br, ai - bi

    def dft4(r, i):
        s0r, s0i, d0r, d0i = dft2(r[0], i[0], r[2], i[2])
        s1r, s1i, d1r, d1i = dft2(r[1], i[1], r[3], i[3])
        return (
            [s0r + s1r, d0r - d1i, s0r - s1r, d0r + d1i],
            [s0i + s1i, d0i + d1r, s0i - s1i, d0i - d1r],
        )

    er, ei = dft4(re[0::2], im[0::2])
    orr, oi = dft4(re[1::2], im[1::2])
    half = math.sqrt(0.5)
    turned_r = [orr[0], (orr[1] - oi[1]) * half, -oi[2], (-orr[3] - oi[3]) * half]
    turned_i = [oi[0], (orr[1] + oi[1]) * half, orr[2], (orr[3] - oi[3]) * half]
    out_r = [er[k] + turned_r[k] for k in range(4)] + [er[k] - turned_r[k] for k in range(4)]
    out_i = [ei[k] + turned_i[k] for k in range(4)] + [ei[k] - turned_i[k] for k in range(4)]
    return out_r, out_i


def column_kernel(held, x_ref, twiddle_ref, table_ref, *refs):
    *out_refs, mid = refs[held:]
    rows, length = x_ref.shape[1:]
    inner = length // RADIX
    step = 16
    for i in range(rows // step):
        at = slice(i * step, (i + 1) * step)
        for block in range(inner // LANES):
            re, im = [], []
            for a in range(RADIX):
                lanes = slice(a * inner + block * LANES, a * inner + (block + 1) * LANES)
                re.append(x_ref[0, at, lanes].astype(jnp.float32))
                im.append(x_ref[1, at, lanes].astype(jnp.float32))
            re, im = butterfly8(re, im)
            lanes = slice(block * LANES, (block + 1) * LANES)
            other = slice(inner + block * LANES, inner + (block + 1) * LANES)
            for y_lo in range(RADIX):
                if y_lo == 0:
                    tr, ti = re[0], im[0]
                else:
                    cosine = twiddle_ref[y_lo, 0:1, lanes]
                    sine = twiddle_ref[y_lo, 1:2, lanes]
                    tr = re[y_lo] * cosine - im[y_lo] * sine
                    ti = re[y_lo] * sine + im[y_lo] * cosine
                mid[y_lo, at, lanes] = tr.astype(jnp.bfloat16)
                mid[y_lo, at, other] = ti.astype(jnp.bfloat16)
    groups = out_refs[0].shape[0] // RADIX
    for part in range(2):
        for block in range(0, inner // LANES, 2):
            start = part * inner + block * LANES
            pair = min(2, inner // LANES - block)
            wide = jnp.dot(
                mid[...].reshape(RADIX * rows, 2 * inner),
                table_ref[:, start : start + pair * LANES],
                preferred_element_type=jnp.float32,
            ).astype(jnp.bfloat16)
            for k in range(pair):
                chunk, group = divmod(block + k, groups)
                for y_lo in range(RADIX):
                    out_refs[chunk][group * RADIX + y_lo, part] = wide[
                        y_lo * rows : (y_lo + 1) * rows, k * LANES : (k + 1) * LANES
                    ]


def column_transform(x, pieces, share, held):
    _, rows, length = x.shape
    inner = length // RADIX
    count = length // pieces // LANES
    own = rows // PARTS
    block = math.gcd(own, 64)
    first = share * (own // block)
    kept = pl.BlockSpec((pieces, 2, block, LANES), lambda i: (0, 0, i + first, 0))
    return pl.pallas_call(
        functools.partial(column_kernel, len(held)),
        grid=(own // block,),
        in_specs=[
            pl.BlockSpec((2, block, length), lambda i: (0, i + first, 0)),
            pl.BlockSpec((RADIX, 2, inner), lambda i: (0, 0, 0)),
            pl.BlockSpec((2 * inner, 2 * inner), lambda i: (0, 0)),
        ]
        + [pl.BlockSpec(memory_space=pl.ANY)] * len(held),
        out_specs=[pl.BlockSpec((pieces, 2, block, LANES), lambda i: (0, 0, i, 0))]
        + [kept] * (count - 1),
        out_shape=[jax.ShapeDtypeStruct((pieces, 2, own, LANES), jnp.bfloat16)]
        + [jax.ShapeDtypeStruct((pieces, 2, rows, LANES), jnp.bfloat16)] * (count - 1),
        scratch_shapes=[pltpu.VMEM((RADIX, block, 2 * inner), jnp.bfloat16)],
        input_output_aliases={3 + i: 1 + i for i in range(len(held))},
        compiler_params=params(),
        cost_estimate=pl.CostEstimate(
            flops=16 * own * length * inner, bytes_accessed=8 * own * length, transcendentals=0
        ),
        name="column_transform",
    )(x, jnp.asarray(twiddle_table(length)), jnp.asarray(inner_table(inner)), *held)


def clean_kernel(count, after, later, at_ref, *refs):
    x_refs, refs = refs[:count], refs[count:]
    basis_ref, basis_t_ref, gain_ref, swap_ref, back_ref = refs[:5]
    *out_refs, slab = refs[5 + after + later :]
    out_refs = out_refs[: len(out_refs) - later]
    chans = slab.shape[0]
    rows_dev = slab.shape[1] // LANES
    tall = swap_ref.shape[0]
    group = tall // rows_dev
    begin = 0
    for source in range(x_refs[0].shape[0]):
        for x_ref in x_refs:
            for row in range(0, x_ref.shape[2], tall):
                turned = jnp.dot(
                    swap_ref[...],
                    x_ref[source, 0, row : row + tall, :],
                    preferred_element_type=jnp.float32,
                ).astype(jnp.bfloat16)
                for u in range(rows_dev):
                    slab[begin : begin + group, u * LANES : (u + 1) * LANES] = turned[
                        u * group : (u + 1) * group
                    ]
                begin += group
    pair = math.gcd(rows_dev, 2)
    for first in range(0, rows_dev, pair):
        lanes = slice(first * LANES, (first + pair) * LANES)
        line = slab[:, lanes]
        amps = jnp.dot(basis_t_ref[...], line, preferred_element_type=jnp.float32)
        amps = amps.astype(jnp.bfloat16).astype(jnp.float32)
        front = jnp.concatenate(
            [
                gain_ref[:, first + k : first + k + 1] * amps[:, k * LANES : (k + 1) * LANES]
                for k in range(pair)
            ],
            axis=1,
        ).astype(jnp.bfloat16)
        drop = jnp.dot(basis_ref[...], front, preferred_element_type=jnp.float32)
        slab[:, lanes] = (line.astype(jnp.float32) - drop).astype(jnp.bfloat16)
    steps = len(out_refs)
    share = chans // steps
    out_rows = out_refs[0].shape[2]
    tall = back_ref.shape[0]
    group = tall // rows_dev
    for step, out_ref in enumerate(out_refs):
        start = lax.rem(at_ref[0] + step, steps) * share
        for b in range(share // group):
            channels = pl.ds(pl.multiple_of(start + b * group, group), group)
            tile = jnp.concatenate(
                [slab[channels, u * LANES : (u + 1) * LANES] for u in range(rows_dev)], axis=0
            )
            value = jnp.dot(back_ref[...], tile, preferred_element_type=jnp.float32)
            if out_rows % tall == 0:
                target, row = divmod(b * tall, out_rows)
                out_ref[target, 0, row : row + tall, :] = value.astype(jnp.bfloat16)
            else:
                take = tall // out_rows
                out_ref[b * take : (b + 1) * take, 0] = value.reshape(
                    take, out_rows, LANES
                ).astype(jnp.bfloat16)


def clean(at, xs, basis, basis_t, gain, steps, targets, rows_dev, after, later):
    sources = xs[0].shape[0]
    chans = basis.shape[0]
    own = chans // sources // len(xs)
    swap = swap_table(min(256 // rows_dev, own), rows_dev)
    back = np.ascontiguousarray(swap_table(256 // rows_dev, rows_dev).T)
    out_rows = chans * rows_dev // (targets * steps)
    whole = lambda s, at: (0, 0)
    waits = [pl.BlockSpec(memory_space=pl.ANY)] * (len(after) + len(later))
    first_later = 1 + len(xs) + 5 + len(after)
    return pl.pallas_call(
        functools.partial(clean_kernel, len(xs), len(after), len(later)),
        grid_spec=pltpu.PrefetchScalarGridSpec(
            num_scalar_prefetch=1,
            grid=(2,),
            in_specs=[
                pl.BlockSpec((sources, 1, own * rows_dev, LANES), lambda s, at: (0, s, 0, 0))
                for x in xs
            ]
            + [
                pl.BlockSpec(basis.shape, whole),
                pl.BlockSpec(basis.shape, whole),
                pl.BlockSpec(gain.shape, whole),
                pl.BlockSpec(swap.shape, whole),
                pl.BlockSpec(back.shape, whole),
            ]
            + waits,
            out_specs=[
                pl.BlockSpec((targets, 1, out_rows, LANES), lambda s, at: (0, s, 0, 0))
            ] * steps
            + [pl.BlockSpec(memory_space=pl.ANY)] * len(later),
            scratch_shapes=[pltpu.VMEM((chans, rows_dev * LANES), jnp.bfloat16)],
        ),
        out_shape=[jax.ShapeDtypeStruct((targets, 2, out_rows, LANES), jnp.bfloat16)] * steps
        + [jax.ShapeDtypeStruct(a.shape, a.dtype) for a in later],
        input_output_aliases={first_later + i: steps + i for i in range(len(later))},
        compiler_params=params(),
        cost_estimate=pl.CostEstimate(
            flops=12 * chans * chans * rows_dev * LANES,
            bytes_accessed=8 * chans * rows_dev * LANES,
            transcendentals=0,
        ),
        name="clean",
    )(at, *xs, basis, basis_t, gain, jnp.asarray(swap), jnp.asarray(back), *after, *later)


def row_kernel(scale, group, steps, *refs):
    x_refs, table_ref, out_ref = refs[:steps], refs[steps], refs[-1]
    targets, _, chans, total, _ = out_ref.shape
    rows_dev = x_refs[0].shape[2] // chans
    tall = group * rows_dev
    for target in range(targets):
        for c in range(chans // group):
            rows = slice(c * tall, (c + 1) * tall)
            parts = [x_ref[target, s, rows, :] for x_ref in x_refs for s in range(2)]
            if tall % 16:
                parts = [part.astype(jnp.float32) for part in parts]
            tile = jnp.concatenate(parts, axis=0).astype(jnp.bfloat16)
            value = jnp.dot(table_ref[...], tile, preferred_element_type=jnp.float32) * scale
            out_ref[target, :, c * group : (c + 1) * group] = value.reshape(
                2, group, total, LANES
            ).astype(jnp.bfloat16)


def row_transform(pieces, at, chans, rows_dev, length, after):
    steps = len(pieces)
    targets, _, rows, _ = pieces[0].shape
    total = steps * rows_dev
    group = min(chans, max(1, 256 // (2 * total)))
    tables = jnp.asarray(row_tables(rows_dev, steps, group))
    table = lax.dynamic_index_in_dim(tables, at[0], 0, keepdims=False)
    scale = 1.0 / math.sqrt(total * length)
    block = math.gcd(targets, 2)
    return pl.pallas_call(
        functools.partial(row_kernel, scale, group, steps),
        grid=(targets // block,),
        in_specs=[pl.BlockSpec((block, 2, rows, LANES), lambda j: (j, 0, 0, 0))] * steps
        + [pl.BlockSpec(table.shape, lambda j: (0, 0))]
        + [pl.BlockSpec(memory_space=pl.ANY)] * len(after),
        out_specs=pl.BlockSpec((block, 2, chans, total, LANES), lambda j: (j, 0, 0, 0, 0)),
        out_shape=jax.ShapeDtypeStruct((targets, 2, chans, total, LANES), jnp.bfloat16),
        compiler_params=params(),
        cost_estimate=pl.CostEstimate(
            flops=1024 * targets * chans * total * LANES,
            bytes_accessed=8 * targets * chans * total * LANES,
            transcendentals=0,
        ),
        name="row_transform",
    )(*pieces, table, *after)


def place_kernel(x_ref, table_ref, *refs):
    out_ref = refs[-1]
    shape = out_ref.shape
    rows = shape[0] * shape[1] * shape[2]
    tile = jnp.concatenate(
        [x_ref[y_lo].reshape(rows, LANES) for y_lo in range(RADIX)], axis=1
    )
    value = jnp.dot(tile, table_ref[...], preferred_element_type=jnp.float32)
    out_ref[...] = value.astype(jnp.bfloat16).reshape(shape)


def place(x, chunk, count, held):
    pieces, _, chans, total, _ = x.shape
    groups = pieces // RADIX
    table = order_table()
    wide = RADIX * LANES
    block = math.gcd(chans, 4)
    return pl.pallas_call(
        place_kernel,
        grid=(chans // block, groups),
        in_specs=[
            pl.BlockSpec((RADIX, 2, block, total, LANES), lambda c, g: (g, 0, c, 0, 0)),
            pl.BlockSpec(table.shape, lambda c, g: (0, 0)),
        ]
        + [pl.BlockSpec(memory_space=pl.ANY)] * len(held),
        out_specs=pl.BlockSpec(
            (2, block, total, wide), lambda c, g: (0, c, 0, chunk * groups + g)
        ),
        out_shape=jax.ShapeDtypeStruct((2, chans, total, count * groups * wide), jnp.bfloat16),
        input_output_aliases={2: 0} if held else {},
        compiler_params=params(),
        cost_estimate=pl.CostEstimate(
            flops=4 * pieces * chans * total * LANES * wide,
            bytes_accessed=8 * pieces * chans * total * LANES,
            transcendentals=0,
        ),
        name="place",
    )(x, jnp.asarray(table), *held)


def turn_kernel(later, basis_ref, *refs):
    out_ref = refs[-1 - later]
    out_ref[...] = basis_ref[...].T


def turn(basis, after, later):
    untouched = pl.BlockSpec(memory_space=pl.ANY)
    return pl.pallas_call(
        functools.partial(turn_kernel, len(later)),
        in_specs=[pl.BlockSpec(memory_space=pltpu.VMEM)] + [untouched] * (len(after) + len(later)),
        out_specs=[pl.BlockSpec(memory_space=pltpu.VMEM)] + [untouched] * len(later),
        out_shape=[jax.ShapeDtypeStruct(a.shape, a.dtype) for a in (basis, *later)],
        input_output_aliases={1 + len(after) + i: 1 + i for i in range(len(later))},
        compiler_params=params(),
        name="turn",
    )(basis, *after, *later)


def exchange(x):
    return lax.all_to_all(x, "chan", split_axis=0, concat_axis=0, tiled=True)


def shards(visibility, eigen_basis, eigenvalues, noise_power):
    uv_count = lax.axis_size("uv")
    chan_count = lax.axis_size("chan")
    _, chans, rows_dev, length = visibility.shape
    count = length // chan_count // LANES
    out_chans = chans // uv_count
    at = lax.axis_index("uv").astype(jnp.int32).reshape(1)
    basis = exchange(jnp.broadcast_to(eigen_basis, (chan_count,) + eigen_basis.shape))
    basis = basis.reshape(chan_count * chans, -1)
    gain = eigenvalues[:, None] / (eigenvalues[:, None] + noise_power[None, :])
    flat = visibility.reshape(2, chans * rows_dev, length)
    firsts, chunks = [], []
    for share in range(PARTS):
        first, *chunks = column_transform(flat, chan_count, share, chunks)
        firsts.append(exchange(first))
    basis_t, *chunks = turn(basis, firsts[:1], chunks)
    cells = [firsts] + [[exchange(chunk)] for chunk in chunks[:1]]
    chunks = chunks[1:]
    pieces, lines, held = [], [], []
    for k in range(count):
        after = pieces[k - 2][1:] if k >= 2 else []
        later = chunks[:1]
        chunks = chunks[1:]
        result = clean(
            at, cells[k], basis, basis_t, gain, uv_count, chan_count, rows_dev, after, later
        )
        cells += [[exchange(chunk)] for chunk in result[uv_count:]]
        pieces.append(
            [result[0]]
            + [
                lax.ppermute(
                    result[step], "uv", [(z, (z + step) % uv_count) for z in range(uv_count)]
                )
                for step in range(1, uv_count)
            ]
        )
    for k in range(count):
        after = [parts[0] for parts in pieces[k + 2 : k + 3]]
        after += [parts[1] for parts in pieces[k + 1 : k + 2]]
        if k == 0:
            after += cells[-1]
        lines = row_transform(pieces[k], at, out_chans, rows_dev, length, after)
        held = [place(exchange(lines), k, count, held)]
    return held[0]


def solution(mesh):
    in_specs = (P(None, "chan", "uv", None), P("chan", None), P(), P("uv"))
    out_specs = P(None, ("uv", "chan"), None, None)
    return jax.shard_map(shards, mesh=mesh, in_specs=in_specs, out_specs=out_specs, check_vma=False)
```

```python
import functools
import math

import jax
import jax.numpy as jnp
import numpy as np
from jax import lax
from jax.experimental import pallas as pl
from jax.experimental.pallas import tpu as pltpu
from jax.sharding import PartitionSpec as P

LANES = 128
RADIX = 8
VMEM_BYTES = 56 * 1024 * 1024


def params():
    return pltpu.CompilerParams(vmem_limit_bytes=VMEM_BYTES)


def inner_table(size):
    position = np.arange(size)
    phase = 2.0 * np.pi * (np.outer(position, position) % size) / size
    cosine, sine = np.cos(phase), np.sin(phase)
    return np.block([[cosine, sine], [-sine, cosine]]).astype(jnp.bfloat16)


def twiddle_table(length):
    inner = length // RADIX
    phase = 2.0 * np.pi * np.outer(np.arange(RADIX), np.arange(inner)) / length
    return np.stack([np.cos(phase), np.sin(phase)], axis=1).astype(np.float32)


def order_table():
    table = np.zeros((RADIX, LANES, LANES, RADIX), np.float32)
    for y_lo in range(RADIX):
        for y_hi in range(LANES):
            table[y_lo, y_hi, y_hi, y_lo] = 1.0
    return table.reshape(RADIX * LANES, RADIX * LANES).astype(jnp.bfloat16)


def swap_table(major, minor):
    table = np.zeros((major * minor, major * minor), np.float32)
    for a in range(major):
        for b in range(minor):
            table[b * major + a, a * minor + b] = 1.0
    return table.astype(jnp.bfloat16)


def row_tables(rows_dev, uv_count, group):
    total = rows_dev * uv_count
    position = np.arange(total)
    phase = 2.0 * np.pi * (np.outer(position, position) % total) / total
    cosine, sine = np.cos(phase), np.sin(phase)
    parts = np.array([[cosine, -sine], [sine, cosine]])
    parts = parts.reshape(2, 2, total, uv_count, rows_dev)
    eye = np.eye(group)
    size = 2 * group * total
    tables = []
    for at in range(uv_count):
        order = (at - np.arange(uv_count)) % uv_count
        table = np.einsum("tsxzu,cd->tcxzsdu", parts[:, :, :, order], eye)
        tables.append(table.reshape(size, size).astype(jnp.bfloat16))
    return np.stack(tables)


def butterfly8(re, im):
    def dft2(ar, ai, br, bi):
        return ar + br, ai + bi, ar - br, ai - bi

    def dft4(r, i):
        s0r, s0i, d0r, d0i = dft2(r[0], i[0], r[2], i[2])
        s1r, s1i, d1r, d1i = dft2(r[1], i[1], r[3], i[3])
        return (
            [s0r + s1r, d0r - d1i, s0r - s1r, d0r + d1i],
            [s0i + s1i, d0i + d1r, s0i - s1i, d0i - d1r],
        )

    er, ei = dft4(re[0::2], im[0::2])
    orr, oi = dft4(re[1::2], im[1::2])
    half = math.sqrt(0.5)
    turned_r = [orr[0], (orr[1] - oi[1]) * half, -oi[2], (-orr[3] - oi[3]) * half]
    turned_i = [oi[0], (orr[1] + oi[1]) * half, orr[2], (orr[3] - oi[3]) * half]
    out_r = [er[k] + turned_r[k] for k in range(4)] + [er[k] - turned_r[k] for k in range(4)]
    out_i = [ei[k] + turned_i[k] for k in range(4)] + [ei[k] - turned_i[k] for k in range(4)]
    return out_r, out_i


def column_kernel(groups, x_ref, twiddle_ref, table_ref, *refs):
    *out_refs, mid = refs
    if len(out_refs) > len(groups):
        basis_ref, *out_refs, copy_ref = out_refs
        copy_ref[...] = basis_ref[...]
    rows, length = x_ref.shape[1:]
    inner = length // RADIX
    step = 16
    for i in range(rows // step):
        at = slice(i * step, (i + 1) * step)
        for block in range(inner // LANES):
            re, im = [], []
            for a in range(RADIX):
                lanes = slice(a * inner + block * LANES, a * inner + (block + 1) * LANES)
                re.append(x_ref[0, at, lanes].astype(jnp.float32))
                im.append(x_ref[1, at, lanes].astype(jnp.float32))
            re, im = butterfly8(re, im)
            lanes = slice(block * LANES, (block + 1) * LANES)
            other = slice(inner + block * LANES, inner + (block + 1) * LANES)
            for y_lo in range(RADIX):
                if y_lo == 0:
                    tr, ti = re[0], im[0]
                else:
                    cosine = twiddle_ref[y_lo, 0:1, lanes]
                    sine = twiddle_ref[y_lo, 1:2, lanes]
                    tr = re[y_lo] * cosine - im[y_lo] * sine
                    ti = re[y_lo] * sine + im[y_lo] * cosine
                mid[y_lo, at, lanes] = tr.astype(jnp.bfloat16)
                mid[y_lo, at, other] = ti.astype(jnp.bfloat16)
    spread = out_refs[0].shape[0] // RADIX
    wanted = []
    for out_ref, chunks in zip(out_refs, groups):
        for place_at, chunk in enumerate(chunks):
            for group in range(spread):
                for part in range(2):
                    column = part * inner + (chunk * spread + group) * LANES
                    wanted.append((column, out_ref, group * RADIX, part, place_at * LANES))
    for first in range(0, len(wanted), 2):
        pair = wanted[first : first + 2]
        table = jnp.concatenate([table_ref[:, item[0] : item[0] + LANES] for item in pair], axis=1)
        wide = jnp.dot(
            mid[...].reshape(RADIX * rows, 2 * inner), table, preferred_element_type=jnp.float32
        ).astype(jnp.bfloat16)
        for k, (_, out_ref, piece, part, lane) in enumerate(pair):
            for y_lo in range(RADIX):
                out_ref[piece + y_lo, part, :, lane : lane + LANES] = wide[
                    y_lo * rows : (y_lo + 1) * rows, k * LANES : (k + 1) * LANES
                ]


def column_transform(x, pieces, groups, passed):
    _, rows, length = x.shape
    inner = length // RADIX
    block = math.gcd(rows, 64)
    lanes = [len(chunks) * LANES for chunks in groups]
    kept = [pl.BlockSpec(a.shape, lambda i: (0, 0)) for a in passed]
    return pl.pallas_call(
        functools.partial(column_kernel, groups),
        grid=(rows // block,),
        in_specs=[
            pl.BlockSpec((2, block, length), lambda i: (0, i, 0)),
            pl.BlockSpec((RADIX, 2, inner), lambda i: (0, 0, 0)),
            pl.BlockSpec((2 * inner, 2 * inner), lambda i: (0, 0)),
        ]
        + kept,
        out_specs=[pl.BlockSpec((pieces, 2, block, n), lambda i: (0, 0, i, 0)) for n in lanes] + kept,
        out_shape=[jax.ShapeDtypeStruct((pieces, 2, rows, n), jnp.bfloat16) for n in lanes]
        + [jax.ShapeDtypeStruct(a.shape, a.dtype) for a in passed],
        scratch_shapes=[pltpu.VMEM((RADIX, block, 2 * inner), jnp.bfloat16)],
        compiler_params=params(),
        cost_estimate=pl.CostEstimate(
            flops=4 * rows * length * sum(lanes), bytes_accessed=8 * rows * length, transcendentals=0
        ),
        name="column_transform",
    )(x, jnp.asarray(twiddle_table(length)), jnp.asarray(inner_table(inner)), *passed)


def clean_kernel(after, later, at_ref, x_ref, basis_ref, basis_t_ref, gain_ref, swap_ref, back_ref, *refs):
    *out_refs, slab = refs[after + later :]
    out_refs = out_refs[: len(out_refs) - later]
    chans = slab.shape[0]
    rows_dev = slab.shape[1] // LANES
    tall = swap_ref.shape[0]
    group = tall // rows_dev
    begin = 0
    for source in range(x_ref.shape[0]):
        for row in range(0, x_ref.shape[2], tall):
            turned = jnp.dot(
                swap_ref[...],
                x_ref[source, 0, row : row + tall, :],
                preferred_element_type=jnp.float32,
            ).astype(jnp.bfloat16)
            for u in range(rows_dev):
                slab[begin : begin + group, u * LANES : (u + 1) * LANES] = turned[
                    u * group : (u + 1) * group
                ]
            begin += group
    pair = math.gcd(rows_dev, 2)
    for first in range(0, rows_dev, pair):
        lanes = slice(first * LANES, (first + pair) * LANES)
        line = slab[:, lanes]
        amps = jnp.dot(basis_t_ref[...], line, preferred_element_type=jnp.float32)
        amps = amps.astype(jnp.bfloat16).astype(jnp.float32)
        front = jnp.concatenate(
            [
                gain_ref[:, first + k : first + k + 1] * amps[:, k * LANES : (k + 1) * LANES]
                for k in range(pair)
            ],
            axis=1,
        ).astype(jnp.bfloat16)
        drop = jnp.dot(basis_ref[...], front, preferred_element_type=jnp.float32)
        slab[:, lanes] = (line.astype(jnp.float32) - drop).astype(jnp.bfloat16)
    if len(out_refs) == 1 and len(out_refs[0].shape) == 5:
        joined = out_refs[0]
        out_refs = [joined.at[:, step] for step in range(joined.shape[1])]
    steps = len(out_refs)
    share = chans // steps
    out_rows = out_refs[0].shape[2]
    tall = back_ref.shape[0]
    group = tall // rows_dev
    for step, out_ref in enumerate(out_refs):
        start = lax.rem(at_ref[0] + step, steps) * share
        for b in range(share // group):
            channels = pl.ds(pl.multiple_of(start + b * group, group), group)
            tile = jnp.concatenate(
                [slab[channels, u * LANES : (u + 1) * LANES] for u in range(rows_dev)], axis=0
            )
            value = jnp.dot(back_ref[...], tile, preferred_element_type=jnp.float32)
            if out_rows % tall == 0:
                target, row = divmod(b * tall, out_rows)
                out_ref[target, 0, row : row + tall, :] = value.astype(jnp.bfloat16)
            else:
                take = tall // out_rows
                out_ref[b * take : (b + 1) * take, 0] = value.reshape(
                    take, out_rows, LANES
                ).astype(jnp.bfloat16)


def clean(at, x, tile, basis, basis_t, gain, steps, targets, rows_dev, joined, after, later):
    sources = x.shape[0]
    chans = basis.shape[0]
    own = chans // sources
    swap = swap_table(min(256 // rows_dev, own), rows_dev)
    back = np.ascontiguousarray(swap_table(256 // rows_dev, rows_dev).T)
    out_rows = chans * rows_dev // (targets * steps)
    whole = lambda s, at: (0, 0)
    untouched = pl.BlockSpec(memory_space=pl.ANY)
    if joined:
        out_specs = [
            pl.BlockSpec((targets, steps, 1, out_rows, LANES), lambda s, at: (0, 0, s, 0, 0))
        ]
        out_shape = [jax.ShapeDtypeStruct((targets, steps, 2, out_rows, LANES), jnp.bfloat16)]
    else:
        out_specs = [
            pl.BlockSpec((targets, 1, out_rows, LANES), lambda s, at: (0, s, 0, 0))
        ] * steps
        out_shape = [jax.ShapeDtypeStruct((targets, 2, out_rows, LANES), jnp.bfloat16)] * steps
    aliases = {7 + len(after) + i: len(out_shape) + i for i in range(len(later))}
    result = pl.pallas_call(
        functools.partial(clean_kernel, len(after), len(later)),
        grid_spec=pltpu.PrefetchScalarGridSpec(
            num_scalar_prefetch=1,
            grid=(2,),
            in_specs=[
                pl.BlockSpec((sources, 1, own * rows_dev, LANES), lambda s, at: (0, s, 0, tile)),
                pl.BlockSpec(basis.shape, whole),
                pl.BlockSpec(basis.shape, whole),
                pl.BlockSpec(gain.shape, whole),
                pl.BlockSpec(swap.shape, whole),
                pl.BlockSpec(back.shape, whole),
            ]
            + [untouched] * (len(after) + len(later)),
            out_specs=out_specs + [untouched] * len(later),
            scratch_shapes=[pltpu.VMEM((chans, rows_dev * LANES), jnp.bfloat16)],
        ),
        out_shape=out_shape + [jax.ShapeDtypeStruct(a.shape, a.dtype) for a in later],
        input_output_aliases=aliases,
        compiler_params=params(),
        cost_estimate=pl.CostEstimate(
            flops=12 * chans * chans * rows_dev * LANES,
            bytes_accessed=8 * chans * rows_dev * LANES,
            transcendentals=0,
        ),
        name="clean",
    )(at, x, basis, basis_t, gain, jnp.asarray(swap), jnp.asarray(back), *after, *later)
    return result[: len(out_shape)], result[len(out_shape) :]


def row_kernel(scale, group, steps, *refs):
    x_refs, table_ref, out_ref = refs[:steps], refs[steps], refs[-1]
    targets, _, chans, total, _ = out_ref.shape
    rows_dev = x_refs[0].shape[2] // chans
    tall = group * rows_dev
    for target in range(targets):
        for c in range(chans // group):
            rows = slice(c * tall, (c + 1) * tall)
            parts = [x_ref[target, s, rows, :] for x_ref in x_refs for s in range(2)]
            if tall % 16:
                parts = [part.astype(jnp.float32) for part in parts]
            tile = jnp.concatenate(parts, axis=0).astype(jnp.bfloat16)
            value = jnp.dot(table_ref[...], tile, preferred_element_type=jnp.float32) * scale
            out_ref[target, :, c * group : (c + 1) * group] = value.reshape(
                2, group, total, LANES
            ).astype(jnp.bfloat16)


def row_transform(pieces, at, chans, rows_dev, length, after):
    steps = len(pieces)
    targets, _, rows, _ = pieces[0].shape
    total = steps * rows_dev
    group = min(chans, max(1, 256 // (2 * total)))
    tables = jnp.asarray(row_tables(rows_dev, steps, group))
    table = lax.dynamic_index_in_dim(tables, at[0], 0, keepdims=False)
    scale = 1.0 / math.sqrt(total * length)
    block = math.gcd(targets, 2)
    return pl.pallas_call(
        functools.partial(row_kernel, scale, group, steps),
        grid=(targets // block,),
        in_specs=[pl.BlockSpec((block, 2, rows, LANES), lambda j: (j, 0, 0, 0))] * steps
        + [pl.BlockSpec(table.shape, lambda j: (0, 0))]
        + [pl.BlockSpec(memory_space=pl.ANY)] * len(after),
        out_specs=pl.BlockSpec((block, 2, chans, total, LANES), lambda j: (j, 0, 0, 0, 0)),
        out_shape=jax.ShapeDtypeStruct((targets, 2, chans, total, LANES), jnp.bfloat16),
        compiler_params=params(),
        cost_estimate=pl.CostEstimate(
            flops=1024 * targets * chans * total * LANES,
            bytes_accessed=8 * targets * chans * total * LANES,
            transcendentals=0,
        ),
        name="row_transform",
    )(*pieces, table, *after)


def place_kernel(x_ref, table_ref, *refs):
    out_ref = refs[-1]
    shape = out_ref.shape
    rows = shape[0] * shape[1] * shape[2]
    tile = jnp.concatenate(
        [x_ref[y_lo].reshape(rows, LANES) for y_lo in range(RADIX)], axis=1
    )
    value = jnp.dot(tile, table_ref[...], preferred_element_type=jnp.float32)
    out_ref[...] = value.astype(jnp.bfloat16).reshape(shape)


def place(x, chunk, count, held):
    pieces, _, chans, total, _ = x.shape
    groups = pieces // RADIX
    table = order_table()
    wide = RADIX * LANES
    block = math.gcd(chans, 4)
    return pl.pallas_call(
        place_kernel,
        grid=(chans // block, groups),
        in_specs=[
            pl.BlockSpec((RADIX, 2, block, total, LANES), lambda c, g: (g, 0, c, 0, 0)),
            pl.BlockSpec(table.shape, lambda c, g: (0, 0)),
        ]
        + [pl.BlockSpec(memory_space=pl.ANY)] * len(held),
        out_specs=pl.BlockSpec(
            (2, block, total, wide), lambda c, g: (0, c, 0, chunk * groups + g)
        ),
        out_shape=jax.ShapeDtypeStruct((2, chans, total, count * groups * wide), jnp.bfloat16),
        input_output_aliases={2: 0} if held else {},
        compiler_params=params(),
        cost_estimate=pl.CostEstimate(
            flops=4 * pieces * chans * total * LANES * wide,
            bytes_accessed=8 * pieces * chans * total * LANES,
            transcendentals=0,
        ),
        name="place",
    )(x, jnp.asarray(table), *held)


def gather_kernel(at_ref, *refs):
    *block_refs, basis_ref, turned_ref = refs
    count = len(block_refs)
    rows = block_refs[0].shape[0]
    for step, block_ref in enumerate(block_refs):
        owner = lax.rem(at_ref[0] - step + count, count)
        basis_ref[pl.ds(pl.multiple_of(owner * rows, rows), rows), :] = block_ref[...]
    turned_ref[...] = basis_ref[...].T


def gather(block):
    count = lax.axis_size("chan")
    blocks = [block] + [
        lax.ppermute(block, "chan", [(j, (j + step) % count) for j in range(count)])
        for step in range(1, count)
    ]
    rows, modes = block.shape
    vmem = pl.BlockSpec(memory_space=pltpu.VMEM)
    return pl.pallas_call(
        gather_kernel,
        in_specs=[pl.BlockSpec(memory_space=pltpu.SMEM)] + [vmem] * count,
        out_specs=[vmem] * 2,
        out_shape=[
            jax.ShapeDtypeStruct((count * rows, modes), block.dtype),
            jax.ShapeDtypeStruct((modes, count * rows), block.dtype),
        ],
        compiler_params=params(),
        name="gather",
    )(lax.axis_index("chan").astype(jnp.int32).reshape(1), *blocks)


def hold_kernel(*refs):
    pass


def hold(x, after):
    untouched = pl.BlockSpec(memory_space=pl.ANY)
    return pl.pallas_call(
        hold_kernel,
        in_specs=[untouched] * (1 + len(after)),
        out_specs=untouched,
        out_shape=jax.ShapeDtypeStruct(x.shape, x.dtype),
        input_output_aliases={0: 0},
        name="hold",
    )(x, *after)


def exchange(x):
    return lax.all_to_all(x, "chan", split_axis=0, concat_axis=0, tiled=True)


def spread_rows(parts):
    count = len(parts)
    return [parts[0]] + [
        lax.ppermute(parts[step], "uv", [(z, (z + step) % count) for z in range(count)])
        for step in range(1, count)
    ]


def shards(visibility, eigen_basis, eigenvalues, noise_power):
    uv_count = lax.axis_size("uv")
    chan_count = lax.axis_size("chan")
    _, chans, rows_dev, length = visibility.shape
    count = length // chan_count // LANES
    out_chans = chans // uv_count
    at = lax.axis_index("uv").astype(jnp.int32).reshape(1)
    gain = eigenvalues[:, None] / (eigenvalues[:, None] + noise_power[None, :])
    flat = visibility.reshape(2, chans * rows_dev, length)
    groups = [g for g in ([1], list(range(2, count))) if g and g[-1] < count]
    first, block = column_transform(flat, chan_count, [[0]], [eigen_basis])
    cells = [exchange(first)]
    basis, basis_t = gather(block)
    sends = column_transform(flat, chan_count, groups, []) if groups else []
    cells += [exchange(send) for send in sends[:1]]
    sends = sends[1:]

    pieces, returned = {}, {}
    for k in range(count):
        last = k == count - 1 and count > 1
        after = [pieces[k - 1][1]] if k else []
        results, passed = clean(
            at,
            cells[min(k, 2)],
            max(k - 2, 0),
            basis,
            basis_t,
            gain,
            uv_count,
            chan_count,
            rows_dev,
            last,
            after,
            sends,
        )
        cells += [exchange(send) for send in passed]
        sends = []
        if not last:
            pieces[k] = spread_rows(results)
        else:
            joined = results[0]
    transform = lambda k, after: row_transform(pieces[k], at, out_chans, rows_dev, length, after)
    following = lambda k: [pieces[k + 1][1]] if k + 1 in pieces else []
    if count == 1:
        returned[0] = exchange(transform(0, []))
    else:
        first_lines = transform(0, following(0))
        returned[0] = exchange(hold(first_lines, cells[-1:]))
        joined = exchange(hold(joined, [returned[0]]))
        middle = {k: transform(k, following(k)) for k in range(1, count - 1)}
        pieces[count - 1] = spread_rows([joined[:, step] for step in range(uv_count)])
        before = joined
        for k in range(1, count - 1):
            returned[k] = exchange(hold(middle[k], [before]))
            before = returned[k]
        returned[count - 1] = transform(count - 1, [])
    order = list(range(count))
    if count > 2:
        order = order[:-2] + [count - 1, count - 2]
    held = []
    for k in order:
        held = [place(returned[k], k, count, held)]
    return held[0]


def solution(mesh):
    in_specs = (P(None, "chan", "uv", None), P("chan", None), P(), P("uv"))
    out_specs = P(None, ("uv", "chan"), None, None)
    return jax.shard_map(shards, mesh=mesh, in_specs=in_specs, out_specs=out_specs, check_vma=False)
```

```python
import functools
import math

import jax
import jax.numpy as jnp
import numpy as np
from jax import lax
from jax.experimental import pallas as pl
from jax.experimental.pallas import tpu as pltpu
from jax.sharding import PartitionSpec as P

LANES = 128
RADIX = 8
VMEM_BYTES = 56 * 1024 * 1024


def params():
    return pltpu.CompilerParams(vmem_limit_bytes=VMEM_BYTES)


def inner_table(size):
    position = np.arange(size)
    phase = 2.0 * np.pi * (np.outer(position, position) % size) / size
    cosine, sine = np.cos(phase), np.sin(phase)
    return np.block([[cosine, sine], [-sine, cosine]]).astype(jnp.bfloat16)


def twiddle_table(length):
    inner = length // RADIX
    phase = 2.0 * np.pi * np.outer(np.arange(RADIX), np.arange(inner)) / length
    return np.stack([np.cos(phase), np.sin(phase)], axis=1).astype(np.float32)


def order_table():
    table = np.zeros((RADIX, LANES, LANES, RADIX), np.float32)
    for y_lo in range(RADIX):
        for y_hi in range(LANES):
            table[y_lo, y_hi, y_hi, y_lo] = 1.0
    return table.reshape(RADIX * LANES, RADIX * LANES).astype(jnp.bfloat16)


def swap_table(major, minor):
    table = np.zeros((major * minor, major * minor), np.float32)
    for a in range(major):
        for b in range(minor):
            table[b * major + a, a * minor + b] = 1.0
    return table.astype(jnp.bfloat16)


def row_tables(rows_dev, uv_count, group):
    total = rows_dev * uv_count
    position = np.arange(total)
    phase = 2.0 * np.pi * (np.outer(position, position) % total) / total
    cosine, sine = np.cos(phase), np.sin(phase)
    parts = np.array([[cosine, -sine], [sine, cosine]])
    parts = parts.reshape(2, 2, total, uv_count, rows_dev)
    eye = np.eye(group)
    size = 2 * group * total
    tables = []
    for at in range(uv_count):
        order = (at - np.arange(uv_count)) % uv_count
        table = np.einsum("tsxzu,cd->tcxzsdu", parts[:, :, :, order], eye)
        tables.append(table.reshape(size, size).astype(jnp.bfloat16))
    return np.stack(tables)


def butterfly8(re, im):
    def dft2(ar, ai, br, bi):
        return ar + br, ai + bi, ar - br, ai - bi

    def dft4(r, i):
        s0r, s0i, d0r, d0i = dft2(r[0], i[0], r[2], i[2])
        s1r, s1i, d1r, d1i = dft2(r[1], i[1], r[3], i[3])
        return (
            [s0r + s1r, d0r - d1i, s0r - s1r, d0r + d1i],
            [s0i + s1i, d0i + d1r, s0i - s1i, d0i - d1r],
        )

    er, ei = dft4(re[0::2], im[0::2])
    orr, oi = dft4(re[1::2], im[1::2])
    half = math.sqrt(0.5)
    turned_r = [orr[0], (orr[1] - oi[1]) * half, -oi[2], (-orr[3] - oi[3]) * half]
    turned_i = [oi[0], (orr[1] + oi[1]) * half, orr[2], (orr[3] - oi[3]) * half]
    out_r = [er[k] + turned_r[k] for k in range(4)] + [er[k] - turned_r[k] for k in range(4)]
    out_i = [ei[k] + turned_i[k] for k in range(4)] + [ei[k] - turned_i[k] for k in range(4)]
    return out_r, out_i


def column_kernel(groups, x_ref, twiddle_ref, table_ref, *refs):
    *out_refs, mid = refs
    rows, length = x_ref.shape[1:]
    inner = length // RADIX
    step = 16
    for i in range(rows // step):
        at = slice(i * step, (i + 1) * step)
        for block in range(inner // LANES):
            re, im = [], []
            for a in range(RADIX):
                lanes = slice(a * inner + block * LANES, a * inner + (block + 1) * LANES)
                re.append(x_ref[0, at, lanes].astype(jnp.float32))
                im.append(x_ref[1, at, lanes].astype(jnp.float32))
            re, im = butterfly8(re, im)
            lanes = slice(block * LANES, (block + 1) * LANES)
            other = slice(inner + block * LANES, inner + (block + 1) * LANES)
            for y_lo in range(RADIX):
                if y_lo == 0:
                    tr, ti = re[0], im[0]
                else:
                    cosine = twiddle_ref[y_lo, 0:1, lanes]
                    sine = twiddle_ref[y_lo, 1:2, lanes]
                    tr = re[y_lo] * cosine - im[y_lo] * sine
                    ti = re[y_lo] * sine + im[y_lo] * cosine
                mid[y_lo, at, lanes] = tr.astype(jnp.bfloat16)
                mid[y_lo, at, other] = ti.astype(jnp.bfloat16)
    spread = out_refs[0].shape[0] // RADIX
    wanted = []
    for out_ref, chunks in zip(out_refs, groups):
        for place_at, chunk in enumerate(chunks):
            for group in range(spread):
                for part in range(2):
                    column = part * inner + (chunk * spread + group) * LANES
                    wanted.append((column, out_ref, group * RADIX, part, place_at * LANES))
    for first in range(0, len(wanted), 2):
        pair = wanted[first : first + 2]
        table = jnp.concatenate([table_ref[:, item[0] : item[0] + LANES] for item in pair], axis=1)
        wide = jnp.dot(
            mid[...].reshape(RADIX * rows, 2 * inner), table, preferred_element_type=jnp.float32
        ).astype(jnp.bfloat16)
        for k, (_, out_ref, piece, part, lane) in enumerate(pair):
            for y_lo in range(RADIX):
                out_ref[piece + y_lo, part, :, lane : lane + LANES] = wide[
                    y_lo * rows : (y_lo + 1) * rows, k * LANES : (k + 1) * LANES
                ]


def column_transform(x, pieces, groups):
    _, rows, length = x.shape
    inner = length // RADIX
    block = math.gcd(rows, 64)
    lanes = [len(chunks) * LANES for chunks in groups]
    return pl.pallas_call(
        functools.partial(column_kernel, groups),
        grid=(rows // block,),
        in_specs=[
            pl.BlockSpec((2, block, length), lambda i: (0, i, 0)),
            pl.BlockSpec((RADIX, 2, inner), lambda i: (0, 0, 0)),
            pl.BlockSpec((2 * inner, 2 * inner), lambda i: (0, 0)),
        ],
        out_specs=[pl.BlockSpec((pieces, 2, block, n), lambda i: (0, 0, i, 0)) for n in lanes],
        out_shape=[jax.ShapeDtypeStruct((pieces, 2, rows, n), jnp.bfloat16) for n in lanes],
        scratch_shapes=[pltpu.VMEM((RADIX, block, 2 * inner), jnp.bfloat16)],
        compiler_params=params(),
        cost_estimate=pl.CostEstimate(
            flops=4 * rows * length * sum(lanes), bytes_accessed=8 * rows * length, transcendentals=0
        ),
        name="column_transform",
    )(x, jnp.asarray(twiddle_table(length)), jnp.asarray(inner_table(inner)))


def clean_kernel(after, later, at_ref, x_ref, basis_ref, basis_t_ref, gain_ref, swap_ref, back_ref, *refs):
    *out_refs, slab = refs[after + later :]
    out_refs = out_refs[: len(out_refs) - later]
    chans = slab.shape[0]
    rows_dev = slab.shape[1] // LANES
    tall = swap_ref.shape[0]
    group = tall // rows_dev
    begin = 0
    for source in range(x_ref.shape[0]):
        for row in range(0, x_ref.shape[2], tall):
            turned = jnp.dot(
                swap_ref[...],
                x_ref[source, 0, row : row + tall, :],
                preferred_element_type=jnp.float32,
            ).astype(jnp.bfloat16)
            for u in range(rows_dev):
                slab[begin : begin + group, u * LANES : (u + 1) * LANES] = turned[
                    u * group : (u + 1) * group
                ]
            begin += group
    pair = math.gcd(rows_dev, 2)
    for first in range(0, rows_dev, pair):
        lanes = slice(first * LANES, (first + pair) * LANES)
        line = slab[:, lanes]
        amps = jnp.dot(basis_t_ref[...], line, preferred_element_type=jnp.float32)
        amps = amps.astype(jnp.bfloat16).astype(jnp.float32)
        front = jnp.concatenate(
            [
                gain_ref[:, first + k : first + k + 1] * amps[:, k * LANES : (k + 1) * LANES]
                for k in range(pair)
            ],
            axis=1,
        ).astype(jnp.bfloat16)
        drop = jnp.dot(basis_ref[...], front, preferred_element_type=jnp.float32)
        slab[:, lanes] = (line.astype(jnp.float32) - drop).astype(jnp.bfloat16)
    if len(out_refs) == 1 and len(out_refs[0].shape) == 5:
        joined = out_refs[0]
        out_refs = [joined.at[:, step] for step in range(joined.shape[1])]
    steps = len(out_refs)
    share = chans // steps
    out_rows = out_refs[0].shape[2]
    tall = back_ref.shape[0]
    group = tall // rows_dev
    for step, out_ref in enumerate(out_refs):
        start = lax.rem(at_ref[0] + step, steps) * share
        for b in range(share // group):
            channels = pl.ds(pl.multiple_of(start + b * group, group), group)
            tile = jnp.concatenate(
                [slab[channels, u * LANES : (u + 1) * LANES] for u in range(rows_dev)], axis=0
            )
            value = jnp.dot(back_ref[...], tile, preferred_element_type=jnp.float32)
            if out_rows % tall == 0:
                target, row = divmod(b * tall, out_rows)
                out_ref[target, 0, row : row + tall, :] = value.astype(jnp.bfloat16)
            else:
                take = tall // out_rows
                out_ref[b * take : (b + 1) * take, 0] = value.reshape(
                    take, out_rows, LANES
                ).astype(jnp.bfloat16)


def clean(at, x, tile, basis, basis_t, gain, steps, targets, rows_dev, joined, after, later):
    sources = x.shape[0]
    chans = basis.shape[0]
    own = chans // sources
    swap = swap_table(min(256 // rows_dev, own), rows_dev)
    back = np.ascontiguousarray(swap_table(256 // rows_dev, rows_dev).T)
    out_rows = chans * rows_dev // (targets * steps)
    whole = lambda s, at: (0, 0)
    untouched = pl.BlockSpec(memory_space=pl.ANY)
    if joined:
        out_specs = [
            pl.BlockSpec((targets, steps, 1, out_rows, LANES), lambda s, at: (0, 0, s, 0, 0))
        ]
        out_shape = [jax.ShapeDtypeStruct((targets, steps, 2, out_rows, LANES), jnp.bfloat16)]
    else:
        out_specs = [
            pl.BlockSpec((targets, 1, out_rows, LANES), lambda s, at: (0, s, 0, 0))
        ] * steps
        out_shape = [jax.ShapeDtypeStruct((targets, 2, out_rows, LANES), jnp.bfloat16)] * steps
    aliases = {7 + len(after) + i: len(out_shape) + i for i in range(len(later))}
    result = pl.pallas_call(
        functools.partial(clean_kernel, len(after), len(later)),
        grid_spec=pltpu.PrefetchScalarGridSpec(
            num_scalar_prefetch=1,
            grid=(2,),
            in_specs=[
                pl.BlockSpec((sources, 1, own * rows_dev, LANES), lambda s, at: (0, s, 0, tile)),
                pl.BlockSpec(basis.shape, whole),
                pl.BlockSpec(basis.shape, whole),
                pl.BlockSpec(gain.shape, whole),
                pl.BlockSpec(swap.shape, whole),
                pl.BlockSpec(back.shape, whole),
            ]
            + [untouched] * (len(after) + len(later)),
            out_specs=out_specs + [untouched] * len(later),
            scratch_shapes=[pltpu.VMEM((chans, rows_dev * LANES), jnp.bfloat16)],
        ),
        out_shape=out_shape + [jax.ShapeDtypeStruct(a.shape, a.dtype) for a in later],
        input_output_aliases=aliases,
        compiler_params=params(),
        cost_estimate=pl.CostEstimate(
            flops=12 * chans * chans * rows_dev * LANES,
            bytes_accessed=8 * chans * rows_dev * LANES,
            transcendentals=0,
        ),
        name="clean",
    )(at, x, basis, basis_t, gain, jnp.asarray(swap), jnp.asarray(back), *after, *later)
    return result[: len(out_shape)], result[len(out_shape) :]


def row_kernel(scale, group, steps, *refs):
    x_refs, table_ref, out_ref = refs[:steps], refs[steps], refs[-1]
    targets, _, chans, total, _ = out_ref.shape
    rows_dev = x_refs[0].shape[2] // chans
    tall = group * rows_dev
    for target in range(targets):
        for c in range(chans // group):
            rows = slice(c * tall, (c + 1) * tall)
            parts = [x_ref[target, s, rows, :] for x_ref in x_refs for s in range(2)]
            if tall % 16:
                parts = [part.astype(jnp.float32) for part in parts]
            tile = jnp.concatenate(parts, axis=0).astype(jnp.bfloat16)
            value = jnp.dot(table_ref[...], tile, preferred_element_type=jnp.float32) * scale
            out_ref[target, :, c * group : (c + 1) * group] = value.reshape(
                2, group, total, LANES
            ).astype(jnp.bfloat16)


def row_transform(pieces, at, chans, rows_dev, length, after):
    steps = len(pieces)
    targets, _, rows, _ = pieces[0].shape
    total = steps * rows_dev
    group = min(chans, max(1, 256 // (2 * total)))
    tables = jnp.asarray(row_tables(rows_dev, steps, group))
    table = lax.dynamic_index_in_dim(tables, at[0], 0, keepdims=False)
    scale = 1.0 / math.sqrt(total * length)
    block = math.gcd(targets, 2)
    return pl.pallas_call(
        functools.partial(row_kernel, scale, group, steps),
        grid=(targets // block,),
        in_specs=[pl.BlockSpec((block, 2, rows, LANES), lambda j: (j, 0, 0, 0))] * steps
        + [pl.BlockSpec(table.shape, lambda j: (0, 0))]
        + [pl.BlockSpec(memory_space=pl.ANY)] * len(after),
        out_specs=pl.BlockSpec((block, 2, chans, total, LANES), lambda j: (j, 0, 0, 0, 0)),
        out_shape=jax.ShapeDtypeStruct((targets, 2, chans, total, LANES), jnp.bfloat16),
        compiler_params=params(),
        cost_estimate=pl.CostEstimate(
            flops=1024 * targets * chans * total * LANES,
            bytes_accessed=8 * targets * chans * total * LANES,
            transcendentals=0,
        ),
        name="row_transform",
    )(*pieces, table, *after)


def place_kernel(x_ref, table_ref, *refs):
    out_ref = refs[-1]
    shape = out_ref.shape
    rows = shape[0] * shape[1] * shape[2]
    tile = jnp.concatenate(
        [x_ref[y_lo].reshape(rows, LANES) for y_lo in range(RADIX)], axis=1
    )
    value = jnp.dot(tile, table_ref[...], preferred_element_type=jnp.float32)
    out_ref[...] = value.astype(jnp.bfloat16).reshape(shape)


def place(x, chunk, count, held):
    pieces, _, chans, total, _ = x.shape
    groups = pieces // RADIX
    table = order_table()
    wide = RADIX * LANES
    block = math.gcd(chans, 4)
    return pl.pallas_call(
        place_kernel,
        grid=(chans // block, groups),
        in_specs=[
            pl.BlockSpec((RADIX, 2, block, total, LANES), lambda c, g: (g, 0, c, 0, 0)),
            pl.BlockSpec(table.shape, lambda c, g: (0, 0)),
        ]
        + [pl.BlockSpec(memory_space=pl.ANY)] * len(held),
        out_specs=pl.BlockSpec(
            (2, block, total, wide), lambda c, g: (0, c, 0, chunk * groups + g)
        ),
        out_shape=jax.ShapeDtypeStruct((2, chans, total, count * groups * wide), jnp.bfloat16),
        input_output_aliases={2: 0} if held else {},
        compiler_params=params(),
        cost_estimate=pl.CostEstimate(
            flops=4 * pieces * chans * total * LANES * wide,
            bytes_accessed=8 * pieces * chans * total * LANES,
            transcendentals=0,
        ),
        name="place",
    )(x, jnp.asarray(table), *held)


def turn_kernel(basis_ref, out_ref):
    out_ref[...] = basis_ref[...].T


def turn(basis):
    vmem = pl.BlockSpec(memory_space=pltpu.VMEM)
    return pl.pallas_call(
        turn_kernel,
        in_specs=[vmem],
        out_specs=vmem,
        out_shape=jax.ShapeDtypeStruct(basis.shape[::-1], basis.dtype),
        compiler_params=params(),
        name="turn",
    )(basis)


def hold_kernel(*refs):
    pass


def hold(arrays, after):
    if not after:
        return list(arrays)
    untouched = pl.BlockSpec(memory_space=pl.ANY)
    return pl.pallas_call(
        hold_kernel,
        in_specs=[untouched] * (len(arrays) + len(after)),
        out_specs=[untouched] * len(arrays),
        out_shape=[jax.ShapeDtypeStruct(a.shape, a.dtype) for a in arrays],
        input_output_aliases={i: i for i in range(len(arrays))},
        name="hold",
    )(*arrays, *after)


def exchange(x):
    return lax.all_to_all(x, "chan", split_axis=0, concat_axis=0, tiled=True)


def spread_rows(parts, before):
    count = len(parts)
    own, *sent = parts
    sent = hold(sent, before[1:])
    return [own] + [
        lax.ppermute(part, "uv", [(z, (z + step) % count) for z in range(count)])
        for step, part in enumerate(sent, 1)
    ]


def shards(visibility, eigen_basis, eigenvalues, noise_power):
    uv_count = lax.axis_size("uv")
    chan_count = lax.axis_size("chan")
    _, chans, rows_dev, length = visibility.shape
    count = length // chan_count // LANES
    out_chans = chans // uv_count
    at = lax.axis_index("uv").astype(jnp.int32).reshape(1)
    basis = exchange(jnp.broadcast_to(eigen_basis, (chan_count,) + eigen_basis.shape))
    basis = basis.reshape(chan_count * chans, -1)
    basis_t = turn(basis)
    gain = eigenvalues[:, None] / (eigenvalues[:, None] + noise_power[None, :])
    flat = visibility.reshape(2, chans * rows_dev, length)
    groups = [g for g in ([1], list(range(2, count))) if g and g[-1] < count]
    first = column_transform(flat, chan_count, [[0]])
    cells = [exchange(first[0])]
    sends = column_transform(flat, chan_count, groups) if groups else []
    cells += [exchange(send) for send in sends[:1]]
    sends = sends[1:]

    pieces, joined = [], None
    for k in range(count):
        last = k == count - 1 and count > 1
        results, passed = clean(
            at,
            cells[min(k, 2)],
            max(k - 2, 0),
            basis,
            basis_t,
            gain,
            uv_count,
            chan_count,
            rows_dev,
            last,
            [pieces[1][1]] if k > 1 else [],
            sends,
        )
        cells += [exchange(send) for send in passed]
        sends = []
        if last:
            joined = results[0]
        else:
            pieces.append(spread_rows(results, pieces[-1] if pieces else []))

    def transform(k):
        after = [parts[1] for parts in pieces[k + 1 : k + 2]]
        return row_transform(pieces[k], at, out_chans, rows_dev, length, after)

    def exchange_after(x, before):
        return exchange(hold([x], before)[0])

    if count == 1:
        returned = [exchange(transform(0))]
    else:
        returned = [exchange_after(transform(0), cells[-1:])]
        joined = exchange_after(joined, returned)
        pieces.append(
            spread_rows([joined[:, step] for step in range(uv_count)], pieces[-1])
        )
        for k in range(1, count - 1):
            returned.append(exchange_after(transform(k), [joined] if k == 1 else returned[-1:]))
        returned.append(transform(count - 1))
    order = list(range(count))
    if count > 2:
        order = order[:-2] + [count - 1, count - 2]
    held = []
    for k in order:
        held = [place(returned[k], k, count, held)]
    return held[0]


def solution(mesh):
    in_specs = (P(None, "chan", "uv", None), P("chan", None), P(), P("uv"))
    out_specs = P(None, ("uv", "chan"), None, None)
    return jax.shard_map(shards, mesh=mesh, in_specs=in_specs, out_specs=out_specs, check_vma=False)
```

```python
import functools
import math

import jax
import jax.numpy as jnp
import numpy as np
from jax import lax
from jax.experimental import pallas as pl
from jax.experimental.pallas import tpu as pltpu
from jax.sharding import PartitionSpec as P

LANES = 128
RADIX = 8
VMEM_BYTES = 56 * 1024 * 1024


def params():
    return pltpu.CompilerParams(vmem_limit_bytes=VMEM_BYTES)


def small():
    return pl.CostEstimate(flops=1, bytes_accessed=1, transcendentals=0)


def inner_table(size):
    position = np.arange(size)
    phase = 2.0 * np.pi * (np.outer(position, position) % size) / size
    cosine, sine = np.cos(phase), np.sin(phase)
    return np.block([[cosine, sine], [-sine, cosine]]).astype(jnp.bfloat16)


def twiddle_table(length):
    inner = length // RADIX
    phase = 2.0 * np.pi * np.outer(np.arange(RADIX), np.arange(inner)) / length
    return np.stack([np.cos(phase), np.sin(phase)], axis=1).astype(np.float32)


def order_table():
    table = np.zeros((RADIX, LANES, LANES, RADIX), np.float32)
    for y_lo in range(RADIX):
        for y_hi in range(LANES):
            table[y_lo, y_hi, y_hi, y_lo] = 1.0
    return table.reshape(RADIX * LANES, RADIX * LANES).astype(jnp.bfloat16)


def swap_table(major, minor):
    table = np.zeros((major * minor, major * minor), np.float32)
    for a in range(major):
        for b in range(minor):
            table[b * major + a, a * minor + b] = 1.0
    return table.astype(jnp.bfloat16)


def row_tables(rows_dev, uv_count, group):
    total = rows_dev * uv_count
    position = np.arange(total)
    phase = 2.0 * np.pi * (np.outer(position, position) % total) / total
    cosine, sine = np.cos(phase), np.sin(phase)
    parts = np.array([[cosine, -sine], [sine, cosine]])
    parts = parts.reshape(2, 2, total, uv_count, rows_dev)
    eye = np.eye(group)
    size = 2 * group * total
    tables = []
    for at in range(uv_count):
        order = (at - np.arange(uv_count)) % uv_count
        table = np.einsum("tsxzu,cd->tcxzsdu", parts[:, :, :, order], eye)
        tables.append(table.reshape(size, size).astype(jnp.bfloat16))
    return np.stack(tables)


def butterfly8(re, im):
    def dft2(ar, ai, br, bi):
        return ar + br, ai + bi, ar - br, ai - bi

    def dft4(r, i):
        s0r, s0i, d0r, d0i = dft2(r[0], i[0], r[2], i[2])
        s1r, s1i, d1r, d1i = dft2(r[1], i[1], r[3], i[3])
        return (
            [s0r + s1r, d0r - d1i, s0r - s1r, d0r + d1i],
            [s0i + s1i, d0i + d1r, s0i - s1i, d0i - d1r],
        )

    er, ei = dft4(re[0::2], im[0::2])
    orr, oi = dft4(re[1::2], im[1::2])
    half = math.sqrt(0.5)
    turned_r = [orr[0], (orr[1] - oi[1]) * half, -oi[2], (-orr[3] - oi[3]) * half]
    turned_i = [oi[0], (orr[1] + oi[1]) * half, orr[2], (orr[3] - oi[3]) * half]
    out_r = [er[k] + turned_r[k] for k in range(4)] + [er[k] - turned_r[k] for k in range(4)]
    out_i = [ei[k] + turned_i[k] for k in range(4)] + [ei[k] - turned_i[k] for k in range(4)]
    return out_r, out_i


def column_kernel(groups, x_ref, twiddle_ref, table_ref, *refs):
    *out_refs, mid = refs
    rows, length = x_ref.shape[1:]
    inner = length // RADIX
    step = 16
    for i in range(rows // step):
        at = slice(i * step, (i + 1) * step)
        for block in range(inner // LANES):
            re, im = [], []
            for a in range(RADIX):
                lanes = slice(a * inner + block * LANES, a * inner + (block + 1) * LANES)
                re.append(x_ref[0, at, lanes].astype(jnp.float32))
                im.append(x_ref[1, at, lanes].astype(jnp.float32))
            re, im = butterfly8(re, im)
            lanes = slice(block * LANES, (block + 1) * LANES)
            other = slice(inner + block * LANES, inner + (block + 1) * LANES)
            for y_lo in range(RADIX):
                if y_lo == 0:
                    tr, ti = re[0], im[0]
                else:
                    cosine = twiddle_ref[y_lo, 0:1, lanes]
                    sine = twiddle_ref[y_lo, 1:2, lanes]
                    tr = re[y_lo] * cosine - im[y_lo] * sine
                    ti = re[y_lo] * sine + im[y_lo] * cosine
                mid[y_lo, at, lanes] = tr.astype(jnp.bfloat16)
                mid[y_lo, at, other] = ti.astype(jnp.bfloat16)
    spread = out_refs[0].shape[0] // RADIX
    wanted = []
    for out_ref, chunks in zip(out_refs, groups):
        for place_at, chunk in enumerate(chunks):
            for group in range(spread):
                for part in range(2):
                    column = part * inner + (chunk * spread + group) * LANES
                    wanted.append((column, out_ref, group * RADIX, part, place_at * LANES))
    for first in range(0, len(wanted), 2):
        pair = wanted[first : first + 2]
        table = jnp.concatenate([table_ref[:, item[0] : item[0] + LANES] for item in pair], axis=1)
        wide = jnp.dot(
            mid[...].reshape(RADIX * rows, 2 * inner), table, preferred_element_type=jnp.float32
        ).astype(jnp.bfloat16)
        for k, (_, out_ref, piece, part, lane) in enumerate(pair):
            for y_lo in range(RADIX):
                out_ref[piece + y_lo, part, :, lane : lane + LANES] = wide[
                    y_lo * rows : (y_lo + 1) * rows, k * LANES : (k + 1) * LANES
                ]


def column_transform(x, pieces, groups):
    _, rows, length = x.shape
    inner = length // RADIX
    block = math.gcd(rows, 64)
    lanes = [len(chunks) * LANES for chunks in groups]
    return pl.pallas_call(
        functools.partial(column_kernel, groups),
        grid=(rows // block,),
        in_specs=[
            pl.BlockSpec((2, block, length), lambda i: (0, i, 0)),
            pl.BlockSpec((RADIX, 2, inner), lambda i: (0, 0, 0)),
            pl.BlockSpec((2 * inner, 2 * inner), lambda i: (0, 0)),
        ],
        out_specs=[pl.BlockSpec((pieces, 2, block, n), lambda i: (0, 0, i, 0)) for n in lanes],
        out_shape=[jax.ShapeDtypeStruct((pieces, 2, rows, n), jnp.bfloat16) for n in lanes],
        scratch_shapes=[pltpu.VMEM((RADIX, block, 2 * inner), jnp.bfloat16)],
        compiler_params=params(),
        cost_estimate=small(),
        name="column_transform",
    )(x, jnp.asarray(twiddle_table(length)), jnp.asarray(inner_table(inner)))


def clean_kernel(after, later, at_ref, x_ref, basis_ref, basis_t_ref, gain_ref, swap_ref, back_ref, *refs):
    *out_refs, slab = refs[after + later :]
    out_refs = out_refs[: len(out_refs) - later]
    chans = slab.shape[0]
    rows_dev = slab.shape[1] // LANES
    tall = swap_ref.shape[0]
    group = tall // rows_dev
    begin = 0
    for source in range(x_ref.shape[0]):
        for row in range(0, x_ref.shape[2], tall):
            turned = jnp.dot(
                swap_ref[...],
                x_ref[source, 0, row : row + tall, :],
                preferred_element_type=jnp.float32,
            ).astype(jnp.bfloat16)
            for u in range(rows_dev):
                slab[begin : begin + group, u * LANES : (u + 1) * LANES] = turned[
                    u * group : (u + 1) * group
                ]
            begin += group
    pair = math.gcd(rows_dev, 2)
    for first in range(0, rows_dev, pair):
        lanes = slice(first * LANES, (first + pair) * LANES)
        line = slab[:, lanes]
        amps = jnp.dot(basis_t_ref[...], line, preferred_element_type=jnp.float32)
        amps = amps.astype(jnp.bfloat16).astype(jnp.float32)
        front = jnp.concatenate(
            [
                gain_ref[:, first + k : first + k + 1] * amps[:, k * LANES : (k + 1) * LANES]
                for k in range(pair)
            ],
            axis=1,
        ).astype(jnp.bfloat16)
        drop = jnp.dot(basis_ref[...], front, preferred_element_type=jnp.float32)
        slab[:, lanes] = (line.astype(jnp.float32) - drop).astype(jnp.bfloat16)
    if len(out_refs) == 1 and len(out_refs[0].shape) == 5:
        joined = out_refs[0]
        out_refs = [joined.at[:, step] for step in range(joined.shape[1])]
    steps = len(out_refs)
    share = chans // steps
    out_rows = out_refs[0].shape[2]
    tall = back_ref.shape[0]
    group = tall // rows_dev
    for step, out_ref in enumerate(out_refs):
        start = lax.rem(at_ref[0] + step, steps) * share
        for b in range(share // group):
            channels = pl.ds(pl.multiple_of(start + b * group, group), group)
            tile = jnp.concatenate(
                [slab[channels, u * LANES : (u + 1) * LANES] for u in range(rows_dev)], axis=0
            )
            value = jnp.dot(back_ref[...], tile, preferred_element_type=jnp.float32)
            if out_rows % tall == 0:
                target, row = divmod(b * tall, out_rows)
                out_ref[target, 0, row : row + tall, :] = value.astype(jnp.bfloat16)
            else:
                take = tall // out_rows
                out_ref[b * take : (b + 1) * take, 0] = value.reshape(
                    take, out_rows, LANES
                ).astype(jnp.bfloat16)


def clean(at, x, tile, basis, basis_t, gain, steps, targets, rows_dev, joined, after, later):
    sources = x.shape[0]
    chans = basis.shape[0]
    own = chans // sources
    swap = swap_table(min(256 // rows_dev, own), rows_dev)
    back = np.ascontiguousarray(swap_table(256 // rows_dev, rows_dev).T)
    out_rows = chans * rows_dev // (targets * steps)
    whole = lambda s, at: (0, 0)
    untouched = pl.BlockSpec(memory_space=pl.ANY)
    if joined:
        out_specs = [
            pl.BlockSpec((targets, steps, 1, out_rows, LANES), lambda s, at: (0, 0, s, 0, 0))
        ]
        out_shape = [jax.ShapeDtypeStruct((targets, steps, 2, out_rows, LANES), jnp.bfloat16)]
    else:
        out_specs = [
            pl.BlockSpec((targets, 1, out_rows, LANES), lambda s, at: (0, s, 0, 0))
        ] * steps
        out_shape = [jax.ShapeDtypeStruct((targets, 2, out_rows, LANES), jnp.bfloat16)] * steps
    aliases = {7 + len(after) + i: len(out_shape) + i for i in range(len(later))}
    result = pl.pallas_call(
        functools.partial(clean_kernel, len(after), len(later)),
        grid_spec=pltpu.PrefetchScalarGridSpec(
            num_scalar_prefetch=1,
            grid=(2,),
            in_specs=[
                pl.BlockSpec((sources, 1, own * rows_dev, LANES), lambda s, at: (0, s, 0, tile)),
                pl.BlockSpec(basis.shape, whole),
                pl.BlockSpec(basis.shape, whole),
                pl.BlockSpec(gain.shape, whole),
                pl.BlockSpec(swap.shape, whole),
                pl.BlockSpec(back.shape, whole),
            ]
            + [untouched] * (len(after) + len(later)),
            out_specs=out_specs + [untouched] * len(later),
            scratch_shapes=[pltpu.VMEM((chans, rows_dev * LANES), jnp.bfloat16)],
        ),
        out_shape=out_shape + [jax.ShapeDtypeStruct(a.shape, a.dtype) for a in later],
        input_output_aliases=aliases,
        compiler_params=params(),
        cost_estimate=small(),
        name="clean",
    )(at, x, basis, basis_t, gain, jnp.asarray(swap), jnp.asarray(back), *after, *later)
    return result[: len(out_shape)], result[len(out_shape) :]


def row_kernel(scale, group, steps, *refs):
    x_refs, table_ref, out_ref = refs[:steps], refs[steps], refs[-1]
    targets, _, chans, total, _ = out_ref.shape
    rows_dev = x_refs[0].shape[2] // chans
    tall = group * rows_dev
    for target in range(targets):
        for c in range(chans // group):
            rows = slice(c * tall, (c + 1) * tall)
            parts = [x_ref[target, s, rows, :] for x_ref in x_refs for s in range(2)]
            if tall % 16:
                parts = [part.astype(jnp.float32) for part in parts]
            tile = jnp.concatenate(parts, axis=0).astype(jnp.bfloat16)
            value = jnp.dot(table_ref[...], tile, preferred_element_type=jnp.float32) * scale
            out_ref[target, :, c * group : (c + 1) * group] = value.reshape(
                2, group, total, LANES
            ).astype(jnp.bfloat16)


def row_transform(pieces, at, chans, rows_dev, length, after):
    steps = len(pieces)
    targets, _, rows, _ = pieces[0].shape
    total = steps * rows_dev
    group = min(chans, max(1, 256 // (2 * total)))
    tables = jnp.asarray(row_tables(rows_dev, steps, group))
    table = lax.dynamic_index_in_dim(tables, at[0], 0, keepdims=False)
    scale = 1.0 / math.sqrt(total * length)
    block = math.gcd(targets, 2)
    return pl.pallas_call(
        functools.partial(row_kernel, scale, group, steps),
        grid=(targets // block,),
        in_specs=[pl.BlockSpec((block, 2, rows, LANES), lambda j: (j, 0, 0, 0))] * steps
        + [pl.BlockSpec(table.shape, lambda j: (0, 0))]
        + [pl.BlockSpec(memory_space=pl.ANY)] * len(after),
        out_specs=pl.BlockSpec((block, 2, chans, total, LANES), lambda j: (j, 0, 0, 0, 0)),
        out_shape=jax.ShapeDtypeStruct((targets, 2, chans, total, LANES), jnp.bfloat16),
        compiler_params=params(),
        cost_estimate=small(),
        name="row_transform",
    )(*pieces, table, *after)


def place_kernel(x_ref, table_ref, *refs):
    out_ref = refs[-1]
    shape = out_ref.shape
    rows = shape[0] * shape[1] * shape[2]
    tile = jnp.concatenate(
        [x_ref[y_lo].reshape(rows, LANES) for y_lo in range(RADIX)], axis=1
    )
    value = jnp.dot(tile, table_ref[...], preferred_element_type=jnp.float32)
    out_ref[...] = value.astype(jnp.bfloat16).reshape(shape)


def place(x, chunk, count, held):
    pieces, _, chans, total, _ = x.shape
    groups = pieces // RADIX
    table = order_table()
    wide = RADIX * LANES
    block = math.gcd(chans, 4)
    return pl.pallas_call(
        place_kernel,
        grid=(chans // block, groups),
        in_specs=[
            pl.BlockSpec((RADIX, 2, block, total, LANES), lambda c, g: (g, 0, c, 0, 0)),
            pl.BlockSpec(table.shape, lambda c, g: (0, 0)),
        ]
        + [pl.BlockSpec(memory_space=pl.ANY)] * len(held),
        out_specs=pl.BlockSpec(
            (2, block, total, wide), lambda c, g: (0, c, 0, chunk * groups + g)
        ),
        out_shape=jax.ShapeDtypeStruct((2, chans, total, count * groups * wide), jnp.bfloat16),
        input_output_aliases={2: 0} if held else {},
        compiler_params=params(),
        cost_estimate=small(),
        name="place",
    )(x, jnp.asarray(table), *held)


def turn_kernel(basis_ref, out_ref):
    out_ref[...] = basis_ref[...].T


def turn(basis):
    vmem = pl.BlockSpec(memory_space=pltpu.VMEM)
    return pl.pallas_call(
        turn_kernel,
        in_specs=[vmem],
        out_specs=vmem,
        out_shape=jax.ShapeDtypeStruct(basis.shape[::-1], basis.dtype),
        compiler_params=params(),
        name="turn",
    )(basis)


def hold_kernel(*refs):
    pass


def hold(arrays, after):
    if not after:
        return list(arrays)
    untouched = pl.BlockSpec(memory_space=pl.ANY)
    return pl.pallas_call(
        hold_kernel,
        in_specs=[untouched] * (len(arrays) + len(after)),
        out_specs=[untouched] * len(arrays),
        out_shape=[jax.ShapeDtypeStruct(a.shape, a.dtype) for a in arrays],
        input_output_aliases={i: i for i in range(len(arrays))},
        name="hold",
    )(*arrays, *after)


def exchange(x):
    return lax.all_to_all(x, "chan", split_axis=0, concat_axis=0, tiled=True)


def spread_rows(parts, before):
    count = len(parts)
    own, *sent = parts
    sent = hold(sent, before[1:])
    return [own] + [
        lax.ppermute(part, "uv", [(z, (z + step) % count) for z in range(count)])
        for step, part in enumerate(sent, 1)
    ]


def shards(visibility, eigen_basis, eigenvalues, noise_power):
    uv_count = lax.axis_size("uv")
    chan_count = lax.axis_size("chan")
    _, chans, rows_dev, length = visibility.shape
    count = length // chan_count // LANES
    out_chans = chans // uv_count
    at = lax.axis_index("uv").astype(jnp.int32).reshape(1)
    basis = exchange(jnp.broadcast_to(eigen_basis, (chan_count,) + eigen_basis.shape))
    basis = basis.reshape(chan_count * chans, -1)
    basis_t = turn(basis)
    gain = eigenvalues[:, None] / (eigenvalues[:, None] + noise_power[None, :])
    flat = visibility.reshape(2, chans * rows_dev, length)
    groups = [g for g in ([1], list(range(2, count))) if g and g[-1] < count]
    first = column_transform(flat, chan_count, [[0]])
    cells = [exchange(first[0])]
    sends = column_transform(flat, chan_count, groups) if groups else []
    cells += [exchange(send) for send in sends[:1]]
    sends = sends[1:]

    pieces, joined = [], None
    for k in range(count):
        last = k == count - 1 and count > 1
        results, passed = clean(
            at,
            cells[min(k, 2)],
            max(k - 2, 0),
            basis,
            basis_t,
            gain,
            uv_count,
            chan_count,
            rows_dev,
            last,
            [pieces[1][1]] if k > 1 else [],
            sends,
        )
        cells += [exchange(send) for send in passed]
        sends = []
        if last:
            joined = results[0]
        else:
            pieces.append(spread_rows(results, pieces[-1] if pieces else []))

    def transform(k):
        after = [parts[1] for parts in pieces[k + 1 : k + 2]]
        return row_transform(pieces[k], at, out_chans, rows_dev, length, after)

    def exchange_after(x, before):
        return exchange(hold([x], before)[0])

    if count == 1:
        returned = [exchange(transform(0))]
    else:
        returned = [exchange_after(transform(0), cells[-1:])]
        joined = exchange_after(joined, returned)
        pieces.append(
            spread_rows([joined[:, step] for step in range(uv_count)], pieces[-1])
        )
        for k in range(1, count - 1):
            returned.append(exchange_after(transform(k), [joined] if k == 1 else returned[-1:]))
        returned.append(transform(count - 1))
    order = list(range(count))
    if count > 2:
        order = order[:-2] + [count - 1, count - 2]
    held = []
    for k in order:
        held = [place(returned[k], k, count, held)]
    return held[0]


def solution(mesh):
    in_specs = (P(None, "chan", "uv", None), P("chan", None), P(), P("uv"))
    out_specs = P(None, ("uv", "chan"), None, None)
    return jax.shard_map(shards, mesh=mesh, in_specs=in_specs, out_specs=out_specs, check_vma=False)
```

```python
import functools
import math

import jax
import jax.numpy as jnp
import numpy as np
from jax import lax
from jax.experimental import pallas as pl
from jax.experimental.pallas import tpu as pltpu
from jax.sharding import PartitionSpec as P

LANES = 128
RADIX = 8
VMEM_BYTES = 56 * 1024 * 1024


def params():
    return pltpu.CompilerParams(vmem_limit_bytes=VMEM_BYTES)


def inner_table(size):
    position = np.arange(size)
    phase = 2.0 * np.pi * (np.outer(position, position) % size) / size
    cosine, sine = np.cos(phase), np.sin(phase)
    return np.block([[cosine, sine], [-sine, cosine]]).astype(jnp.bfloat16)


def twiddle_table(length):
    inner = length // RADIX
    phase = 2.0 * np.pi * np.outer(np.arange(RADIX), np.arange(inner)) / length
    return np.stack([np.cos(phase), np.sin(phase)], axis=1).astype(np.float32)


def order_table():
    table = np.zeros((RADIX, LANES, LANES, RADIX), np.float32)
    for y_lo in range(RADIX):
        for y_hi in range(LANES):
            table[y_lo, y_hi, y_hi, y_lo] = 1.0
    return table.reshape(RADIX * LANES, RADIX * LANES).astype(jnp.bfloat16)


def swap_table(major, minor):
    table = np.zeros((major * minor, major * minor), np.float32)
    for a in range(major):
        for b in range(minor):
            table[b * major + a, a * minor + b] = 1.0
    return table.astype(jnp.bfloat16)


def row_table(rows_dev, uv_count, group):
    total = rows_dev * uv_count
    position = np.arange(total)
    phase = 2.0 * np.pi * (np.outer(position, position) % total) / total
    cosine, sine = np.cos(phase), np.sin(phase)
    parts = np.array([[cosine, -sine], [sine, cosine]])
    parts = parts.reshape(2, 2, total, uv_count, rows_dev)
    size = 2 * group * total
    table = np.einsum("tsxzu,cd->tcxzsdu", parts, np.eye(group))
    return table.reshape(size, size).astype(jnp.bfloat16)


def butterfly8(re, im):
    def dft2(ar, ai, br, bi):
        return ar + br, ai + bi, ar - br, ai - bi

    def dft4(r, i):
        s0r, s0i, d0r, d0i = dft2(r[0], i[0], r[2], i[2])
        s1r, s1i, d1r, d1i = dft2(r[1], i[1], r[3], i[3])
        return (
            [s0r + s1r, d0r - d1i, s0r - s1r, d0r + d1i],
            [s0i + s1i, d0i + d1r, s0i - s1i, d0i - d1r],
        )

    er, ei = dft4(re[0::2], im[0::2])
    orr, oi = dft4(re[1::2], im[1::2])
    half = math.sqrt(0.5)
    turned_r = [orr[0], (orr[1] - oi[1]) * half, -oi[2], (-orr[3] - oi[3]) * half]
    turned_i = [oi[0], (orr[1] + oi[1]) * half, orr[2], (orr[3] - oi[3]) * half]
    out_r = [er[k] + turned_r[k] for k in range(4)] + [er[k] - turned_r[k] for k in range(4)]
    out_i = [ei[k] + turned_i[k] for k in range(4)] + [ei[k] - turned_i[k] for k in range(4)]
    return out_r, out_i


def column_kernel(chunks, spread, split, at_ref, x_ref, twiddle_ref, table_ref, *refs):
    if split:
        *out_refs, mid, stage = refs
    else:
        *out_refs, mid = refs
    rows, length = x_ref.shape[1:]
    inner = length // RADIX
    step = 16
    for i in range(rows // step):
        at = slice(i * step, (i + 1) * step)
        for block in range(inner // LANES):
            re, im = [], []
            for a in range(RADIX):
                lanes = slice(a * inner + block * LANES, a * inner + (block + 1) * LANES)
                re.append(x_ref[0, at, lanes].astype(jnp.float32))
                im.append(x_ref[1, at, lanes].astype(jnp.float32))
            re, im = butterfly8(re, im)
            lanes = slice(block * LANES, (block + 1) * LANES)
            other = slice(inner + block * LANES, inner + (block + 1) * LANES)
            for y_lo in range(RADIX):
                if y_lo == 0:
                    tr, ti = re[0], im[0]
                else:
                    cosine = twiddle_ref[y_lo, 0:1, lanes]
                    sine = twiddle_ref[y_lo, 1:2, lanes]
                    tr = re[y_lo] * cosine - im[y_lo] * sine
                    ti = re[y_lo] * sine + im[y_lo] * cosine
                mid[y_lo, at, lanes] = tr.astype(jnp.bfloat16)
                mid[y_lo, at, other] = ti.astype(jnp.bfloat16)
    for n, chunk in enumerate(chunks):
        for group in range(spread):
            column = (chunk * spread + group) * LANES
            table = jnp.concatenate(
                [table_ref[:, at : at + LANES] for at in (column, inner + column)], axis=1
            )
            wide = jnp.dot(
                mid[...].reshape(RADIX * rows, 2 * inner), table, preferred_element_type=jnp.float32
            ).astype(jnp.bfloat16)
            for y_lo in range(RADIX):
                for part in range(2):
                    value = wide[y_lo * rows : (y_lo + 1) * rows, part * LANES : (part + 1) * LANES]
                    if split:
                        stage[group * RADIX + y_lo, part] = value
                    else:
                        out_refs[n][group * RADIX + y_lo, part] = value
        if split:
            pieces = spread * RADIX
            for step in range(pieces):
                out_refs[n * pieces + step][...] = stage[partner(at_ref[0], step, pieces)]


def partner(at, step, count):
    if count & (count - 1):
        return (count - at + step) % count
    return at ^ step


def column_transform(x, at, pieces, chunks, split):
    _, rows, length = x.shape
    inner = length // RADIX
    block = math.gcd(rows, 64)
    if split:
        spec = pl.BlockSpec((2, block, LANES), lambda i, at: (0, i, 0))
        shape = jax.ShapeDtypeStruct((2, rows, LANES), jnp.bfloat16)
        stage = [pltpu.VMEM((pieces, 2, block, LANES), jnp.bfloat16)]
        outs = len(chunks) * pieces
    else:
        spec = pl.BlockSpec((pieces, 2, block, LANES), lambda i, at: (0, 0, i, 0))
        shape = jax.ShapeDtypeStruct((pieces, 2, rows, LANES), jnp.bfloat16)
        stage = []
        outs = len(chunks)
    return pl.pallas_call(
        functools.partial(column_kernel, chunks, pieces // RADIX, split),
        grid_spec=pltpu.PrefetchScalarGridSpec(
            num_scalar_prefetch=1,
            grid=(rows // block,),
            in_specs=[
                pl.BlockSpec((2, block, length), lambda i, at: (0, i, 0)),
                pl.BlockSpec((RADIX, 2, inner), lambda i, at: (0, 0, 0)),
                pl.BlockSpec((2 * inner, 2 * inner), lambda i, at: (0, 0)),
            ],
            out_specs=[spec] * outs,
            scratch_shapes=[pltpu.VMEM((RADIX, block, 2 * inner), jnp.bfloat16)] + stage,
        ),
        out_shape=[shape] * outs,
        compiler_params=params(),
        cost_estimate=pl.CostEstimate(
            flops=4 * rows * length * LANES * pieces * len(chunks),
            bytes_accessed=8 * rows * length,
            transcendentals=0,
        ),
        name="column_transform",
    )(at, x, jnp.asarray(twiddle_table(length)), jnp.asarray(inner_table(inner)))


def clean_kernel(split, at_ref, *refs):
    *x_refs, basis_ref, basis_t_ref, gain_ref, swap_ref, back_ref, out_ref, slab = refs
    chans = slab.shape[0]
    rows_dev = slab.shape[1] // LANES
    tall = swap_ref.shape[0]
    group = tall // rows_dev
    sources = len(x_refs) if split else x_refs[0].shape[0]
    own = chans // sources
    for source in range(sources):
        block = x_refs[source].at[0] if split else x_refs[0].at[source, 0]
        begin = partner(at_ref[0], source, sources) * own if split else source * own
        for k in range(own // group):
            turned = jnp.dot(
                swap_ref[...], block[k * tall : (k + 1) * tall, :], preferred_element_type=jnp.float32
            ).astype(jnp.bfloat16)
            channels = pl.ds(pl.multiple_of(begin + k * group, group), group)
            for u in range(rows_dev):
                slab[channels, u * LANES : (u + 1) * LANES] = turned[u * group : (u + 1) * group]
    pair = math.gcd(rows_dev, 2)
    for first in range(0, rows_dev, pair):
        lanes = slice(first * LANES, (first + pair) * LANES)
        line = slab[:, lanes]
        amps = jnp.dot(basis_t_ref[...], line, preferred_element_type=jnp.float32)
        amps = amps.astype(jnp.bfloat16).astype(jnp.float32)
        front = jnp.concatenate(
            [
                gain_ref[:, first + k : first + k + 1] * amps[:, k * LANES : (k + 1) * LANES]
                for k in range(pair)
            ],
            axis=1,
        ).astype(jnp.bfloat16)
        drop = jnp.dot(basis_ref[...], front, preferred_element_type=jnp.float32)
        slab[:, lanes] = (line.astype(jnp.float32) - drop).astype(jnp.bfloat16)
    out_rows = out_ref.shape[2]
    tall = back_ref.shape[0]
    group = tall // rows_dev
    for b in range(chans // group):
        channels = slice(b * group, (b + 1) * group)
        tile = jnp.concatenate(
            [slab[channels, u * LANES : (u + 1) * LANES] for u in range(rows_dev)], axis=0
        )
        value = jnp.dot(back_ref[...], tile, preferred_element_type=jnp.float32)
        if out_rows % tall == 0:
            target, row = divmod(b * tall, out_rows)
            out_ref[target, 0, row : row + tall, :] = value.astype(jnp.bfloat16)
        else:
            take = tall // out_rows
            out_ref[b * take : (b + 1) * take, 0] = value.reshape(take, out_rows, LANES).astype(
                jnp.bfloat16
            )


def clean(at, xs, basis, basis_t, gain, targets, rows_dev):
    split = len(xs) > 1
    chans = basis.shape[0]
    sources = len(xs) if split else xs[0].shape[0]
    own = chans // sources
    swap = swap_table(min(256 // rows_dev, own), rows_dev)
    back = np.ascontiguousarray(swap_table(256 // rows_dev, rows_dev).T)
    out_rows = chans * rows_dev // targets
    whole = lambda s, at: (0, 0)
    if split:
        spec = pl.BlockSpec((1, own * rows_dev, LANES), lambda s, at: (s, 0, 0))
    else:
        spec = pl.BlockSpec((sources, 1, own * rows_dev, LANES), lambda s, at: (0, s, 0, 0))
    return pl.pallas_call(
        functools.partial(clean_kernel, split),
        grid_spec=pltpu.PrefetchScalarGridSpec(
            num_scalar_prefetch=1,
            grid=(2,),
            in_specs=[spec] * len(xs)
            + [
                pl.BlockSpec(basis.shape, whole),
                pl.BlockSpec(basis.shape, whole),
                pl.BlockSpec(gain.shape, whole),
                pl.BlockSpec(swap.shape, whole),
                pl.BlockSpec(back.shape, whole),
            ],
            out_specs=pl.BlockSpec((targets, 1, out_rows, LANES), lambda s, at: (0, s, 0, 0)),
            scratch_shapes=[pltpu.VMEM((chans, rows_dev * LANES), jnp.bfloat16)],
        ),
        out_shape=jax.ShapeDtypeStruct((targets, 2, out_rows, LANES), jnp.bfloat16),
        compiler_params=params(),
        cost_estimate=pl.CostEstimate(
            flops=12 * chans * chans * rows_dev * LANES,
            bytes_accessed=8 * chans * rows_dev * LANES,
            transcendentals=0,
        ),
        name="clean",
    )(at, *xs, basis, basis_t, gain, jnp.asarray(swap), jnp.asarray(back))


def image_kernel(scale, x_ref, table_ref, order_ref, *refs):
    out_ref = refs[-1]
    z, _, parts, rows, _ = x_ref.shape
    tiles = []
    for y_lo in range(RADIX):
        tile = x_ref[:, y_lo]
        if rows % 16:
            tile = tile.astype(jnp.float32)
        tile = tile.reshape(z * parts * rows, LANES).astype(jnp.bfloat16)
        tiles.append(tile)
    value = jnp.dot(table_ref[...], jnp.concatenate(tiles, axis=1), preferred_element_type=jnp.float32)
    value = (value * scale).astype(jnp.bfloat16)
    value = jnp.dot(value, order_ref[...], preferred_element_type=jnp.float32)
    out_ref[...] = value.astype(jnp.bfloat16).reshape(out_ref.shape)


def image(x, chunk, count, rows_dev, held):
    z, pieces, _, rows, _ = x.shape
    chans = rows // rows_dev
    total = z * rows_dev
    spread = pieces // RADIX
    wide = RADIX * LANES
    group = min(chans, max(1, 256 // (2 * total)))
    table = row_table(rows_dev, z, group)
    order = order_table()
    scale = 1.0 / math.sqrt(total * count * spread * wide)
    return pl.pallas_call(
        functools.partial(image_kernel, scale),
        grid=(chans // group, spread),
        in_specs=[
            pl.BlockSpec((z, RADIX, 2, group * rows_dev, LANES), lambda c, g: (0, g, 0, c, 0)),
            pl.BlockSpec(table.shape, lambda c, g: (0, 0)),
            pl.BlockSpec(order.shape, lambda c, g: (0, 0)),
        ]
        + [pl.BlockSpec(memory_space=pl.ANY)] * len(held),
        out_specs=pl.BlockSpec(
            (2, group, total, wide), lambda c, g: (0, c, 0, chunk * spread + g)
        ),
        out_shape=jax.ShapeDtypeStruct((2, chans, total, count * spread * wide), jnp.bfloat16),
        input_output_aliases={3: 0} if held else {},
        compiler_params=params(),
        cost_estimate=pl.CostEstimate(
            flops=4 * pieces * chans * total * LANES * wide,
            bytes_accessed=8 * pieces * chans * total * LANES,
            transcendentals=0,
        ),
        name="image",
    )(x, jnp.asarray(table), jnp.asarray(order), *held)


def turn_kernel(basis_ref, out_ref):
    out_ref[...] = basis_ref[...].T


def turn(basis):
    vmem = pl.BlockSpec(memory_space=pltpu.VMEM)
    return pl.pallas_call(
        turn_kernel,
        in_specs=[vmem],
        out_specs=vmem,
        out_shape=jax.ShapeDtypeStruct(basis.shape[::-1], basis.dtype),
        compiler_params=params(),
        name="turn",
    )(basis)


def exchange(x, axes):
    return lax.all_to_all(x, axes, split_axis=0, concat_axis=0, tiled=True)


def scatter(pieces):
    count = len(pieces)
    return [pieces[0]] + [
        lax.ppermute(
            pieces[step], "chan", [(j, int(partner(np.int32(j), step, count))) for j in range(count)]
        )
        for step in range(1, count)
    ]


def shards(visibility, eigen_basis, eigenvalues, noise_power):
    uv_count = lax.axis_size("uv")
    chan_count = lax.axis_size("chan")
    _, chans, rows_dev, length = visibility.shape
    count = length // chan_count // LANES
    targets = uv_count * chan_count
    at = lax.axis_index("chan").astype(jnp.int32).reshape(1)
    basis = exchange(jnp.broadcast_to(eigen_basis, (chan_count,) + eigen_basis.shape), "chan")
    basis = basis.reshape(chan_count * chans, -1)
    basis_t = turn(basis)
    gain = eigenvalues[:, None] / (eigenvalues[:, None] + noise_power[None, :])
    flat = visibility.reshape(2, chans * rows_dev, length)
    first = column_transform(flat, at, chan_count, [0], False)
    cells = [[exchange(first[0], "chan")]]
    if count > 1:
        sends = column_transform(flat, at, chan_count, list(range(1, count)), True)
        cells += [
            scatter(sends[k * chan_count : (k + 1) * chan_count]) for k in range(count - 1)
        ]
    held = []
    for k in range(count):
        cleaned = clean(at, cells[k], basis, basis_t, gain, targets, rows_dev)
        planes = exchange(cleaned, ("uv", "chan"))
        planes = planes.reshape((uv_count, chan_count) + planes.shape[1:])
        held = [image(planes, k, count, rows_dev, held)]
    return held[0]


def solution(mesh):
    in_specs = (P(None, "chan", "uv", None), P("chan", None), P(), P("uv"))
    out_specs = P(None, ("uv", "chan"), None, None)
    return jax.shard_map(shards, mesh=mesh, in_specs=in_specs, out_specs=out_specs, check_vma=False)
```

```python
import functools
import math

import jax
import jax.numpy as jnp
import numpy as np
from jax import lax
from jax.experimental import pallas as pl
from jax.experimental.pallas import tpu as pltpu
from jax.sharding import PartitionSpec as P

LANES = 128
RADIX = 8
VMEM_BYTES = 56 * 1024 * 1024


def params():
    return pltpu.CompilerParams(vmem_limit_bytes=VMEM_BYTES)


def inner_table(size):
    position = np.arange(size)
    phase = 2.0 * np.pi * (np.outer(position, position) % size) / size
    cosine, sine = np.cos(phase), np.sin(phase)
    return np.block([[cosine, sine], [-sine, cosine]]).astype(jnp.bfloat16)


def twiddle_table(length):
    inner = length // RADIX
    phase = 2.0 * np.pi * np.outer(np.arange(RADIX), np.arange(inner)) / length
    return np.stack([np.cos(phase), np.sin(phase)], axis=1).astype(np.float32)


def order_table():
    table = np.zeros((RADIX, LANES, LANES, RADIX), np.float32)
    for y_lo in range(RADIX):
        for y_hi in range(LANES):
            table[y_lo, y_hi, y_hi, y_lo] = 1.0
    return table.reshape(RADIX * LANES, RADIX * LANES).astype(jnp.bfloat16)


def swap_table(major, minor):
    table = np.zeros((major * minor, major * minor), np.float32)
    for a in range(major):
        for b in range(minor):
            table[b * major + a, a * minor + b] = 1.0
    return table.astype(jnp.bfloat16)


def row_table(rows_dev, uv_count, group):
    total = rows_dev * uv_count
    position = np.arange(total)
    phase = 2.0 * np.pi * (np.outer(position, position) % total) / total
    cosine, sine = np.cos(phase), np.sin(phase)
    parts = np.array([[cosine, -sine], [sine, cosine]])
    parts = parts.reshape(2, 2, total, uv_count, rows_dev)
    size = 2 * group * total
    table = np.einsum("tsxzu,cd->tcxzsdu", parts, np.eye(group))
    return table.reshape(size, size).astype(jnp.bfloat16)


def butterfly8(re, im):
    def dft2(ar, ai, br, bi):
        return ar + br, ai + bi, ar - br, ai - bi

    def dft4(r, i):
        s0r, s0i, d0r, d0i = dft2(r[0], i[0], r[2], i[2])
        s1r, s1i, d1r, d1i = dft2(r[1], i[1], r[3], i[3])
        return (
            [s0r + s1r, d0r - d1i, s0r - s1r, d0r + d1i],
            [s0i + s1i, d0i + d1r, s0i - s1i, d0i - d1r],
        )

    er, ei = dft4(re[0::2], im[0::2])
    orr, oi = dft4(re[1::2], im[1::2])
    half = math.sqrt(0.5)
    turned_r = [orr[0], (orr[1] - oi[1]) * half, -oi[2], (-orr[3] - oi[3]) * half]
    turned_i = [oi[0], (orr[1] + oi[1]) * half, orr[2], (orr[3] - oi[3]) * half]
    out_r = [er[k] + turned_r[k] for k in range(4)] + [er[k] - turned_r[k] for k in range(4)]
    out_i = [ei[k] + turned_i[k] for k in range(4)] + [ei[k] - turned_i[k] for k in range(4)]
    return out_r, out_i


def column_kernel(chunks, spread, split, at_ref, x_ref, twiddle_ref, table_ref, *refs):
    if split:
        *out_refs, mid, stage = refs
    else:
        *out_refs, mid = refs
    rows, length = x_ref.shape[1:]
    inner = length // RADIX
    step = 16
    for i in range(rows // step):
        at = slice(i * step, (i + 1) * step)
        for block in range(inner // LANES):
            re, im = [], []
            for a in range(RADIX):
                lanes = slice(a * inner + block * LANES, a * inner + (block + 1) * LANES)
                re.append(x_ref[0, at, lanes].astype(jnp.float32))
                im.append(x_ref[1, at, lanes].astype(jnp.float32))
            re, im = butterfly8(re, im)
            lanes = slice(block * LANES, (block + 1) * LANES)
            other = slice(inner + block * LANES, inner + (block + 1) * LANES)
            for y_lo in range(RADIX):
                if y_lo == 0:
                    tr, ti = re[0], im[0]
                else:
                    cosine = twiddle_ref[y_lo, 0:1, lanes]
                    sine = twiddle_ref[y_lo, 1:2, lanes]
                    tr = re[y_lo] * cosine - im[y_lo] * sine
                    ti = re[y_lo] * sine + im[y_lo] * cosine
                mid[y_lo, at, lanes] = tr.astype(jnp.bfloat16)
                mid[y_lo, at, other] = ti.astype(jnp.bfloat16)
    for n, chunk in enumerate(chunks):
        for group in range(spread):
            column = (chunk * spread + group) * LANES
            table = jnp.concatenate(
                [table_ref[:, at : at + LANES] for at in (column, inner + column)], axis=1
            )
            wide = jnp.dot(
                mid[...].reshape(RADIX * rows, 2 * inner), table, preferred_element_type=jnp.float32
            ).astype(jnp.bfloat16)
            for y_lo in range(RADIX):
                for part in range(2):
                    value = wide[y_lo * rows : (y_lo + 1) * rows, part * LANES : (part + 1) * LANES]
                    if split:
                        stage[group * RADIX + y_lo, part] = value
                    else:
                        out_refs[n][group * RADIX + y_lo, part] = value
        if split:
            pieces = spread * RADIX
            for step in range(pieces):
                out_refs[n * pieces + step][...] = stage[partner(at_ref[0], step, pieces)]


def partner(at, step, count):
    if count & (count - 1):
        return (count - at + step) % count
    if step:
        step = sorted(range(1, count), key=lambda n: (-bin(n // 2).count("1"), -n))[step - 1]
    return at ^ step


def column_transform(x, at, pieces, chunks, split):
    _, rows, length = x.shape
    inner = length // RADIX
    block = math.gcd(rows, 64)
    if split:
        spec = pl.BlockSpec((2, block, LANES), lambda i, at: (0, i, 0))
        shape = jax.ShapeDtypeStruct((2, rows, LANES), jnp.bfloat16)
        stage = [pltpu.VMEM((pieces, 2, block, LANES), jnp.bfloat16)]
        outs = len(chunks) * pieces
    else:
        spec = pl.BlockSpec((pieces, 2, block, LANES), lambda i, at: (0, 0, i, 0))
        shape = jax.ShapeDtypeStruct((pieces, 2, rows, LANES), jnp.bfloat16)
        stage = []
        outs = len(chunks)
    return pl.pallas_call(
        functools.partial(column_kernel, chunks, pieces // RADIX, split),
        grid_spec=pltpu.PrefetchScalarGridSpec(
            num_scalar_prefetch=1,
            grid=(rows // block,),
            in_specs=[
                pl.BlockSpec((2, block, length), lambda i, at: (0, i, 0)),
                pl.BlockSpec((RADIX, 2, inner), lambda i, at: (0, 0, 0)),
                pl.BlockSpec((2 * inner, 2 * inner), lambda i, at: (0, 0)),
            ],
            out_specs=[spec] * outs,
            scratch_shapes=[pltpu.VMEM((RADIX, block, 2 * inner), jnp.bfloat16)] + stage,
        ),
        out_shape=[shape] * outs,
        compiler_params=params(),
        cost_estimate=pl.CostEstimate(
            flops=4 * rows * length * LANES * pieces * len(chunks),
            bytes_accessed=8 * rows * length,
            transcendentals=0,
        ),
        name="column_transform",
    )(at, x, jnp.asarray(twiddle_table(length)), jnp.asarray(inner_table(inner)))


def clean_kernel(split, waits, at_ref, *refs):
    *refs, out_ref, slab = refs
    *x_refs, basis_ref, basis_t_ref, gain_ref, swap_ref, back_ref = refs[: len(refs) - waits]
    chans = slab.shape[0]
    rows_dev = slab.shape[1] // LANES
    tall = swap_ref.shape[0]
    group = tall // rows_dev
    sources = len(x_refs) if split else x_refs[0].shape[0]
    own = chans // sources
    for source in range(sources):
        block = x_refs[source].at[0] if split else x_refs[0].at[source, 0]
        begin = partner(at_ref[0], source, sources) * own if split else source * own
        for k in range(own // group):
            turned = jnp.dot(
                swap_ref[...], block[k * tall : (k + 1) * tall, :], preferred_element_type=jnp.float32
            ).astype(jnp.bfloat16)
            channels = pl.ds(pl.multiple_of(begin + k * group, group), group)
            for u in range(rows_dev):
                slab[channels, u * LANES : (u + 1) * LANES] = turned[u * group : (u + 1) * group]
    pair = math.gcd(rows_dev, 2)
    for first in range(0, rows_dev, pair):
        lanes = slice(first * LANES, (first + pair) * LANES)
        line = slab[:, lanes]
        amps = jnp.dot(basis_t_ref[...], line, preferred_element_type=jnp.float32)
        amps = amps.astype(jnp.bfloat16).astype(jnp.float32)
        front = jnp.concatenate(
            [
                gain_ref[:, first + k : first + k + 1] * amps[:, k * LANES : (k + 1) * LANES]
                for k in range(pair)
            ],
            axis=1,
        ).astype(jnp.bfloat16)
        drop = jnp.dot(basis_ref[...], front, preferred_element_type=jnp.float32)
        slab[:, lanes] = (line.astype(jnp.float32) - drop).astype(jnp.bfloat16)
    out_rows = out_ref.shape[3]
    tall = back_ref.shape[0]
    group = tall // rows_dev
    for b in range(chans // group):
        channels = slice(b * group, (b + 1) * group)
        tile = jnp.concatenate(
            [slab[channels, u * LANES : (u + 1) * LANES] for u in range(rows_dev)], axis=0
        )
        value = jnp.dot(back_ref[...], tile, preferred_element_type=jnp.float32)
        if out_rows % tall == 0:
            target, row = divmod(b * tall, out_rows)
            out_ref[target, 0, 0, row : row + tall, :] = value.astype(jnp.bfloat16)
        else:
            take = tall // out_rows
            out_ref[b * take : (b + 1) * take, 0, 0] = value.reshape(
                take, out_rows, LANES
            ).astype(jnp.bfloat16)


def clean(at, xs, basis, basis_t, gain, targets, rows_dev, slot, slots, before):
    split = len(xs) > 1
    chans = basis.shape[0]
    sources = len(xs) if split else xs[0].shape[0]
    own = chans // sources
    swap = swap_table(min(256 // rows_dev, own), rows_dev)
    back = np.ascontiguousarray(swap_table(256 // rows_dev, rows_dev).T)
    out_rows = chans * rows_dev // targets
    whole = lambda s, at: (0, 0)
    if split:
        spec = pl.BlockSpec((1, own * rows_dev, LANES), lambda s, at: (s, 0, 0))
    else:
        spec = pl.BlockSpec((sources, 1, own * rows_dev, LANES), lambda s, at: (0, s, 0, 0))
    return pl.pallas_call(
        functools.partial(clean_kernel, split, len(before)),
        grid_spec=pltpu.PrefetchScalarGridSpec(
            num_scalar_prefetch=1,
            grid=(2,),
            in_specs=[spec] * len(xs)
            + [
                pl.BlockSpec(basis.shape, whole),
                pl.BlockSpec(basis.shape, whole),
                pl.BlockSpec(gain.shape, whole),
                pl.BlockSpec(swap.shape, whole),
                pl.BlockSpec(back.shape, whole),
            ]
            + [pl.BlockSpec(memory_space=pl.ANY)] * len(before),
            out_specs=pl.BlockSpec(
                (targets, 1, 1, out_rows, LANES), lambda s, at: (0, slot, s, 0, 0)
            ),
            scratch_shapes=[pltpu.VMEM((chans, rows_dev * LANES), jnp.bfloat16)],
        ),
        out_shape=jax.ShapeDtypeStruct((targets, slots, 2, out_rows, LANES), jnp.bfloat16),
        input_output_aliases={6 + len(xs): 0} if slot else {},
        compiler_params=params(),
        cost_estimate=pl.CostEstimate(
            flops=12 * chans * chans * rows_dev * LANES,
            bytes_accessed=8 * chans * rows_dev * LANES,
            transcendentals=0,
        ),
        name="clean",
    )(at, *xs, basis, basis_t, gain, jnp.asarray(swap), jnp.asarray(back), *before)


def image_kernel(scale, x_ref, table_ref, order_ref, *refs):
    out_ref = refs[-1]
    z, _, _, parts, rows, _ = x_ref.shape
    tiles = []
    for y_lo in range(RADIX):
        tile = x_ref[:, y_lo, 0]
        if rows % 16:
            tile = tile.astype(jnp.float32)
        tile = tile.reshape(z * parts * rows, LANES).astype(jnp.bfloat16)
        tiles.append(tile)
    value = jnp.dot(table_ref[...], jnp.concatenate(tiles, axis=1), preferred_element_type=jnp.float32)
    value = (value * scale).astype(jnp.bfloat16)
    value = jnp.dot(value, order_ref[...], preferred_element_type=jnp.float32)
    out_ref[...] = value.astype(jnp.bfloat16).reshape(out_ref.shape)


def image(x, slot, chunk, count, rows_dev, held):
    z, pieces, _, _, rows, _ = x.shape
    chans = rows // rows_dev
    total = z * rows_dev
    spread = pieces // RADIX
    wide = RADIX * LANES
    group = min(chans, max(1, 256 // (2 * total)))
    table = row_table(rows_dev, z, group)
    order = order_table()
    scale = 1.0 / math.sqrt(total * count * spread * wide)
    return pl.pallas_call(
        functools.partial(image_kernel, scale),
        grid=(chans // group, spread),
        in_specs=[
            pl.BlockSpec(
                (z, RADIX, 1, 2, group * rows_dev, LANES), lambda c, g: (0, g, slot, 0, c, 0)
            ),
            pl.BlockSpec(table.shape, lambda c, g: (0, 0)),
            pl.BlockSpec(order.shape, lambda c, g: (0, 0)),
        ]
        + [pl.BlockSpec(memory_space=pl.ANY)] * len(held),
        out_specs=pl.BlockSpec(
            (2, group, total, wide), lambda c, g: (0, c, 0, chunk * spread + g)
        ),
        out_shape=jax.ShapeDtypeStruct((2, chans, total, count * spread * wide), jnp.bfloat16),
        input_output_aliases={3: 0} if held else {},
        compiler_params=params(),
        cost_estimate=pl.CostEstimate(
            flops=4 * pieces * chans * total * LANES * wide,
            bytes_accessed=8 * pieces * chans * total * LANES,
            transcendentals=0,
        ),
        name="image",
    )(x, jnp.asarray(table), jnp.asarray(order), *held)


def turn_kernel(basis_ref, out_ref):
    out_ref[...] = basis_ref[...].T


def turn(basis):
    vmem = pl.BlockSpec(memory_space=pltpu.VMEM)
    return pl.pallas_call(
        turn_kernel,
        in_specs=[vmem],
        out_specs=vmem,
        out_shape=jax.ShapeDtypeStruct(basis.shape[::-1], basis.dtype),
        compiler_params=params(),
        name="turn",
    )(basis)


def exchange(x, axes):
    return lax.all_to_all(x, axes, split_axis=0, concat_axis=0, tiled=True)


def scatter(pieces):
    count = len(pieces)
    return [pieces[0]] + [
        lax.ppermute(
            pieces[step], "chan", [(j, int(partner(np.int32(j), step, count))) for j in range(count)]
        )
        for step in range(1, count)
    ]


def shards(visibility, eigen_basis, eigenvalues, noise_power):
    uv_count = lax.axis_size("uv")
    chan_count = lax.axis_size("chan")
    _, chans, rows_dev, length = visibility.shape
    count = length // chan_count // LANES
    targets = uv_count * chan_count
    at = lax.axis_index("chan").astype(jnp.int32).reshape(1)
    basis = exchange(jnp.broadcast_to(eigen_basis, (chan_count,) + eigen_basis.shape), "chan")
    basis = basis.reshape(chan_count * chans, -1)
    basis_t = turn(basis)
    gain = eigenvalues[:, None] / (eigenvalues[:, None] + noise_power[None, :])
    flat = visibility.reshape(2, chans * rows_dev, length)
    first = column_transform(flat, at, chan_count, [0], False)
    cells = [[exchange(first[0], "chan")]]
    if count > 1:
        sends = column_transform(flat, at, chan_count, list(range(1, count)), True)
        cells += [
            scatter(sends[k * chan_count : (k + 1) * chan_count]) for k in range(count - 1)
        ]
    groups = [[0]] + [g for g in (list(range(1, count - 1)), [count - 1]) if g and count > 1]
    held, cleaned = [], []
    for chunks in groups:
        for slot, k in enumerate(chunks):
            cleaned = [
                clean(
                    at, cells[k], basis, basis_t, gain, targets, rows_dev, slot, len(chunks), cleaned
                )
            ]
        planes = exchange(cleaned[0], ("uv", "chan"))
        planes = planes.reshape((uv_count, chan_count) + planes.shape[1:])
        for slot, k in enumerate(chunks):
            held = [image(planes, slot, k, count, rows_dev, held)]
    return held[0]


def solution(mesh):
    in_specs = (P(None, "chan", "uv", None), P("chan", None), P(), P("uv"))
    out_specs = P(None, ("uv", "chan"), None, None)
    return jax.shard_map(shards, mesh=mesh, in_specs=in_specs, out_specs=out_specs, check_vma=False)
```

```python
import functools
import math

import jax
import jax.numpy as jnp
import numpy as np
from jax import lax
from jax.experimental import pallas as pl
from jax.experimental.pallas import tpu as pltpu
from jax.sharding import PartitionSpec as P

LANES = 128
RADIX = 8
VMEM_BYTES = 56 * 1024 * 1024


def params():
    return pltpu.CompilerParams(vmem_limit_bytes=VMEM_BYTES)


def inner_table(size):
    position = np.arange(size)
    phase = 2.0 * np.pi * (np.outer(position, position) % size) / size
    cosine, sine = np.cos(phase), np.sin(phase)
    return np.block([[cosine, sine], [-sine, cosine]]).astype(jnp.bfloat16)


def twiddle_table(length):
    inner = length // RADIX
    phase = 2.0 * np.pi * np.outer(np.arange(RADIX), np.arange(inner)) / length
    return np.stack([np.cos(phase), np.sin(phase)], axis=1).astype(np.float32)


def order_table():
    table = np.zeros((RADIX, LANES, LANES, RADIX), np.float32)
    for y_lo in range(RADIX):
        for y_hi in range(LANES):
            table[y_lo, y_hi, y_hi, y_lo] = 1.0
    return table.reshape(RADIX * LANES, RADIX * LANES).astype(jnp.bfloat16)


def swap_table(major, minor):
    table = np.zeros((major * minor, major * minor), np.float32)
    for a in range(major):
        for b in range(minor):
            table[b * major + a, a * minor + b] = 1.0
    return table.astype(jnp.bfloat16)


def row_table(rows_dev, uv_count, group):
    total = rows_dev * uv_count
    position = np.arange(total)
    phase = 2.0 * np.pi * (np.outer(position, position) % total) / total
    cosine, sine = np.cos(phase), np.sin(phase)
    parts = np.array([[cosine, -sine], [sine, cosine]])
    parts = parts.reshape(2, 2, total, uv_count, rows_dev)
    size = 2 * group * total
    table = np.einsum("tsxzu,cd->tcxzsdu", parts, np.eye(group))
    return table.reshape(size, size).astype(jnp.bfloat16)


def butterfly8(re, im):
    def dft2(ar, ai, br, bi):
        return ar + br, ai + bi, ar - br, ai - bi

    def dft4(r, i):
        s0r, s0i, d0r, d0i = dft2(r[0], i[0], r[2], i[2])
        s1r, s1i, d1r, d1i = dft2(r[1], i[1], r[3], i[3])
        return (
            [s0r + s1r, d0r - d1i, s0r - s1r, d0r + d1i],
            [s0i + s1i, d0i + d1r, s0i - s1i, d0i - d1r],
        )

    er, ei = dft4(re[0::2], im[0::2])
    orr, oi = dft4(re[1::2], im[1::2])
    half = math.sqrt(0.5)
    turned_r = [orr[0], (orr[1] - oi[1]) * half, -oi[2], (-orr[3] - oi[3]) * half]
    turned_i = [oi[0], (orr[1] + oi[1]) * half, orr[2], (orr[3] - oi[3]) * half]
    out_r = [er[k] + turned_r[k] for k in range(4)] + [er[k] - turned_r[k] for k in range(4)]
    out_i = [ei[k] + turned_i[k] for k in range(4)] + [ei[k] - turned_i[k] for k in range(4)]
    return out_r, out_i


def column_kernel(chunks, spread, split, at_ref, x_ref, twiddle_ref, table_ref, *refs):
    if split:
        *out_refs, mid, stage = refs
    else:
        *out_refs, mid = refs
    rows, length = x_ref.shape[1:]
    inner = length // RADIX
    step = 16
    for i in range(rows // step):
        at = slice(i * step, (i + 1) * step)
        for block in range(inner // LANES):
            re, im = [], []
            for a in range(RADIX):
                lanes = slice(a * inner + block * LANES, a * inner + (block + 1) * LANES)
                re.append(x_ref[0, at, lanes].astype(jnp.float32))
                im.append(x_ref[1, at, lanes].astype(jnp.float32))
            re, im = butterfly8(re, im)
            lanes = slice(block * LANES, (block + 1) * LANES)
            other = slice(inner + block * LANES, inner + (block + 1) * LANES)
            for y_lo in range(RADIX):
                if y_lo == 0:
                    tr, ti = re[0], im[0]
                else:
                    cosine = twiddle_ref[y_lo, 0:1, lanes]
                    sine = twiddle_ref[y_lo, 1:2, lanes]
                    tr = re[y_lo] * cosine - im[y_lo] * sine
                    ti = re[y_lo] * sine + im[y_lo] * cosine
                mid[y_lo, at, lanes] = tr.astype(jnp.bfloat16)
                mid[y_lo, at, other] = ti.astype(jnp.bfloat16)
    for n, chunk in enumerate(chunks):
        for group in range(spread):
            column = (chunk * spread + group) * LANES
            table = jnp.concatenate(
                [table_ref[:, at : at + LANES] for at in (column, inner + column)], axis=1
            )
            wide = jnp.dot(
                mid[...].reshape(RADIX * rows, 2 * inner), table, preferred_element_type=jnp.float32
            ).astype(jnp.bfloat16)
            for y_lo in range(RADIX):
                for part in range(2):
                    value = wide[y_lo * rows : (y_lo + 1) * rows, part * LANES : (part + 1) * LANES]
                    if split:
                        stage[group * RADIX + y_lo, part] = value
                    else:
                        out_refs[n][group * RADIX + y_lo, part] = value
        if split:
            pieces = spread * RADIX
            for step in range(pieces):
                out_refs[n * pieces + step][...] = stage[partner(at_ref[0], step, pieces)]


def partner(at, step, count):
    if count & (count - 1):
        return (count - at + step) % count
    if step:
        step = sorted(range(1, count), key=lambda n: (-bin(n // 2).count("1"), -n))[step - 1]
    return at ^ step


def column_transform(x, at, pieces, chunks, split):
    _, rows, length = x.shape
    inner = length // RADIX
    block = math.gcd(rows, 64)
    if split:
        spec = pl.BlockSpec((2, block, LANES), lambda i, at: (0, i, 0))
        shape = jax.ShapeDtypeStruct((2, rows, LANES), jnp.bfloat16)
        stage = [pltpu.VMEM((pieces, 2, block, LANES), jnp.bfloat16)]
        outs = len(chunks) * pieces
    else:
        spec = pl.BlockSpec((pieces, 2, block, LANES), lambda i, at: (0, 0, i, 0))
        shape = jax.ShapeDtypeStruct((pieces, 2, rows, LANES), jnp.bfloat16)
        stage = []
        outs = len(chunks)
    return pl.pallas_call(
        functools.partial(column_kernel, chunks, pieces // RADIX, split),
        grid_spec=pltpu.PrefetchScalarGridSpec(
            num_scalar_prefetch=1,
            grid=(rows // block,),
            in_specs=[
                pl.BlockSpec((2, block, length), lambda i, at: (0, i, 0)),
                pl.BlockSpec((RADIX, 2, inner), lambda i, at: (0, 0, 0)),
                pl.BlockSpec((2 * inner, 2 * inner), lambda i, at: (0, 0)),
            ],
            out_specs=[spec] * outs,
            scratch_shapes=[pltpu.VMEM((RADIX, block, 2 * inner), jnp.bfloat16)] + stage,
        ),
        out_shape=[shape] * outs,
        compiler_params=params(),
        cost_estimate=pl.CostEstimate(
            flops=4 * rows * length * LANES * pieces * len(chunks),
            bytes_accessed=8 * rows * length,
            transcendentals=0,
        ),
        name="column_transform",
    )(at, x, jnp.asarray(twiddle_table(length)), jnp.asarray(inner_table(inner)))


def clean_kernel(split, waits, at_ref, *refs):
    *refs, out_ref, slab = refs
    *x_refs, basis_ref, basis_t_ref, gain_ref, swap_ref, back_ref = refs[: len(refs) - waits]
    chans = slab.shape[0]
    rows_dev = slab.shape[1] // LANES
    tall = swap_ref.shape[0]
    group = tall // rows_dev
    sources = len(x_refs) if split else x_refs[0].shape[0]
    own = chans // sources
    for source in range(sources):
        block = x_refs[source].at[0] if split else x_refs[0].at[source, 0]
        begin = partner(at_ref[0], source, sources) * own if split else source * own
        for k in range(own // group):
            turned = jnp.dot(
                swap_ref[...], block[k * tall : (k + 1) * tall, :], preferred_element_type=jnp.float32
            ).astype(jnp.bfloat16)
            channels = pl.ds(pl.multiple_of(begin + k * group, group), group)
            for u in range(rows_dev):
                slab[channels, u * LANES : (u + 1) * LANES] = turned[u * group : (u + 1) * group]
    pair = math.gcd(rows_dev, 2)
    for first in range(0, rows_dev, pair):
        lanes = slice(first * LANES, (first + pair) * LANES)
        line = slab[:, lanes]
        amps = jnp.dot(basis_t_ref[...], line, preferred_element_type=jnp.float32)
        amps = amps.astype(jnp.bfloat16).astype(jnp.float32)
        front = jnp.concatenate(
            [
                gain_ref[:, first + k : first + k + 1] * amps[:, k * LANES : (k + 1) * LANES]
                for k in range(pair)
            ],
            axis=1,
        ).astype(jnp.bfloat16)
        drop = jnp.dot(basis_ref[...], front, preferred_element_type=jnp.float32)
        slab[:, lanes] = (line.astype(jnp.float32) - drop).astype(jnp.bfloat16)
    out_rows = out_ref.shape[3]
    tall = back_ref.shape[0]
    group = tall // rows_dev
    for b in range(chans // group):
        channels = slice(b * group, (b + 1) * group)
        tile = jnp.concatenate(
            [slab[channels, u * LANES : (u + 1) * LANES] for u in range(rows_dev)], axis=0
        )
        value = jnp.dot(back_ref[...], tile, preferred_element_type=jnp.float32)
        if out_rows % tall == 0:
            target, row = divmod(b * tall, out_rows)
            out_ref[target, 0, 0, row : row + tall, :] = value.astype(jnp.bfloat16)
        else:
            take = tall // out_rows
            out_ref[b * take : (b + 1) * take, 0, 0] = value.reshape(
                take, out_rows, LANES
            ).astype(jnp.bfloat16)


def clean(at, xs, basis, basis_t, gain, targets, rows_dev, slot, slots, before):
    split = len(xs) > 1
    chans = basis.shape[0]
    sources = len(xs) if split else xs[0].shape[0]
    own = chans // sources
    swap = swap_table(min(256 // rows_dev, own), rows_dev)
    back = np.ascontiguousarray(swap_table(256 // rows_dev, rows_dev).T)
    out_rows = chans * rows_dev // targets
    whole = lambda s, at: (0, 0)
    if split:
        spec = pl.BlockSpec((1, own * rows_dev, LANES), lambda s, at: (s, 0, 0))
    else:
        spec = pl.BlockSpec((sources, 1, own * rows_dev, LANES), lambda s, at: (0, s, 0, 0))
    return pl.pallas_call(
        functools.partial(clean_kernel, split, len(before)),
        grid_spec=pltpu.PrefetchScalarGridSpec(
            num_scalar_prefetch=1,
            grid=(2,),
            in_specs=[spec] * len(xs)
            + [
                pl.BlockSpec(basis.shape, whole),
                pl.BlockSpec(basis.shape, whole),
                pl.BlockSpec(gain.shape, whole),
                pl.BlockSpec(swap.shape, whole),
                pl.BlockSpec(back.shape, whole),
            ]
            + [pl.BlockSpec(memory_space=pl.ANY)] * len(before),
            out_specs=pl.BlockSpec(
                (targets, 1, 1, out_rows, LANES), lambda s, at: (0, slot, s, 0, 0)
            ),
            scratch_shapes=[pltpu.VMEM((chans, rows_dev * LANES), jnp.bfloat16)],
        ),
        out_shape=jax.ShapeDtypeStruct((targets, slots, 2, out_rows, LANES), jnp.bfloat16),
        input_output_aliases={6 + len(xs): 0} if slot else {},
        compiler_params=params(),
        cost_estimate=pl.CostEstimate(
            flops=12 * chans * chans * rows_dev * LANES,
            bytes_accessed=8 * chans * rows_dev * LANES,
            transcendentals=0,
        ),
        name="clean",
    )(at, *xs, basis, basis_t, gain, jnp.asarray(swap), jnp.asarray(back), *before)


def image_kernel(scale, x_ref, table_ref, order_ref, *refs):
    out_ref = refs[-1]
    z, _, _, parts, rows, _ = x_ref.shape
    tiles = []
    for y_lo in range(RADIX):
        tile = x_ref[:, y_lo, 0]
        if rows % 16:
            tile = tile.astype(jnp.float32)
        tile = tile.reshape(z * parts * rows, LANES).astype(jnp.bfloat16)
        tiles.append(tile)
    value = jnp.dot(table_ref[...], jnp.concatenate(tiles, axis=1), preferred_element_type=jnp.float32)
    value = (value * scale).astype(jnp.bfloat16)
    value = jnp.dot(value, order_ref[...], preferred_element_type=jnp.float32)
    out_ref[...] = value.astype(jnp.bfloat16).reshape(out_ref.shape)


def image(x, slot, chunk, count, rows_dev, held):
    z, pieces, _, _, rows, _ = x.shape
    chans = rows // rows_dev
    total = z * rows_dev
    spread = pieces // RADIX
    wide = RADIX * LANES
    group = min(chans, max(1, 256 // (2 * total)))
    table = row_table(rows_dev, z, group)
    order = order_table()
    scale = 1.0 / math.sqrt(total * count * spread * wide)
    return pl.pallas_call(
        functools.partial(image_kernel, scale),
        grid=(chans // group, spread),
        in_specs=[
            pl.BlockSpec(
                (z, RADIX, 1, 2, group * rows_dev, LANES), lambda c, g: (0, g, slot, 0, c, 0)
            ),
            pl.BlockSpec(table.shape, lambda c, g: (0, 0)),
            pl.BlockSpec(order.shape, lambda c, g: (0, 0)),
        ]
        + [pl.BlockSpec(memory_space=pl.ANY)] * len(held),
        out_specs=pl.BlockSpec(
            (2, group, total, wide), lambda c, g: (0, c, 0, chunk * spread + g)
        ),
        out_shape=jax.ShapeDtypeStruct((2, chans, total, count * spread * wide), jnp.bfloat16),
        input_output_aliases={3: 0} if held else {},
        compiler_params=params(),
        cost_estimate=pl.CostEstimate(
            flops=4 * pieces * chans * total * LANES * wide,
            bytes_accessed=8 * pieces * chans * total * LANES,
            transcendentals=0,
        ),
        name="image",
    )(x, jnp.asarray(table), jnp.asarray(order), *held)


def turn_kernel(basis_ref, out_ref):
    out_ref[...] = basis_ref[...].T


def turn(basis):
    vmem = pl.BlockSpec(memory_space=pltpu.VMEM)
    return pl.pallas_call(
        turn_kernel,
        in_specs=[vmem],
        out_specs=vmem,
        out_shape=jax.ShapeDtypeStruct(basis.shape[::-1], basis.dtype),
        compiler_params=params(),
        name="turn",
    )(basis)


def exchange(x, axes):
    return lax.all_to_all(x, axes, split_axis=0, concat_axis=0, tiled=True)


def scatter(pieces):
    count = len(pieces)
    return [pieces[0]] + [
        lax.ppermute(
            pieces[step], "chan", [(j, int(partner(np.int32(j), step, count))) for j in range(count)]
        )
        for step in range(1, count)
    ]


def shards(visibility, eigen_basis, eigenvalues, noise_power):
    uv_count = lax.axis_size("uv")
    chan_count = lax.axis_size("chan")
    _, chans, rows_dev, length = visibility.shape
    count = length // chan_count // LANES
    targets = uv_count * chan_count
    at = lax.axis_index("chan").astype(jnp.int32).reshape(1)
    basis = exchange(jnp.broadcast_to(eigen_basis, (chan_count,) + eigen_basis.shape), "chan")
    basis = basis.reshape(chan_count * chans, -1)
    basis_t = turn(basis)
    gain = eigenvalues[:, None] / (eigenvalues[:, None] + noise_power[None, :])
    flat = visibility.reshape(2, chans * rows_dev, length)
    first = column_transform(flat, at, chan_count, [0], False)
    cells = [[exchange(first[0], "chan")]]
    if count > 1:
        sends = column_transform(flat, at, chan_count, list(range(1, count)), True)
        cells += [
            scatter(sends[k * chan_count : (k + 1) * chan_count]) for k in range(count - 1)
        ]
    groups = [[0]] + [g for g in (list(range(1, count - 1)), [count - 1]) if g and count > 1]
    held, cleaned = [], cells[1][:1] if count > 1 else []
    for chunks in groups:
        for slot, k in enumerate(chunks):
            cleaned = [
                clean(
                    at, cells[k], basis, basis_t, gain, targets, rows_dev, slot, len(chunks), cleaned
                )
            ]
        planes = exchange(cleaned[0], ("uv", "chan"))
        planes = planes.reshape((uv_count, chan_count) + planes.shape[1:])
        for slot, k in enumerate(chunks):
            held = [image(planes, slot, k, count, rows_dev, held)]
    return held[0]


def solution(mesh):
    in_specs = (P(None, "chan", "uv", None), P("chan", None), P(), P("uv"))
    out_specs = P(None, ("uv", "chan"), None, None)
    return jax.shard_map(shards, mesh=mesh, in_specs=in_specs, out_specs=out_specs, check_vma=False)
```

```python
import functools
import math

import jax
import jax.numpy as jnp
import numpy as np
from jax import lax
from jax.experimental import pallas as pl
from jax.experimental.pallas import tpu as pltpu
from jax.sharding import PartitionSpec as P

LANES = 128
RADIX = 8
ROWS = 16
VMEM_BYTES = 56 * 1024 * 1024


def params():
    return pltpu.CompilerParams(vmem_limit_bytes=VMEM_BYTES)


def inner_table(size):
    position = np.arange(size)
    phase = 2.0 * np.pi * (np.outer(position, position) % size) / size
    cosine, sine = np.cos(phase), np.sin(phase)
    return np.block([[cosine, sine], [-sine, cosine]]).astype(jnp.bfloat16)


def twiddle_table(length):
    inner = length // RADIX
    phase = 2.0 * np.pi * np.outer(np.arange(RADIX), np.arange(inner)) / length
    table = np.stack([np.cos(phase), np.sin(phase)], axis=1)
    return np.repeat(table[:, :, None], ROWS, axis=2).astype(jnp.bfloat16)


def order_table():
    table = np.zeros((RADIX, LANES, LANES, RADIX), np.float32)
    for y_lo in range(RADIX):
        for y_hi in range(LANES):
            table[y_lo, y_hi, y_hi, y_lo] = 1.0
    return table.reshape(RADIX * LANES, RADIX * LANES).astype(jnp.bfloat16)


def swap_table(major, minor):
    table = np.zeros((major * minor, major * minor), np.float32)
    for a in range(major):
        for b in range(minor):
            table[b * major + a, a * minor + b] = 1.0
    return table.astype(jnp.bfloat16)


def row_table(rows_dev, uv_count, group):
    total = rows_dev * uv_count
    position = np.arange(total)
    phase = 2.0 * np.pi * (np.outer(position, position) % total) / total
    cosine, sine = np.cos(phase), np.sin(phase)
    parts = np.array([[cosine, -sine], [sine, cosine]])
    parts = parts.reshape(2, 2, total, uv_count, rows_dev)
    size = 2 * group * total
    table = np.einsum("tsxzu,cd->tcxzsdu", parts, np.eye(group))
    return table.reshape(size, size).astype(jnp.bfloat16)


def butterfly8(re, im):
    def dft2(ar, ai, br, bi):
        return ar + br, ai + bi, ar - br, ai - bi

    def dft4(r, i):
        s0r, s0i, d0r, d0i = dft2(r[0], i[0], r[2], i[2])
        s1r, s1i, d1r, d1i = dft2(r[1], i[1], r[3], i[3])
        return (
            [s0r + s1r, d0r - d1i, s0r - s1r, d0r + d1i],
            [s0i + s1i, d0i + d1r, s0i - s1i, d0i - d1r],
        )

    er, ei = dft4(re[0::2], im[0::2])
    orr, oi = dft4(re[1::2], im[1::2])
    half = math.sqrt(0.5)
    turned_r = [orr[0], (orr[1] - oi[1]) * half, -oi[2], (-orr[3] - oi[3]) * half]
    turned_i = [oi[0], (orr[1] + oi[1]) * half, orr[2], (orr[3] - oi[3]) * half]
    out_r = [er[k] + turned_r[k] for k in range(4)] + [er[k] - turned_r[k] for k in range(4)]
    out_i = [ei[k] + turned_i[k] for k in range(4)] + [ei[k] - turned_i[k] for k in range(4)]
    return out_r, out_i


def column_kernel(chunks, spread, split, at_ref, x_ref, twiddle_ref, table_ref, *refs):
    if split:
        *out_refs, mid, stage = refs
    else:
        *out_refs, mid = refs
    rows, length = x_ref.shape[1:]
    inner = length // RADIX
    for block in range(inner // LANES):
        lanes = slice(block * LANES, (block + 1) * LANES)
        other = slice(inner + block * LANES, inner + (block + 1) * LANES)
        for i in range(rows // ROWS):
            at = slice(i * ROWS, (i + 1) * ROWS)
            re, im = [], []
            for a in range(RADIX):
                wide = slice(a * inner + block * LANES, a * inner + (block + 1) * LANES)
                re.append(x_ref[0, at, wide])
                im.append(x_ref[1, at, wide])
            re, im = butterfly8(re, im)
            mid[0, at, lanes] = re[0]
            mid[0, at, other] = im[0]
            for y_lo in range(1, RADIX):
                cosine = twiddle_ref[y_lo, 0, :, lanes]
                sine = twiddle_ref[y_lo, 1, :, lanes]
                mid[y_lo, at, lanes] = re[y_lo] * cosine - im[y_lo] * sine
                mid[y_lo, at, other] = re[y_lo] * sine + im[y_lo] * cosine
    for n, chunk in enumerate(chunks):
        for group in range(spread):
            column = (chunk * spread + group) * LANES
            table = jnp.concatenate(
                [table_ref[:, at : at + LANES] for at in (column, inner + column)], axis=1
            )
            wide = jnp.dot(
                mid[...].reshape(RADIX * rows, 2 * inner), table, preferred_element_type=jnp.float32
            ).astype(jnp.bfloat16)
            for y_lo in range(RADIX):
                for part in range(2):
                    value = wide[y_lo * rows : (y_lo + 1) * rows, part * LANES : (part + 1) * LANES]
                    if split:
                        stage[group * RADIX + y_lo, part] = value
                    else:
                        out_refs[n][group * RADIX + y_lo, part] = value
        if split:
            pieces = spread * RADIX
            for step in range(pieces):
                out_refs[n * pieces + step][...] = stage[partner(at_ref[0], step, pieces)]


def partner(at, step, count):
    if count & (count - 1):
        return (count - at + step) % count
    if step:
        step = sorted(range(1, count), key=lambda n: (-bin(n // 2).count("1"), -n))[step - 1]
    return at ^ step


def column_transform(x, at, pieces, chunks, split):
    _, rows, length = x.shape
    inner = length // RADIX
    block = math.gcd(rows, 64)
    if split:
        spec = pl.BlockSpec((2, block, LANES), lambda i, at: (0, i, 0))
        shape = jax.ShapeDtypeStruct((2, rows, LANES), jnp.bfloat16)
        stage = [pltpu.VMEM((pieces, 2, block, LANES), jnp.bfloat16)]
        outs = len(chunks) * pieces
    else:
        spec = pl.BlockSpec((pieces, 2, block, LANES), lambda i, at: (0, 0, i, 0))
        shape = jax.ShapeDtypeStruct((pieces, 2, rows, LANES), jnp.bfloat16)
        stage = []
        outs = len(chunks)
    return pl.pallas_call(
        functools.partial(column_kernel, chunks, pieces // RADIX, split),
        grid_spec=pltpu.PrefetchScalarGridSpec(
            num_scalar_prefetch=1,
            grid=(rows // block,),
            in_specs=[
                pl.BlockSpec((2, block, length), lambda i, at: (0, i, 0)),
                pl.BlockSpec((RADIX, 2, ROWS, inner), lambda i, at: (0, 0, 0, 0)),
                pl.BlockSpec((2 * inner, 2 * inner), lambda i, at: (0, 0)),
            ],
            out_specs=[spec] * outs,
            scratch_shapes=[pltpu.VMEM((RADIX, block, 2 * inner), jnp.bfloat16)] + stage,
        ),
        out_shape=[shape] * outs,
        compiler_params=params(),
        cost_estimate=pl.CostEstimate(
            flops=4 * rows * length * LANES * pieces * len(chunks),
            bytes_accessed=8 * rows * length,
            transcendentals=0,
        ),
        name="column_transform",
    )(at, x, jnp.asarray(twiddle_table(length)), jnp.asarray(inner_table(inner)))


def clean_kernel(split, waits, at_ref, *refs):
    *refs, out_ref, slab = refs
    *x_refs, basis_ref, basis_t_ref, gain_ref, swap_ref, back_ref = refs[: len(refs) - waits]
    chans = slab.shape[0]
    pair = 2 * LANES
    rows_dev = slab.shape[1] // pair
    tall = swap_ref.shape[0]
    group = tall // rows_dev
    sources = len(x_refs) if split else x_refs[0].shape[0]
    own = chans // sources
    for source in range(sources):
        block = x_refs[source] if split else x_refs[0].at[source]
        begin = partner(at_ref[0], source, sources) * own if split else source * own
        for k in range(own // group):
            rows = slice(k * tall, (k + 1) * tall)
            turned = jnp.dot(
                swap_ref[...],
                jnp.concatenate([block[0, rows, :], block[1, rows, :]], axis=1),
                preferred_element_type=jnp.float32,
            ).astype(jnp.bfloat16)
            channels = pl.ds(pl.multiple_of(begin + k * group, group), group)
            for u in range(rows_dev):
                slab[channels, u * pair : (u + 1) * pair] = turned[u * group : (u + 1) * group]
    for u in range(rows_dev):
        lanes = slice(u * pair, (u + 1) * pair)
        line = slab[:, lanes]
        amps = jnp.dot(basis_t_ref[...], line, preferred_element_type=jnp.float32)
        amps = amps.astype(jnp.bfloat16).astype(jnp.float32)
        front = (gain_ref[:, u : u + 1] * amps).astype(jnp.bfloat16)
        drop = jnp.dot(basis_ref[...], front, preferred_element_type=jnp.float32)
        slab[:, lanes] = (line.astype(jnp.float32) - drop).astype(jnp.bfloat16)
    out_rows = out_ref.shape[2]
    tall = back_ref.shape[0]
    group = tall // rows_dev
    for b in range(chans // group):
        channels = slice(b * group, (b + 1) * group)
        tile = jnp.concatenate(
            [slab[channels, u * pair : (u + 1) * pair] for u in range(rows_dev)], axis=0
        )
        value = jnp.dot(back_ref[...], tile, preferred_element_type=jnp.float32)
        for part in range(2):
            half = value[:, part * LANES : (part + 1) * LANES]
            if out_rows % tall == 0:
                target, row = divmod(b * tall, out_rows)
                out_ref[target, part, row : row + tall, :] = half.astype(jnp.bfloat16)
            else:
                take = tall // out_rows
                out_ref[b * take : (b + 1) * take, part] = half.reshape(
                    take, out_rows, LANES
                ).astype(jnp.bfloat16)


def clean(at, xs, basis, basis_t, gain, targets, rows_dev, before):
    split = len(xs) > 1
    chans = basis.shape[0]
    sources = len(xs) if split else xs[0].shape[0]
    own = chans // sources
    swap = swap_table(min(256 // rows_dev, own), rows_dev)
    back = np.ascontiguousarray(swap_table(256 // rows_dev, rows_dev).T)
    vmem = pl.BlockSpec(memory_space=pltpu.VMEM)
    return pl.pallas_call(
        functools.partial(clean_kernel, split, len(before)),
        in_specs=[pl.BlockSpec(memory_space=pltpu.SMEM)]
        + [vmem] * (len(xs) + 5)
        + [pl.BlockSpec(memory_space=pl.ANY)] * len(before),
        out_specs=vmem,
        out_shape=jax.ShapeDtypeStruct(
            (targets, 2, chans * rows_dev // targets, LANES), jnp.bfloat16
        ),
        scratch_shapes=[pltpu.VMEM((chans, rows_dev * 2 * LANES), jnp.bfloat16)],
        compiler_params=params(),
        cost_estimate=pl.CostEstimate(
            flops=12 * chans * chans * rows_dev * LANES,
            bytes_accessed=8 * chans * rows_dev * LANES,
            transcendentals=0,
        ),
        name="clean",
    )(at, *xs, basis, basis_t, gain, jnp.asarray(swap), jnp.asarray(back), *before)


def image_kernel(scale, x_ref, table_ref, order_ref, *refs):
    out_ref = refs[-1]
    z, _, parts, rows, _ = x_ref.shape
    tiles = []
    for y_lo in range(RADIX):
        tile = x_ref[:, y_lo]
        if rows % 16:
            tile = tile.astype(jnp.float32)
        tile = tile.reshape(z * parts * rows, LANES).astype(jnp.bfloat16)
        tiles.append(tile)
    value = jnp.dot(table_ref[...], jnp.concatenate(tiles, axis=1), preferred_element_type=jnp.float32)
    value = (value * scale).astype(jnp.bfloat16)
    value = jnp.dot(value, order_ref[...], preferred_element_type=jnp.float32)
    out_ref[...] = value.astype(jnp.bfloat16).reshape(out_ref.shape)


def image(x, chunk, count, rows_dev, held):
    z, pieces, _, rows, _ = x.shape
    chans = rows // rows_dev
    total = z * rows_dev
    spread = pieces // RADIX
    wide = RADIX * LANES
    group = min(chans, max(1, 256 // (2 * total)))
    table = row_table(rows_dev, z, group)
    order = order_table()
    scale = 1.0 / math.sqrt(total * count * spread * wide)
    return pl.pallas_call(
        functools.partial(image_kernel, scale),
        grid=(chans // group, spread),
        in_specs=[
            pl.BlockSpec((z, RADIX, 2, group * rows_dev, LANES), lambda c, g: (0, g, 0, c, 0)),
            pl.BlockSpec(table.shape, lambda c, g: (0, 0)),
            pl.BlockSpec(order.shape, lambda c, g: (0, 0)),
        ]
        + [pl.BlockSpec(memory_space=pl.ANY)] * len(held),
        out_specs=pl.BlockSpec(
            (2, group, total, wide), lambda c, g: (0, c, 0, chunk * spread + g)
        ),
        out_shape=jax.ShapeDtypeStruct((2, chans, total, count * spread * wide), jnp.bfloat16),
        input_output_aliases={3: 0} if held else {},
        compiler_params=params(),
        cost_estimate=pl.CostEstimate(
            flops=4 * pieces * chans * total * LANES * wide,
            bytes_accessed=8 * pieces * chans * total * LANES,
            transcendentals=0,
        ),
        name="image",
    )(x, jnp.asarray(table), jnp.asarray(order), *held)


def turn_kernel(basis_ref, out_ref):
    out_ref[...] = basis_ref[...].T


def turn(basis):
    vmem = pl.BlockSpec(memory_space=pltpu.VMEM)
    return pl.pallas_call(
        turn_kernel,
        in_specs=[vmem],
        out_specs=vmem,
        out_shape=jax.ShapeDtypeStruct(basis.shape[::-1], basis.dtype),
        compiler_params=params(),
        name="turn",
    )(basis)


def exchange(x, axes):
    return lax.all_to_all(x, axes, split_axis=0, concat_axis=0, tiled=True)


def scatter(pieces):
    count = len(pieces)
    return [pieces[0]] + [
        lax.ppermute(
            pieces[step], "chan", [(j, int(partner(np.int32(j), step, count))) for j in range(count)]
        )
        for step in range(1, count)
    ]


def shards(visibility, eigen_basis, eigenvalues, noise_power):
    uv_count = lax.axis_size("uv")
    chan_count = lax.axis_size("chan")
    _, chans, rows_dev, length = visibility.shape
    count = length // chan_count // LANES
    targets = uv_count * chan_count
    at = lax.axis_index("chan").astype(jnp.int32).reshape(1)
    basis = exchange(jnp.broadcast_to(eigen_basis, (chan_count,) + eigen_basis.shape), "chan")
    basis = basis.reshape(chan_count * chans, -1)
    basis_t = turn(basis)
    gain = eigenvalues[:, None] / (eigenvalues[:, None] + noise_power[None, :])
    flat = visibility.reshape(2, chans * rows_dev, length)
    first = column_transform(flat, at, chan_count, [0], False)
    cells = [[exchange(first[0], "chan")]]
    if count > 1:
        sends = column_transform(flat, at, chan_count, list(range(1, count)), True)
        cells += [
            scatter(sends[k * chan_count : (k + 1) * chan_count]) for k in range(count - 1)
        ]
    held, before = [], cells[1][:1] if count > 1 else []
    for k in range(count):
        cleaned = clean(at, cells[k], basis, basis_t, gain, targets, rows_dev, before)
        before = [cleaned]
        planes = exchange(cleaned, ("uv", "chan"))
        planes = planes.reshape((uv_count, chan_count) + planes.shape[1:])
        held = [image(planes, k, count, rows_dev, held)]
    return held[0]


def solution(mesh):
    in_specs = (P(None, "chan", "uv", None), P("chan", None), P(), P("uv"))
    out_specs = P(None, ("uv", "chan"), None, None)
    return jax.shard_map(shards, mesh=mesh, in_specs=in_specs, out_specs=out_specs, check_vma=False)
```

```python
import functools
import math

import jax
import jax.numpy as jnp
import numpy as np
from jax import lax
from jax.experimental import pallas as pl
from jax.experimental.pallas import tpu as pltpu
from jax.sharding import PartitionSpec as P

LANES = 128
RADIX = 8
EARLY = 6
VMEM_BYTES = 56 * 1024 * 1024


def params():
    return pltpu.CompilerParams(vmem_limit_bytes=VMEM_BYTES)


def inner_table(size):
    position = np.arange(size)
    phase = 2.0 * np.pi * (np.outer(position, position) % size) / size
    cosine, sine = np.cos(phase), np.sin(phase)
    return np.block([[cosine, sine], [-sine, cosine]]).astype(jnp.bfloat16)


def twiddle_table(length):
    inner = length // RADIX
    phase = 2.0 * np.pi * np.outer(np.arange(RADIX), np.arange(inner)) / length
    return np.stack([np.cos(phase), np.sin(phase)], axis=1).astype(np.float32)


def order_table():
    table = np.zeros((RADIX, LANES, LANES, RADIX), np.float32)
    for y_lo in range(RADIX):
        for y_hi in range(LANES):
            table[y_lo, y_hi, y_hi, y_lo] = 1.0
    return table.reshape(RADIX * LANES, RADIX * LANES).astype(jnp.bfloat16)


def swap_table(major, minor):
    table = np.zeros((major * minor, major * minor), np.float32)
    for a in range(major):
        for b in range(minor):
            table[b * major + a, a * minor + b] = 1.0
    return table.astype(jnp.bfloat16)


def row_table(rows_dev, uv_count, group):
    total = rows_dev * uv_count
    position = np.arange(total)
    phase = 2.0 * np.pi * (np.outer(position, position) % total) / total
    cosine, sine = np.cos(phase), np.sin(phase)
    parts = np.array([[cosine, -sine], [sine, cosine]])
    parts = parts.reshape(2, 2, total, uv_count, rows_dev)
    size = 2 * group * total
    table = np.einsum("tsxzu,cd->tcxzsdu", parts, np.eye(group))
    return table.reshape(size, size).astype(jnp.bfloat16)


def butterfly8(re, im):
    def dft2(ar, ai, br, bi):
        return ar + br, ai + bi, ar - br, ai - bi

    def dft4(r, i):
        s0r, s0i, d0r, d0i = dft2(r[0], i[0], r[2], i[2])
        s1r, s1i, d1r, d1i = dft2(r[1], i[1], r[3], i[3])
        return (
            [s0r + s1r, d0r - d1i, s0r - s1r, d0r + d1i],
            [s0i + s1i, d0i + d1r, s0i - s1i, d0i - d1r],
        )

    er, ei = dft4(re[0::2], im[0::2])
    orr, oi = dft4(re[1::2], im[1::2])
    half = math.sqrt(0.5)
    turned_r = [orr[0], (orr[1] - oi[1]) * half, -oi[2], (-orr[3] - oi[3]) * half]
    turned_i = [oi[0], (orr[1] + oi[1]) * half, orr[2], (orr[3] - oi[3]) * half]
    out_r = [er[k] + turned_r[k] for k in range(4)] + [er[k] - turned_r[k] for k in range(4)]
    out_i = [ei[k] + turned_i[k] for k in range(4)] + [ei[k] - turned_i[k] for k in range(4)]
    return out_r, out_i


def column_kernel(chunks, spread, split, at_ref, x_ref, twiddle_ref, table_ref, *refs):
    if split:
        *out_refs, mid, stage = refs
    else:
        *out_refs, mid = refs
    rows, length = x_ref.shape[1:]
    inner = length // RADIX
    step = 16
    for i in range(rows // step):
        at = slice(i * step, (i + 1) * step)
        for block in range(inner // LANES):
            re, im = [], []
            for a in range(RADIX):
                lanes = slice(a * inner + block * LANES, a * inner + (block + 1) * LANES)
                re.append(x_ref[0, at, lanes].astype(jnp.float32))
                im.append(x_ref[1, at, lanes].astype(jnp.float32))
            re, im = butterfly8(re, im)
            lanes = slice(block * LANES, (block + 1) * LANES)
            other = slice(inner + block * LANES, inner + (block + 1) * LANES)
            for y_lo in range(RADIX):
                if y_lo == 0:
                    tr, ti = re[0], im[0]
                else:
                    cosine = twiddle_ref[y_lo, 0:1, lanes]
                    sine = twiddle_ref[y_lo, 1:2, lanes]
                    tr = re[y_lo] * cosine - im[y_lo] * sine
                    ti = re[y_lo] * sine + im[y_lo] * cosine
                mid[y_lo, at, lanes] = tr.astype(jnp.bfloat16)
                mid[y_lo, at, other] = ti.astype(jnp.bfloat16)
    for n, chunk in enumerate(chunks):
        for group in range(spread):
            column = (chunk * spread + group) * LANES
            table = jnp.concatenate(
                [table_ref[:, at : at + LANES] for at in (column, inner + column)], axis=1
            )
            wide = jnp.dot(
                mid[...].reshape(RADIX * rows, 2 * inner), table, preferred_element_type=jnp.float32
            ).astype(jnp.bfloat16)
            for y_lo in range(RADIX):
                for part in range(2):
                    value = wide[y_lo * rows : (y_lo + 1) * rows, part * LANES : (part + 1) * LANES]
                    if split:
                        stage[group * RADIX + y_lo, part] = value
                    else:
                        out_refs[n][group * RADIX + y_lo, part] = value
        if split:
            pieces = spread * RADIX
            for step in range(pieces):
                out_refs[n * pieces + step][...] = stage[partner(at_ref[0], step, pieces)]


def partner(at, step, count):
    if count & (count - 1):
        return (count - at + step) % count
    if step:
        step = sorted(range(1, count), key=lambda n: (-bin(n // 2).count("1"), -n))[step - 1]
    return at ^ step


def column_transform(x, at, pieces, chunks, split):
    _, rows, length = x.shape
    inner = length // RADIX
    block = math.gcd(rows, 64)
    if split:
        spec = pl.BlockSpec((2, block, LANES), lambda i, at: (0, i, 0))
        shape = jax.ShapeDtypeStruct((2, rows, LANES), jnp.bfloat16)
        stage = [pltpu.VMEM((pieces, 2, block, LANES), jnp.bfloat16)]
        outs = len(chunks) * pieces
    else:
        spec = pl.BlockSpec((pieces, 2, block, LANES), lambda i, at: (0, 0, i, 0))
        shape = jax.ShapeDtypeStruct((pieces, 2, rows, LANES), jnp.bfloat16)
        stage = []
        outs = len(chunks)
    return pl.pallas_call(
        functools.partial(column_kernel, chunks, pieces // RADIX, split),
        grid_spec=pltpu.PrefetchScalarGridSpec(
            num_scalar_prefetch=1,
            grid=(rows // block,),
            in_specs=[
                pl.BlockSpec((2, block, length), lambda i, at: (0, i, 0)),
                pl.BlockSpec((RADIX, 2, inner), lambda i, at: (0, 0, 0)),
                pl.BlockSpec((2 * inner, 2 * inner), lambda i, at: (0, 0)),
            ],
            out_specs=[spec] * outs,
            scratch_shapes=[pltpu.VMEM((RADIX, block, 2 * inner), jnp.bfloat16)] + stage,
        ),
        out_shape=[shape] * outs,
        compiler_params=params(),
        cost_estimate=pl.CostEstimate(
            flops=4 * rows * length * LANES * pieces * len(chunks),
            bytes_accessed=8 * rows * length,
            transcendentals=0,
        ),
        name="column_transform",
    )(at, x, jnp.asarray(twiddle_table(length)), jnp.asarray(inner_table(inner)))


def clean_kernel(split, waits, at_ref, *refs):
    *refs, out_ref, slab = refs
    *x_refs, basis_ref, basis_t_ref, gain_ref, swap_ref, back_ref = refs[: len(refs) - waits]
    chans = slab.shape[0]
    pair = 2 * LANES
    rows_dev = slab.shape[1] // pair
    tall = swap_ref.shape[0]
    group = tall // rows_dev
    sources = len(x_refs) if split else x_refs[0].shape[0]
    own = chans // sources
    for source in range(sources):
        block = x_refs[source] if split else x_refs[0].at[source]
        begin = partner(at_ref[0], source, sources) * own if split else source * own
        for k in range(own // group):
            rows = slice(k * tall, (k + 1) * tall)
            turned = jnp.dot(
                swap_ref[...],
                jnp.concatenate([block[0, rows, :], block[1, rows, :]], axis=1),
                preferred_element_type=jnp.float32,
            ).astype(jnp.bfloat16)
            channels = pl.ds(pl.multiple_of(begin + k * group, group), group)
            for u in range(rows_dev):
                slab[channels, u * pair : (u + 1) * pair] = turned[u * group : (u + 1) * group]
    for u in range(rows_dev):
        lanes = slice(u * pair, (u + 1) * pair)
        line = slab[:, lanes]
        amps = jnp.dot(basis_t_ref[...], line, preferred_element_type=jnp.float32)
        amps = amps.astype(jnp.bfloat16).astype(jnp.float32)
        front = (gain_ref[:, u : u + 1] * amps).astype(jnp.bfloat16)
        drop = jnp.dot(basis_ref[...], front, preferred_element_type=jnp.float32)
        slab[:, lanes] = (line.astype(jnp.float32) - drop).astype(jnp.bfloat16)
    out_rows = out_ref.shape[3]
    tall = back_ref.shape[0]
    group = tall // rows_dev
    for b in range(chans // group):
        channels = slice(b * group, (b + 1) * group)
        tile = jnp.concatenate(
            [slab[channels, u * pair : (u + 1) * pair] for u in range(rows_dev)], axis=0
        )
        value = jnp.dot(back_ref[...], tile, preferred_element_type=jnp.float32)
        for part in range(2):
            half = value[:, part * LANES : (part + 1) * LANES]
            if out_rows % tall == 0:
                target, row = divmod(b * tall, out_rows)
                out_ref[target, 0, part, row : row + tall, :] = half.astype(jnp.bfloat16)
            else:
                take = tall // out_rows
                out_ref[b * take : (b + 1) * take, 0, part] = half.reshape(
                    take, out_rows, LANES
                ).astype(jnp.bfloat16)


def clean(at, xs, basis, basis_t, gain, targets, rows_dev, slot, slots, before):
    split = len(xs) > 1
    chans = basis.shape[0]
    sources = len(xs) if split else xs[0].shape[0]
    own = chans // sources
    swap = swap_table(min(256 // rows_dev, own), rows_dev)
    back = np.ascontiguousarray(swap_table(256 // rows_dev, rows_dev).T)
    vmem = pl.BlockSpec(memory_space=pltpu.VMEM)
    out_rows = chans * rows_dev // targets
    return pl.pallas_call(
        functools.partial(clean_kernel, split, len(before)),
        grid=(1,),
        in_specs=[pl.BlockSpec(memory_space=pltpu.SMEM)]
        + [vmem] * (len(xs) + 5)
        + [pl.BlockSpec(memory_space=pl.ANY)] * len(before),
        out_specs=pl.BlockSpec((targets, 1, 2, out_rows, LANES), lambda i: (0, slot, 0, 0, 0)),
        out_shape=jax.ShapeDtypeStruct((targets, slots, 2, out_rows, LANES), jnp.bfloat16),
        input_output_aliases={6 + len(xs): 0} if slot else {},
        scratch_shapes=[pltpu.VMEM((chans, rows_dev * 2 * LANES), jnp.bfloat16)],
        compiler_params=params(),
        cost_estimate=pl.CostEstimate(
            flops=12 * chans * chans * rows_dev * LANES,
            bytes_accessed=8 * chans * rows_dev * LANES,
            transcendentals=0,
        ),
        name="clean",
    )(at, *xs, basis, basis_t, gain, jnp.asarray(swap), jnp.asarray(back), *before)


def image_kernel(scale, x_ref, table_ref, order_ref, *refs):
    out_ref = refs[-1]
    z, _, _, parts, rows, _ = x_ref.shape
    tiles = []
    for y_lo in range(RADIX):
        tile = x_ref[:, y_lo, 0]
        if rows % 16:
            tile = tile.astype(jnp.float32)
        tile = tile.reshape(z * parts * rows, LANES).astype(jnp.bfloat16)
        tiles.append(tile)
    value = jnp.dot(table_ref[...], jnp.concatenate(tiles, axis=1), preferred_element_type=jnp.float32)
    value = (value * scale).astype(jnp.bfloat16)
    value = jnp.dot(value, order_ref[...], preferred_element_type=jnp.float32)
    out_ref[...] = value.astype(jnp.bfloat16).reshape(out_ref.shape)


def image(x, slot, chunk, count, rows_dev, held):
    z, pieces, _, _, rows, _ = x.shape
    chans = rows // rows_dev
    total = z * rows_dev
    spread = pieces // RADIX
    wide = RADIX * LANES
    group = min(chans, max(1, 256 // (2 * total)))
    table = row_table(rows_dev, z, group)
    order = order_table()
    scale = 1.0 / math.sqrt(total * count * spread * wide)
    return pl.pallas_call(
        functools.partial(image_kernel, scale),
        grid=(chans // group, spread),
        in_specs=[
            pl.BlockSpec(
                (z, RADIX, 1, 2, group * rows_dev, LANES), lambda c, g: (0, g, slot, 0, c, 0)
            ),
            pl.BlockSpec(table.shape, lambda c, g: (0, 0)),
            pl.BlockSpec(order.shape, lambda c, g: (0, 0)),
        ]
        + [pl.BlockSpec(memory_space=pl.ANY)] * len(held),
        out_specs=pl.BlockSpec(
            (2, group, total, wide), lambda c, g: (0, c, 0, chunk * spread + g)
        ),
        out_shape=jax.ShapeDtypeStruct((2, chans, total, count * spread * wide), jnp.bfloat16),
        input_output_aliases={3: 0} if held else {},
        compiler_params=params(),
        cost_estimate=pl.CostEstimate(
            flops=4 * pieces * chans * total * LANES * wide,
            bytes_accessed=8 * pieces * chans * total * LANES,
            transcendentals=0,
        ),
        name="image",
    )(x, jnp.asarray(table), jnp.asarray(order), *held)


def turn_kernel(basis_ref, out_ref):
    out_ref[...] = basis_ref[...].T


def turn(basis):
    vmem = pl.BlockSpec(memory_space=pltpu.VMEM)
    return pl.pallas_call(
        turn_kernel,
        in_specs=[vmem],
        out_specs=vmem,
        out_shape=jax.ShapeDtypeStruct(basis.shape[::-1], basis.dtype),
        compiler_params=params(),
        name="turn",
    )(basis)


def exchange(x, axes):
    return lax.all_to_all(x, axes, split_axis=0, concat_axis=0, tiled=True)


def scatter(pieces):
    count = len(pieces)
    return [pieces[0]] + [
        lax.ppermute(
            pieces[step], "chan", [(j, int(partner(np.int32(j), step, count))) for j in range(count)]
        )
        for step in range(1, count)
    ]


def shards(visibility, eigen_basis, eigenvalues, noise_power):
    uv_count = lax.axis_size("uv")
    chan_count = lax.axis_size("chan")
    _, chans, rows_dev, length = visibility.shape
    count = length // chan_count // LANES
    targets = uv_count * chan_count
    at = lax.axis_index("chan").astype(jnp.int32).reshape(1)
    basis = exchange(jnp.broadcast_to(eigen_basis, (chan_count,) + eigen_basis.shape), "chan")
    basis = basis.reshape(chan_count * chans, -1)
    basis_t = turn(basis)
    gain = eigenvalues[:, None] / (eigenvalues[:, None] + noise_power[None, :])
    flat = visibility.reshape(2, chans * rows_dev, length)
    first = column_transform(flat, at, chan_count, [0], False)
    cells = [[exchange(first[0], "chan")]]
    if count > 1:
        sends = column_transform(flat, at, chan_count, list(range(1, count)), True)
        cells += [
            scatter(sends[k * chan_count : (k + 1) * chan_count]) for k in range(count - 1)
        ]
    groups = [[0]] + [g for g in (list(range(1, count - 1)), [count - 1]) if g and count > 1]
    held, before = [], cells[1][1:EARLY] if count > 1 else []
    for chunks in groups:
        for slot, k in enumerate(chunks):
            cleaned = clean(
                at, cells[k], basis, basis_t, gain, targets, rows_dev, slot, len(chunks), before
            )
            before = [cleaned]
        planes = exchange(cleaned, ("uv", "chan"))
        planes = planes.reshape((uv_count, chan_count) + planes.shape[1:])
        for slot, k in enumerate(chunks):
            held = [image(planes, slot, k, count, rows_dev, held)]
    return held[0]


def solution(mesh):
    in_specs = (P(None, "chan", "uv", None), P("chan", None), P(), P("uv"))
    out_specs = P(None, ("uv", "chan"), None, None)
    return jax.shard_map(shards, mesh=mesh, in_specs=in_specs, out_specs=out_specs, check_vma=False)
```

```python
import functools
import math

import jax
import jax.numpy as jnp
import numpy as np
from jax import lax
from jax.experimental import pallas as pl
from jax.experimental.pallas import tpu as pltpu
from jax.sharding import PartitionSpec as P

LANES = 128
RADIX = 8
VMEM_BYTES = 56 * 1024 * 1024


def params():
    return pltpu.CompilerParams(vmem_limit_bytes=VMEM_BYTES)


def inner_table(size):
    position = np.arange(size)
    phase = 2.0 * np.pi * (np.outer(position, position) % size) / size
    cosine, sine = np.cos(phase), np.sin(phase)
    return np.block([[cosine, sine], [-sine, cosine]]).astype(jnp.bfloat16)


def twiddle_table(length):
    inner = length // RADIX
    phase = 2.0 * np.pi * np.outer(np.arange(RADIX), np.arange(inner)) / length
    return np.stack([np.cos(phase), np.sin(phase)], axis=1).astype(np.float32)


def order_table():
    table = np.zeros((RADIX, LANES, LANES, RADIX), np.float32)
    for y_lo in range(RADIX):
        for y_hi in range(LANES):
            table[y_lo, y_hi, y_hi, y_lo] = 1.0
    return table.reshape(RADIX * LANES, RADIX * LANES).astype(jnp.bfloat16)


def swap_table(major, minor):
    table = np.zeros((major * minor, major * minor), np.float32)
    for a in range(major):
        for b in range(minor):
            table[b * major + a, a * minor + b] = 1.0
    return table.astype(jnp.bfloat16)


def row_table(rows_dev, uv_count, group):
    total = rows_dev * uv_count
    position = np.arange(total)
    phase = 2.0 * np.pi * (np.outer(position, position) % total) / total
    cosine, sine = np.cos(phase), np.sin(phase)
    parts = np.array([[cosine, -sine], [sine, cosine]])
    parts = parts.reshape(2, 2, total, uv_count, rows_dev)
    size = 2 * group * total
    table = np.einsum("tsxzu,cd->tcxzsdu", parts, np.eye(group))
    return table.reshape(size, size).astype(jnp.bfloat16)


def butterfly8(re, im):
    def dft2(ar, ai, br, bi):
        return ar + br, ai + bi, ar - br, ai - bi

    def dft4(r, i):
        s0r, s0i, d0r, d0i = dft2(r[0], i[0], r[2], i[2])
        s1r, s1i, d1r, d1i = dft2(r[1], i[1], r[3], i[3])
        return (
            [s0r + s1r, d0r - d1i, s0r - s1r, d0r + d1i],
            [s0i + s1i, d0i + d1r, s0i - s1i, d0i - d1r],
        )

    er, ei = dft4(re[0::2], im[0::2])
    orr, oi = dft4(re[1::2], im[1::2])
    half = math.sqrt(0.5)
    turned_r = [orr[0], (orr[1] - oi[1]) * half, -oi[2], (-orr[3] - oi[3]) * half]
    turned_i = [oi[0], (orr[1] + oi[1]) * half, orr[2], (orr[3] - oi[3]) * half]
    out_r = [er[k] + turned_r[k] for k in range(4)] + [er[k] - turned_r[k] for k in range(4)]
    out_i = [ei[k] + turned_i[k] for k in range(4)] + [ei[k] - turned_i[k] for k in range(4)]
    return out_r, out_i


def column_kernel(chunks, spread, at_ref, x_ref, twiddle_ref, table_ref, *refs):
    *out_refs, mid, stage = refs
    pieces = spread * RADIX
    rows, length = x_ref.shape[1:]
    inner = length // RADIX
    step = 16
    for i in range(rows // step):
        at = slice(i * step, (i + 1) * step)
        for block in range(inner // LANES):
            re, im = [], []
            for a in range(RADIX):
                lanes = slice(a * inner + block * LANES, a * inner + (block + 1) * LANES)
                re.append(x_ref[0, at, lanes].astype(jnp.float32))
                im.append(x_ref[1, at, lanes].astype(jnp.float32))
            re, im = butterfly8(re, im)
            lanes = slice(block * LANES, (block + 1) * LANES)
            other = slice(inner + block * LANES, inner + (block + 1) * LANES)
            for y_lo in range(RADIX):
                if y_lo == 0:
                    tr, ti = re[0], im[0]
                else:
                    cosine = twiddle_ref[y_lo, 0:1, lanes]
                    sine = twiddle_ref[y_lo, 1:2, lanes]
                    tr = re[y_lo] * cosine - im[y_lo] * sine
                    ti = re[y_lo] * sine + im[y_lo] * cosine
                mid[y_lo, at, lanes] = tr.astype(jnp.bfloat16)
                mid[y_lo, at, other] = ti.astype(jnp.bfloat16)
    for chunk, split in chunks:
        outs = out_refs[: pieces if split else 1]
        out_refs = out_refs[len(outs) :]
        for group in range(spread):
            column = (chunk * spread + group) * LANES
            table = jnp.concatenate(
                [table_ref[:, at : at + LANES] for at in (column, inner + column)], axis=1
            )
            wide = jnp.dot(
                mid[...].reshape(RADIX * rows, 2 * inner), table, preferred_element_type=jnp.float32
            ).astype(jnp.bfloat16)
            for y_lo in range(RADIX):
                for part in range(2):
                    value = wide[y_lo * rows : (y_lo + 1) * rows, part * LANES : (part + 1) * LANES]
                    if split:
                        stage[group * RADIX + y_lo, part] = value
                    else:
                        outs[0][group * RADIX + y_lo, part] = value
        if split:
            for step, out_ref in enumerate(outs):
                out_ref[...] = stage[partner(at_ref[0], step, pieces)]


def partner(at, step, count):
    if count & (count - 1):
        return (count - at + step) % count
    if step:
        step = sorted(range(1, count), key=lambda n: (-bin(n // 2).count("1"), -n))[step - 1]
    return at ^ step


def column_transform(x, at, pieces, chunks):
    _, rows, length = x.shape
    inner = length // RADIX
    block = math.gcd(rows, 128)
    specs, shapes = [], []
    for _, split in chunks:
        if split:
            specs += [pl.BlockSpec((2, block, LANES), lambda i, at: (0, i, 0))] * pieces
            shapes += [jax.ShapeDtypeStruct((2, rows, LANES), jnp.bfloat16)] * pieces
        else:
            specs.append(pl.BlockSpec((pieces, 2, block, LANES), lambda i, at: (0, 0, i, 0)))
            shapes.append(jax.ShapeDtypeStruct((pieces, 2, rows, LANES), jnp.bfloat16))
    return pl.pallas_call(
        functools.partial(column_kernel, chunks, pieces // RADIX),
        grid_spec=pltpu.PrefetchScalarGridSpec(
            num_scalar_prefetch=1,
            grid=(rows // block,),
            in_specs=[
                pl.BlockSpec((2, block, length), lambda i, at: (0, i, 0)),
                pl.BlockSpec((RADIX, 2, inner), lambda i, at: (0, 0, 0)),
                pl.BlockSpec((2 * inner, 2 * inner), lambda i, at: (0, 0)),
            ],
            out_specs=specs,
            scratch_shapes=[
                pltpu.VMEM((RADIX, block, 2 * inner), jnp.bfloat16),
                pltpu.VMEM((pieces, 2, block, LANES), jnp.bfloat16),
            ],
        ),
        out_shape=shapes,
        compiler_params=params(),
        cost_estimate=pl.CostEstimate(
            flops=4 * rows * length * LANES * pieces * len(chunks),
            bytes_accessed=8 * rows * length,
            transcendentals=0,
        ),
        name="column_transform",
    )(at, x, jnp.asarray(twiddle_table(length)), jnp.asarray(inner_table(inner)))


def clean_kernel(split, waits, at_ref, *refs):
    *refs, out_ref, slab = refs
    *x_refs, basis_ref, basis_t_ref, gain_ref, swap_ref, back_ref = refs[: len(refs) - waits]
    chans = slab.shape[0]
    pair = 2 * LANES
    rows_dev = slab.shape[1] // pair
    tall = swap_ref.shape[0]
    group = tall // rows_dev
    sources = len(x_refs) if split else x_refs[0].shape[0]
    own = chans // sources
    for source in range(sources):
        block = x_refs[source] if split else x_refs[0].at[source]
        begin = partner(at_ref[0], source, sources) * own if split else source * own
        for k in range(own // group):
            rows = slice(k * tall, (k + 1) * tall)
            turned = jnp.dot(
                swap_ref[...],
                jnp.concatenate([block[0, rows, :], block[1, rows, :]], axis=1),
                preferred_element_type=jnp.float32,
            ).astype(jnp.bfloat16)
            channels = pl.ds(pl.multiple_of(begin + k * group, group), group)
            for u in range(rows_dev):
                slab[channels, u * pair : (u + 1) * pair] = turned[u * group : (u + 1) * group]
    for u in range(rows_dev):
        lanes = slice(u * pair, (u + 1) * pair)
        line = slab[:, lanes]
        amps = jnp.dot(basis_t_ref[...], line, preferred_element_type=jnp.float32)
        amps = amps.astype(jnp.bfloat16).astype(jnp.float32)
        front = (gain_ref[:, u : u + 1] * amps).astype(jnp.bfloat16)
        drop = jnp.dot(basis_ref[...], front, preferred_element_type=jnp.float32)
        slab[:, lanes] = (line.astype(jnp.float32) - drop).astype(jnp.bfloat16)
    out_rows = out_ref.shape[3]
    tall = back_ref.shape[0]
    group = tall // rows_dev
    for b in range(chans // group):
        channels = slice(b * group, (b + 1) * group)
        tile = jnp.concatenate(
            [slab[channels, u * pair : (u + 1) * pair] for u in range(rows_dev)], axis=0
        )
        value = jnp.dot(back_ref[...], tile, preferred_element_type=jnp.float32)
        for part in range(2):
            half = value[:, part * LANES : (part + 1) * LANES]
            if out_rows % tall == 0:
                target, row = divmod(b * tall, out_rows)
                out_ref[target, 0, part, row : row + tall, :] = half.astype(jnp.bfloat16)
            else:
                take = tall // out_rows
                out_ref[b * take : (b + 1) * take, 0, part] = half.reshape(
                    take, out_rows, LANES
                ).astype(jnp.bfloat16)


def clean(at, xs, basis, basis_t, gain, targets, rows_dev, slot, slots, before):
    split = len(xs) > 1
    chans = basis.shape[0]
    sources = len(xs) if split else xs[0].shape[0]
    own = chans // sources
    swap = swap_table(min(256 // rows_dev, own), rows_dev)
    back = np.ascontiguousarray(swap_table(256 // rows_dev, rows_dev).T)
    vmem = pl.BlockSpec(memory_space=pltpu.VMEM)
    out_rows = chans * rows_dev // targets
    return pl.pallas_call(
        functools.partial(clean_kernel, split, len(before)),
        grid=(1,),
        in_specs=[pl.BlockSpec(memory_space=pltpu.SMEM)]
        + [vmem] * (len(xs) + 5)
        + [pl.BlockSpec(memory_space=pl.ANY)] * len(before),
        out_specs=pl.BlockSpec((targets, 1, 2, out_rows, LANES), lambda i: (0, slot, 0, 0, 0)),
        out_shape=jax.ShapeDtypeStruct((targets, slots, 2, out_rows, LANES), jnp.bfloat16),
        input_output_aliases={6 + len(xs): 0} if slot else {},
        scratch_shapes=[pltpu.VMEM((chans, rows_dev * 2 * LANES), jnp.bfloat16)],
        compiler_params=params(),
        cost_estimate=pl.CostEstimate(
            flops=12 * chans * chans * rows_dev * LANES,
            bytes_accessed=8 * chans * rows_dev * LANES,
            transcendentals=0,
        ),
        name="clean",
    )(at, *xs, basis, basis_t, gain, jnp.asarray(swap), jnp.asarray(back), *before)


def image_kernel(scale, x_ref, table_ref, order_ref, *refs):
    out_ref = refs[-1]
    z, _, _, parts, rows, _ = x_ref.shape
    tiles = []
    for y_lo in range(RADIX):
        tile = x_ref[:, y_lo, 0]
        if rows % 16:
            tile = tile.astype(jnp.float32)
        tile = tile.reshape(z * parts * rows, LANES).astype(jnp.bfloat16)
        tiles.append(tile)
    value = jnp.dot(table_ref[...], jnp.concatenate(tiles, axis=1), preferred_element_type=jnp.float32)
    value = (value * scale).astype(jnp.bfloat16)
    value = jnp.dot(value, order_ref[...], preferred_element_type=jnp.float32)
    out_ref[...] = value.astype(jnp.bfloat16).reshape(out_ref.shape)


def image(x, slot, chunk, count, rows_dev, held):
    z, pieces, _, _, rows, _ = x.shape
    chans = rows // rows_dev
    total = z * rows_dev
    spread = pieces // RADIX
    wide = RADIX * LANES
    group = min(chans, max(1, 256 // (2 * total)))
    table = row_table(rows_dev, z, group)
    order = order_table()
    scale = 1.0 / math.sqrt(total * count * spread * wide)
    return pl.pallas_call(
        functools.partial(image_kernel, scale),
        grid=(chans // group, spread),
        in_specs=[
            pl.BlockSpec(
                (z, RADIX, 1, 2, group * rows_dev, LANES), lambda c, g: (0, g, slot, 0, c, 0)
            ),
            pl.BlockSpec(table.shape, lambda c, g: (0, 0)),
            pl.BlockSpec(order.shape, lambda c, g: (0, 0)),
        ]
        + [pl.BlockSpec(memory_space=pl.ANY)] * len(held),
        out_specs=pl.BlockSpec(
            (2, group, total, wide), lambda c, g: (0, c, 0, chunk * spread + g)
        ),
        out_shape=jax.ShapeDtypeStruct((2, chans, total, count * spread * wide), jnp.bfloat16),
        input_output_aliases={3: 0} if held else {},
        compiler_params=params(),
        cost_estimate=pl.CostEstimate(
            flops=4 * pieces * chans * total * LANES * wide,
            bytes_accessed=8 * pieces * chans * total * LANES,
            transcendentals=0,
        ),
        name="image",
    )(x, jnp.asarray(table), jnp.asarray(order), *held)


def turn_kernel(basis_ref, out_ref):
    out_ref[...] = basis_ref[...].T


def turn(basis):
    vmem = pl.BlockSpec(memory_space=pltpu.VMEM)
    return pl.pallas_call(
        turn_kernel,
        in_specs=[vmem],
        out_specs=vmem,
        out_shape=jax.ShapeDtypeStruct(basis.shape[::-1], basis.dtype),
        compiler_params=params(),
        name="turn",
    )(basis)


def exchange(x, axes):
    return lax.all_to_all(x, axes, split_axis=0, concat_axis=0, tiled=True)


def scatter(pieces):
    count = len(pieces)
    return [pieces[0]] + [
        lax.ppermute(
            pieces[step], "chan", [(j, int(partner(np.int32(j), step, count))) for j in range(count)]
        )
        for step in range(1, count)
    ]


def shards(visibility, eigen_basis, eigenvalues, noise_power):
    uv_count = lax.axis_size("uv")
    chan_count = lax.axis_size("chan")
    _, chans, rows_dev, length = visibility.shape
    count = length // chan_count // LANES
    targets = uv_count * chan_count
    at = lax.axis_index("chan").astype(jnp.int32).reshape(1)
    basis = exchange(jnp.broadcast_to(eigen_basis, (chan_count,) + eigen_basis.shape), "chan")
    basis = basis.reshape(chan_count * chans, -1)
    basis_t = turn(basis)
    gain = eigenvalues[:, None] / (eigenvalues[:, None] + noise_power[None, :])
    flat = visibility.reshape(2, chans * rows_dev, length)
    first = column_transform(flat, at, chan_count, [(0, False)])
    cells = [[exchange(first[0], "chan")]]
    if count > 1:
        second, *sends = column_transform(
            flat, at, chan_count, [(k, k > 1) for k in range(1, count)]
        )
        cells.append([exchange(second, "chan")])
        cells += [
            scatter(sends[k * chan_count : (k + 1) * chan_count]) for k in range(count - 2)
        ]
    groups = [[0]] + [g for g in (list(range(1, count - 1)), [count - 1]) if g and count > 1]
    held, before = [], [second] if count > 1 else []
    for chunks in groups:
        for slot, k in enumerate(chunks):
            cleaned = clean(
                at, cells[k], basis, basis_t, gain, targets, rows_dev, slot, len(chunks), before
            )
            before = [cleaned]
        planes = exchange(cleaned, ("uv", "chan"))
        planes = planes.reshape((uv_count, chan_count) + planes.shape[1:])
        for slot, k in enumerate(chunks):
            held = [image(planes, slot, k, count, rows_dev, held)]
    return held[0]


def solution(mesh):
    in_specs = (P(None, "chan", "uv", None), P("chan", None), P(), P("uv"))
    out_specs = P(None, ("uv", "chan"), None, None)
    return jax.shard_map(shards, mesh=mesh, in_specs=in_specs, out_specs=out_specs, check_vma=False)
```

```python
import functools
import math

import jax
import jax.numpy as jnp
import numpy as np
from jax import lax
from jax.experimental import pallas as pl
from jax.experimental.pallas import tpu as pltpu
from jax.sharding import PartitionSpec as P

LANES = 128
RADIX = 8
VMEM_BYTES = 56 * 1024 * 1024


def params():
    return pltpu.CompilerParams(vmem_limit_bytes=VMEM_BYTES)


def inner_table(size):
    position = np.arange(size)
    phase = 2.0 * np.pi * (np.outer(position, position) % size) / size
    cosine, sine = np.cos(phase), np.sin(phase)
    return np.block([[cosine, sine], [-sine, cosine]]).astype(jnp.bfloat16)


def twiddle_table(length):
    inner = length // RADIX
    phase = 2.0 * np.pi * np.outer(np.arange(RADIX), np.arange(inner)) / length
    return np.stack([np.cos(phase), np.sin(phase)], axis=1).astype(np.float32)


def order_table():
    table = np.zeros((RADIX, LANES, LANES, RADIX), np.float32)
    for y_lo in range(RADIX):
        for y_hi in range(LANES):
            table[y_lo, y_hi, y_hi, y_lo] = 1.0
    return table.reshape(RADIX * LANES, RADIX * LANES).astype(jnp.bfloat16)


def swap_table(major, minor):
    table = np.zeros((major * minor, major * minor), np.float32)
    for a in range(major):
        for b in range(minor):
            table[b * major + a, a * minor + b] = 1.0
    return table.astype(jnp.bfloat16)


def row_table(rows_dev, uv_count, group):
    total = rows_dev * uv_count
    position = np.arange(total)
    phase = 2.0 * np.pi * (np.outer(position, position) % total) / total
    cosine, sine = np.cos(phase), np.sin(phase)
    parts = np.array([[cosine, -sine], [sine, cosine]])
    parts = parts.reshape(2, 2, total, uv_count, rows_dev)
    size = 2 * group * total
    table = np.einsum("tsxzu,cd->tcxzsdu", parts, np.eye(group))
    return table.reshape(size, size).astype(jnp.bfloat16)


def row_tables(rows_dev, uv_count, group):
    total = rows_dev * uv_count
    position = np.arange(total)
    phase = 2.0 * np.pi * (np.outer(position, position) % total) / total
    cosine, sine = np.cos(phase), np.sin(phase)
    parts = np.array([[cosine, -sine], [sine, cosine]])
    parts = parts.reshape(2, 2, total, uv_count, rows_dev)
    eye = np.eye(group)
    size = 2 * group * total
    tables = []
    for at in range(uv_count):
        order = (at - np.arange(uv_count)) % uv_count
        table = np.einsum("tsxzu,cd->tcxzsdu", parts[:, :, :, order], eye)
        tables.append(table.reshape(size, size).astype(jnp.bfloat16))
    return np.stack(tables)


def butterfly8(re, im):
    def dft2(ar, ai, br, bi):
        return ar + br, ai + bi, ar - br, ai - bi

    def dft4(r, i):
        s0r, s0i, d0r, d0i = dft2(r[0], i[0], r[2], i[2])
        s1r, s1i, d1r, d1i = dft2(r[1], i[1], r[3], i[3])
        return (
            [s0r + s1r, d0r - d1i, s0r - s1r, d0r + d1i],
            [s0i + s1i, d0i + d1r, s0i - s1i, d0i - d1r],
        )

    er, ei = dft4(re[0::2], im[0::2])
    orr, oi = dft4(re[1::2], im[1::2])
    half = math.sqrt(0.5)
    turned_r = [orr[0], (orr[1] - oi[1]) * half, -oi[2], (-orr[3] - oi[3]) * half]
    turned_i = [oi[0], (orr[1] + oi[1]) * half, orr[2], (orr[3] - oi[3]) * half]
    out_r = [er[k] + turned_r[k] for k in range(4)] + [er[k] - turned_r[k] for k in range(4)]
    out_i = [ei[k] + turned_i[k] for k in range(4)] + [ei[k] - turned_i[k] for k in range(4)]
    return out_r, out_i


def column_kernel(chunks, spread, at_ref, x_ref, twiddle_ref, table_ref, *refs):
    *out_refs, mid, stage = refs
    pieces = spread * RADIX
    rows, length = x_ref.shape[1:]
    inner = length // RADIX
    step = 16
    for i in range(rows // step):
        at = slice(i * step, (i + 1) * step)
        for block in range(inner // LANES):
            re, im = [], []
            for a in range(RADIX):
                lanes = slice(a * inner + block * LANES, a * inner + (block + 1) * LANES)
                re.append(x_ref[0, at, lanes].astype(jnp.float32))
                im.append(x_ref[1, at, lanes].astype(jnp.float32))
            re, im = butterfly8(re, im)
            lanes = slice(block * LANES, (block + 1) * LANES)
            other = slice(inner + block * LANES, inner + (block + 1) * LANES)
            for y_lo in range(RADIX):
                if y_lo == 0:
                    tr, ti = re[0], im[0]
                else:
                    cosine = twiddle_ref[y_lo, 0:1, lanes]
                    sine = twiddle_ref[y_lo, 1:2, lanes]
                    tr = re[y_lo] * cosine - im[y_lo] * sine
                    ti = re[y_lo] * sine + im[y_lo] * cosine
                mid[y_lo, at, lanes] = tr.astype(jnp.bfloat16)
                mid[y_lo, at, other] = ti.astype(jnp.bfloat16)
    for chunk, split in chunks:
        outs = out_refs[: pieces if split else 1]
        out_refs = out_refs[len(outs) :]
        for group in range(spread):
            column = (chunk * spread + group) * LANES
            table = jnp.concatenate(
                [table_ref[:, at : at + LANES] for at in (column, inner + column)], axis=1
            )
            wide = jnp.dot(
                mid[...].reshape(RADIX * rows, 2 * inner), table, preferred_element_type=jnp.float32
            ).astype(jnp.bfloat16)
            for y_lo in range(RADIX):
                for part in range(2):
                    value = wide[y_lo * rows : (y_lo + 1) * rows, part * LANES : (part + 1) * LANES]
                    if split:
                        stage[group * RADIX + y_lo, part] = value
                    else:
                        outs[0][group * RADIX + y_lo, part] = value
        if split:
            for step, out_ref in enumerate(outs):
                out_ref[...] = stage[partner(at_ref[0], step, pieces)]


def partner(at, step, count):
    if count & (count - 1):
        return (count - at + step) % count
    if step:
        step = sorted(range(1, count), key=lambda n: (-bin(n // 2).count("1"), -n))[step - 1]
    return at ^ step


def column_transform(x, at, pieces, chunks):
    _, rows, length = x.shape
    inner = length // RADIX
    block = math.gcd(rows, 128)
    specs, shapes = [], []
    for _, split in chunks:
        if split:
            specs += [pl.BlockSpec((2, block, LANES), lambda i, at: (0, i, 0))] * pieces
            shapes += [jax.ShapeDtypeStruct((2, rows, LANES), jnp.bfloat16)] * pieces
        else:
            specs.append(pl.BlockSpec((pieces, 2, block, LANES), lambda i, at: (0, 0, i, 0)))
            shapes.append(jax.ShapeDtypeStruct((pieces, 2, rows, LANES), jnp.bfloat16))
    return pl.pallas_call(
        functools.partial(column_kernel, chunks, pieces // RADIX),
        grid_spec=pltpu.PrefetchScalarGridSpec(
            num_scalar_prefetch=1,
            grid=(rows // block,),
            in_specs=[
                pl.BlockSpec((2, block, length), lambda i, at: (0, i, 0)),
                pl.BlockSpec((RADIX, 2, inner), lambda i, at: (0, 0, 0)),
                pl.BlockSpec((2 * inner, 2 * inner), lambda i, at: (0, 0)),
            ],
            out_specs=specs,
            scratch_shapes=[
                pltpu.VMEM((RADIX, block, 2 * inner), jnp.bfloat16),
                pltpu.VMEM((pieces, 2, block, LANES), jnp.bfloat16),
            ],
        ),
        out_shape=shapes,
        compiler_params=params(),
        cost_estimate=pl.CostEstimate(
            flops=4 * rows * length * LANES * pieces * len(chunks),
            bytes_accessed=8 * rows * length,
            transcendentals=0,
        ),
        name="column_transform",
    )(at, x, jnp.asarray(twiddle_table(length)), jnp.asarray(inner_table(inner)))


def clean_kernel(split, waits, steps, at_ref, *refs):
    refs, out_refs, slab = refs[: -1 - steps], refs[-1 - steps : -1], refs[-1]
    *x_refs, basis_ref, basis_t_ref, gain_ref, swap_ref, back_ref = refs[: len(refs) - waits]
    chans = slab.shape[0]
    pair = 2 * LANES
    rows_dev = slab.shape[1] // pair
    tall = swap_ref.shape[0]
    group = tall // rows_dev
    sources = len(x_refs) if split else x_refs[0].shape[0]
    own = chans // sources
    for source in range(sources):
        block = x_refs[source] if split else x_refs[0].at[source]
        begin = partner(at_ref[0], source, sources) * own if split else source * own
        for k in range(own // group):
            rows = slice(k * tall, (k + 1) * tall)
            turned = jnp.dot(
                swap_ref[...],
                jnp.concatenate([block[0, rows, :], block[1, rows, :]], axis=1),
                preferred_element_type=jnp.float32,
            ).astype(jnp.bfloat16)
            channels = pl.ds(pl.multiple_of(begin + k * group, group), group)
            for u in range(rows_dev):
                slab[channels, u * pair : (u + 1) * pair] = turned[u * group : (u + 1) * group]
    for u in range(rows_dev):
        lanes = slice(u * pair, (u + 1) * pair)
        line = slab[:, lanes]
        amps = jnp.dot(basis_t_ref[...], line, preferred_element_type=jnp.float32)
        amps = amps.astype(jnp.bfloat16).astype(jnp.float32)
        front = (gain_ref[:, u : u + 1] * amps).astype(jnp.bfloat16)
        drop = jnp.dot(basis_ref[...], front, preferred_element_type=jnp.float32)
        slab[:, lanes] = (line.astype(jnp.float32) - drop).astype(jnp.bfloat16)
    out_rows = out_refs[0].shape[3]
    tall = back_ref.shape[0]
    group = tall // rows_dev
    share = chans // steps
    for step, out_ref in enumerate(out_refs):
        start = lax.rem(at_ref[1] + step, steps) * share if steps > 1 else 0
        for b in range(share // group):
            channels = pl.ds(pl.multiple_of(start + b * group, group), group)
            tile = jnp.concatenate(
                [slab[channels, u * pair : (u + 1) * pair] for u in range(rows_dev)], axis=0
            )
            value = jnp.dot(back_ref[...], tile, preferred_element_type=jnp.float32)
            for part in range(2):
                half = value[:, part * LANES : (part + 1) * LANES]
                if out_rows % tall == 0:
                    target, row = divmod(b * tall, out_rows)
                    out_ref[target, 0, part, row : row + tall, :] = half.astype(jnp.bfloat16)
                else:
                    take = tall // out_rows
                    out_ref[b * take : (b + 1) * take, 0, part] = half.reshape(
                        take, out_rows, LANES
                    ).astype(jnp.bfloat16)


def clean(at, xs, basis, basis_t, gain, targets, rows_dev, slot, slots, before, steps=1):
    split = len(xs) > 1
    chans = basis.shape[0]
    sources = len(xs) if split else xs[0].shape[0]
    own = chans // sources
    swap = swap_table(min(256 // rows_dev, own), rows_dev)
    back = np.ascontiguousarray(swap_table(256 // rows_dev, rows_dev).T)
    vmem = pl.BlockSpec(memory_space=pltpu.VMEM)
    out_rows = chans * rows_dev // targets
    return pl.pallas_call(
        functools.partial(clean_kernel, split, len(before), steps),
        grid=(1,),
        in_specs=[pl.BlockSpec(memory_space=pltpu.SMEM)]
        + [vmem] * (len(xs) + 5)
        + [pl.BlockSpec(memory_space=pl.ANY)] * len(before),
        out_specs=[
            pl.BlockSpec((targets // steps, 1, 2, out_rows, LANES), lambda i: (0, slot, 0, 0, 0))
        ]
        * steps,
        out_shape=[
            jax.ShapeDtypeStruct((targets // steps, slots, 2, out_rows, LANES), jnp.bfloat16)
        ]
        * steps,
        input_output_aliases={6 + len(xs): 0} if slot else {},
        scratch_shapes=[pltpu.VMEM((chans, rows_dev * 2 * LANES), jnp.bfloat16)],
        compiler_params=params(),
        cost_estimate=pl.CostEstimate(
            flops=12 * chans * chans * rows_dev * LANES,
            bytes_accessed=8 * chans * rows_dev * LANES,
            transcendentals=0,
        ),
        name="clean",
    )(at, *xs, basis, basis_t, gain, jnp.asarray(swap), jnp.asarray(back), *before)


def image_kernel(scale, x_ref, table_ref, order_ref, *refs):
    out_ref = refs[-1]
    z, _, _, parts, rows, _ = x_ref.shape
    tiles = []
    for y_lo in range(RADIX):
        tile = x_ref[:, y_lo, 0]
        if rows % 16:
            tile = tile.astype(jnp.float32)
        tile = tile.reshape(z * parts * rows, LANES).astype(jnp.bfloat16)
        tiles.append(tile)
    value = jnp.dot(table_ref[...], jnp.concatenate(tiles, axis=1), preferred_element_type=jnp.float32)
    value = (value * scale).astype(jnp.bfloat16)
    value = jnp.dot(value, order_ref[...], preferred_element_type=jnp.float32)
    out_ref[...] = value.astype(jnp.bfloat16).reshape(out_ref.shape)


def image(x, slot, chunk, count, rows_dev, held):
    z, pieces, _, _, rows, _ = x.shape
    chans = rows // rows_dev
    total = z * rows_dev
    spread = pieces // RADIX
    wide = RADIX * LANES
    group = min(chans, max(1, 256 // (2 * total)))
    table = row_table(rows_dev, z, group)
    order = order_table()
    scale = 1.0 / math.sqrt(total * count * spread * wide)
    return pl.pallas_call(
        functools.partial(image_kernel, scale),
        grid=(chans // group, spread),
        in_specs=[
            pl.BlockSpec(
                (z, RADIX, 1, 2, group * rows_dev, LANES), lambda c, g: (0, g, slot, 0, c, 0)
            ),
            pl.BlockSpec(table.shape, lambda c, g: (0, 0)),
            pl.BlockSpec(order.shape, lambda c, g: (0, 0)),
        ]
        + [pl.BlockSpec(memory_space=pl.ANY)] * len(held),
        out_specs=pl.BlockSpec(
            (2, group, total, wide), lambda c, g: (0, c, 0, chunk * spread + g)
        ),
        out_shape=jax.ShapeDtypeStruct((2, chans, total, count * spread * wide), jnp.bfloat16),
        input_output_aliases={3: 0} if held else {},
        compiler_params=params(),
        cost_estimate=pl.CostEstimate(
            flops=4 * pieces * chans * total * LANES * wide,
            bytes_accessed=8 * pieces * chans * total * LANES,
            transcendentals=0,
        ),
        name="image",
    )(x, jnp.asarray(table), jnp.asarray(order), *held)


def row_kernel(scale, group, steps, at_ref, *refs):
    x_refs, table_ref, stage = refs[:steps], refs[steps], refs[-1]
    out_refs = refs[steps + 1 : -1]
    targets, _, chans, total, _ = stage.shape
    tall = x_refs[0].shape[3] // chans * group
    for target in range(targets):
        for c in range(chans // group):
            rows = slice(c * tall, (c + 1) * tall)
            tile = jnp.concatenate(
                [x_ref[target, 0, s, rows, :] for x_ref in x_refs for s in range(2)], axis=0
            )
            value = jnp.dot(table_ref[...], tile, preferred_element_type=jnp.float32) * scale
            stage[target, :, c * group : (c + 1) * group] = value.reshape(
                2, group, total, LANES
            ).astype(jnp.bfloat16)
    for step, out_ref in enumerate(out_refs):
        out_ref[...] = stage[partner(at_ref[0], step, targets)]


def row_transform(parts, at, chans, rows_dev, length):
    steps = len(parts)
    targets = parts[0].shape[0]
    total = steps * rows_dev
    group = min(chans, max(1, 256 // (2 * total)))
    tables = jnp.asarray(row_tables(rows_dev, steps, group))
    table = lax.dynamic_index_in_dim(tables, at[1], 0, keepdims=False)
    vmem = pl.BlockSpec(memory_space=pltpu.VMEM)
    return pl.pallas_call(
        functools.partial(row_kernel, 1.0 / math.sqrt(total * length), group, steps),
        in_specs=[pl.BlockSpec(memory_space=pltpu.SMEM)] + [vmem] * (steps + 1),
        out_specs=[vmem] * targets,
        out_shape=[jax.ShapeDtypeStruct((2, chans, total, LANES), jnp.bfloat16)] * targets,
        scratch_shapes=[pltpu.VMEM((targets, 2, chans, total, LANES), jnp.bfloat16)],
        compiler_params=params(),
        name="row_transform",
    )(at, *parts, table)


def place_kernel(count, at_ref, *refs):
    x_refs, order_ref, out_ref, stage = refs[:count], refs[count], refs[-2], refs[-1]
    for step, x_ref in enumerate(x_refs):
        stage[partner(at_ref[0], step, count)] = x_ref[...].reshape(stage.shape[1:])
    tile = jnp.concatenate([stage[y_lo] for y_lo in range(count)], axis=1)
    value = jnp.dot(tile, order_ref[...], preferred_element_type=jnp.float32)
    out_ref[...] = value.astype(jnp.bfloat16).reshape(out_ref.shape)


def place(xs, at, chunk, count, held):
    _, chans, total, _ = xs[0].shape
    order = order_table()
    wide = RADIX * LANES
    block = math.gcd(chans, 4)
    return pl.pallas_call(
        functools.partial(place_kernel, len(xs)),
        grid=(chans // block,),
        in_specs=[pl.BlockSpec(memory_space=pltpu.SMEM)]
        + [pl.BlockSpec((2, block, total, LANES), lambda c: (0, c, 0, 0))] * len(xs)
        + [pl.BlockSpec(order.shape, lambda c: (0, 0))]
        + [pl.BlockSpec(memory_space=pl.ANY)] * len(held),
        out_specs=pl.BlockSpec((2, block, total, wide), lambda c: (0, c, 0, chunk)),
        out_shape=jax.ShapeDtypeStruct((2, chans, total, count * wide), jnp.bfloat16),
        scratch_shapes=[pltpu.VMEM((len(xs), 2 * block * total, LANES), jnp.bfloat16)],
        input_output_aliases={2 + len(xs): 0} if held else {},
        compiler_params=params(),
        name="place",
    )(at, *xs, jnp.asarray(order), *held)


def hold_kernel(*refs):
    pass


def hold(x, after):
    untouched = pl.BlockSpec(memory_space=pl.ANY)
    return pl.pallas_call(
        hold_kernel,
        in_specs=[untouched] * (1 + len(after)),
        out_specs=untouched,
        out_shape=jax.ShapeDtypeStruct(x.shape, x.dtype),
        input_output_aliases={0: 0},
        name="hold",
    )(x, *after)


def spread_rows(parts):
    count = len(parts)
    out = list(parts)
    for step in sorted(range(1, count), key=lambda n: -min(n, count - n)):
        out[step] = lax.ppermute(parts[step], "uv", [(z, (z + step) % count) for z in range(count)])
    return out


def turn_kernel(basis_ref, out_ref):
    out_ref[...] = basis_ref[...].T


def turn(basis):
    vmem = pl.BlockSpec(memory_space=pltpu.VMEM)
    return pl.pallas_call(
        turn_kernel,
        in_specs=[vmem],
        out_specs=vmem,
        out_shape=jax.ShapeDtypeStruct(basis.shape[::-1], basis.dtype),
        compiler_params=params(),
        name="turn",
    )(basis)


def exchange(x, axes):
    return lax.all_to_all(x, axes, split_axis=0, concat_axis=0, tiled=True)


def scatter(pieces):
    count = len(pieces)
    return [pieces[0]] + [
        lax.ppermute(
            pieces[step], "chan", [(j, int(partner(np.int32(j), step, count))) for j in range(count)]
        )
        for step in range(1, count)
    ]


def shards(visibility, eigen_basis, eigenvalues, noise_power):
    uv_count = lax.axis_size("uv")
    chan_count = lax.axis_size("chan")
    _, chans, rows_dev, length = visibility.shape
    count = length // chan_count // LANES
    targets = uv_count * chan_count
    at = jnp.stack([lax.axis_index("chan"), lax.axis_index("uv")]).astype(jnp.int32)
    basis = exchange(jnp.broadcast_to(eigen_basis, (chan_count,) + eigen_basis.shape), "chan")
    basis = basis.reshape(chan_count * chans, -1)
    basis_t = turn(basis)
    gain = eigenvalues[:, None] / (eigenvalues[:, None] + noise_power[None, :])
    flat = visibility.reshape(2, chans * rows_dev, length)
    rows_first = count > 3 and chan_count == RADIX
    whole = 3 if rows_first else 2
    first = column_transform(flat, at, chan_count, [(0, False)])
    cells = [[exchange(first[0], "chan")]]
    sends = []
    if count > 1:
        sends = column_transform(flat, at, chan_count, [(k, k >= whole) for k in range(1, count)])
        cells.append([exchange(sends[0], "chan")])

    def cleaned_chunk(k, slot, slots, before, steps=1):
        return clean(
            at, cells[k], basis, basis_t, gain, targets, rows_dev, slot, slots, before, steps
        )

    before, lines = sends[:1], []
    groups = [[0]] + [g for g in (list(range(1, count - 1)), [count - 1]) if g and count > 1]
    if rows_first:
        groups = groups[1:]
        parts = spread_rows(cleaned_chunk(0, 0, 1, before, uv_count))
        before = []
        cells.append([exchange(hold(sends[1], [parts[uv_count // 2]]), "chan")])
        sends = sends[1:]
        lines = scatter(row_transform(parts, at, chans // uv_count, rows_dev, length))
    sends = sends[1:]
    for k in range(len(cells), count):
        cells.append(scatter(sends[:chan_count]))
        sends = sends[chan_count:]
    held = []
    for chunks in groups:
        if lines and chunks[-1] == count - 1:
            held = [place(lines, at, 0, count, held)]
        for slot, k in enumerate(chunks):
            if rows_first and k == 2:
                before = before + parts[1:]
            (cleaned,) = cleaned_chunk(k, slot, len(chunks), before)
            before = [cleaned]
        planes = exchange(cleaned, ("uv", "chan"))
        planes = planes.reshape((uv_count, chan_count) + planes.shape[1:])
        for slot, k in enumerate(chunks):
            held = [image(planes, slot, k, count, rows_dev, held)]
    return held[0]


def solution(mesh):
    in_specs = (P(None, "chan", "uv", None), P("chan", None), P(), P("uv"))
    out_specs = P(None, ("uv", "chan"), None, None)
    return jax.shard_map(shards, mesh=mesh, in_specs=in_specs, out_specs=out_specs, check_vma=False)
```

```python
import functools
import math

import jax
import jax.numpy as jnp
import numpy as np
from jax import lax
from jax.experimental import pallas as pl
from jax.experimental.pallas import tpu as pltpu
from jax.sharding import PartitionSpec as P

LANES = 128
RADIX = 8
VMEM_BYTES = 56 * 1024 * 1024


def params():
    return pltpu.CompilerParams(vmem_limit_bytes=VMEM_BYTES)


def inner_table(size):
    position = np.arange(size)
    phase = 2.0 * np.pi * (np.outer(position, position) % size) / size
    cosine, sine = np.cos(phase), np.sin(phase)
    return np.block([[cosine, sine], [-sine, cosine]]).astype(jnp.bfloat16)


def twiddle_table(length):
    inner = length // RADIX
    phase = 2.0 * np.pi * np.outer(np.arange(RADIX), np.arange(inner)) / length
    return np.stack([np.cos(phase), np.sin(phase)], axis=1).astype(np.float32)


def order_table():
    table = np.zeros((RADIX, LANES, LANES, RADIX), np.float32)
    for y_lo in range(RADIX):
        for y_hi in range(LANES):
            table[y_lo, y_hi, y_hi, y_lo] = 1.0
    return table.reshape(RADIX * LANES, RADIX * LANES).astype(jnp.bfloat16)


def swap_table(major, minor):
    table = np.zeros((major * minor, major * minor), np.float32)
    for a in range(major):
        for b in range(minor):
            table[b * major + a, a * minor + b] = 1.0
    return table.astype(jnp.bfloat16)


def row_table(rows_dev, uv_count, group):
    total = rows_dev * uv_count
    position = np.arange(total)
    phase = 2.0 * np.pi * (np.outer(position, position) % total) / total
    cosine, sine = np.cos(phase), np.sin(phase)
    parts = np.array([[cosine, -sine], [sine, cosine]])
    parts = parts.reshape(2, 2, total, uv_count, rows_dev)
    size = 2 * group * total
    table = np.einsum("tsxzu,cd->tcxzsdu", parts, np.eye(group))
    return table.reshape(size, size).astype(jnp.bfloat16)


def row_tables(rows_dev, uv_count, group):
    total = rows_dev * uv_count
    position = np.arange(total)
    phase = 2.0 * np.pi * (np.outer(position, position) % total) / total
    cosine, sine = np.cos(phase), np.sin(phase)
    parts = np.array([[cosine, -sine], [sine, cosine]])
    parts = parts.reshape(2, 2, total, uv_count, rows_dev)
    eye = np.eye(group)
    size = 2 * group * total
    tables = []
    for at in range(uv_count):
        order = (at - np.arange(uv_count)) % uv_count
        table = np.einsum("tsxzu,cd->tcxzsdu", parts[:, :, :, order], eye)
        tables.append(table.reshape(size, size).astype(jnp.bfloat16))
    return np.stack(tables)


def butterfly8(re, im):
    def dft2(ar, ai, br, bi):
        return ar + br, ai + bi, ar - br, ai - bi

    def dft4(r, i):
        s0r, s0i, d0r, d0i = dft2(r[0], i[0], r[2], i[2])
        s1r, s1i, d1r, d1i = dft2(r[1], i[1], r[3], i[3])
        return (
            [s0r + s1r, d0r - d1i, s0r - s1r, d0r + d1i],
            [s0i + s1i, d0i + d1r, s0i - s1i, d0i - d1r],
        )

    er, ei = dft4(re[0::2], im[0::2])
    orr, oi = dft4(re[1::2], im[1::2])
    half = math.sqrt(0.5)
    turned_r = [orr[0], (orr[1] - oi[1]) * half, -oi[2], (-orr[3] - oi[3]) * half]
    turned_i = [oi[0], (orr[1] + oi[1]) * half, orr[2], (orr[3] - oi[3]) * half]
    out_r = [er[k] + turned_r[k] for k in range(4)] + [er[k] - turned_r[k] for k in range(4)]
    out_i = [ei[k] + turned_i[k] for k in range(4)] + [ei[k] - turned_i[k] for k in range(4)]
    return out_r, out_i


def column_kernel(chunks, spread, at_ref, x_ref, twiddle_ref, table_ref, *refs):
    *out_refs, mid, stage = refs
    pieces = spread * RADIX
    rows, length = x_ref.shape[1:]
    inner = length // RADIX
    step = 16
    for i in range(rows // step):
        at = slice(i * step, (i + 1) * step)
        for block in range(inner // LANES):
            re, im = [], []
            for a in range(RADIX):
                lanes = slice(a * inner + block * LANES, a * inner + (block + 1) * LANES)
                re.append(x_ref[0, at, lanes].astype(jnp.float32))
                im.append(x_ref[1, at, lanes].astype(jnp.float32))
            re, im = butterfly8(re, im)
            lanes = slice(block * LANES, (block + 1) * LANES)
            other = slice(inner + block * LANES, inner + (block + 1) * LANES)
            for y_lo in range(RADIX):
                if y_lo == 0:
                    tr, ti = re[0], im[0]
                else:
                    cosine = twiddle_ref[y_lo, 0:1, lanes]
                    sine = twiddle_ref[y_lo, 1:2, lanes]
                    tr = re[y_lo] * cosine - im[y_lo] * sine
                    ti = re[y_lo] * sine + im[y_lo] * cosine
                mid[y_lo, at, lanes] = tr.astype(jnp.bfloat16)
                mid[y_lo, at, other] = ti.astype(jnp.bfloat16)
    for chunk, split in chunks:
        outs = out_refs[: pieces if split else 1]
        out_refs = out_refs[len(outs) :]
        for group in range(spread):
            column = (chunk * spread + group) * LANES
            table = jnp.concatenate(
                [table_ref[:, at : at + LANES] for at in (column, inner + column)], axis=1
            )
            wide = jnp.dot(
                mid[...].reshape(RADIX * rows, 2 * inner), table, preferred_element_type=jnp.float32
            ).astype(jnp.bfloat16)
            for y_lo in range(RADIX):
                for part in range(2):
                    value = wide[y_lo * rows : (y_lo + 1) * rows, part * LANES : (part + 1) * LANES]
                    if split:
                        stage[group * RADIX + y_lo, part] = value
                    else:
                        outs[0][group * RADIX + y_lo, part] = value
        if split:
            for step, out_ref in enumerate(outs):
                out_ref[...] = stage[partner(at_ref[0], step, pieces)]


def partner(at, step, count):
    if count & (count - 1):
        return (count - at + step) % count
    if step:
        step = sorted(range(1, count), key=lambda n: (-bin(n // 2).count("1"), -n))[step - 1]
    return at ^ step


def column_transform(x, at, pieces, chunks):
    _, rows, length = x.shape
    inner = length // RADIX
    block = math.gcd(rows, 128)
    specs, shapes = [], []
    for _, split in chunks:
        if split:
            specs += [pl.BlockSpec((2, block, LANES), lambda i, at: (0, i, 0))] * pieces
            shapes += [jax.ShapeDtypeStruct((2, rows, LANES), jnp.bfloat16)] * pieces
        else:
            specs.append(pl.BlockSpec((pieces, 2, block, LANES), lambda i, at: (0, 0, i, 0)))
            shapes.append(jax.ShapeDtypeStruct((pieces, 2, rows, LANES), jnp.bfloat16))
    return pl.pallas_call(
        functools.partial(column_kernel, chunks, pieces // RADIX),
        grid_spec=pltpu.PrefetchScalarGridSpec(
            num_scalar_prefetch=1,
            grid=(rows // block,),
            in_specs=[
                pl.BlockSpec((2, block, length), lambda i, at: (0, i, 0)),
                pl.BlockSpec((RADIX, 2, inner), lambda i, at: (0, 0, 0)),
                pl.BlockSpec((2 * inner, 2 * inner), lambda i, at: (0, 0)),
            ],
            out_specs=specs,
            scratch_shapes=[
                pltpu.VMEM((RADIX, block, 2 * inner), jnp.bfloat16),
                pltpu.VMEM((pieces, 2, block, LANES), jnp.bfloat16),
            ],
        ),
        out_shape=shapes,
        compiler_params=params(),
        cost_estimate=pl.CostEstimate(
            flops=4 * rows * length * LANES * pieces * len(chunks),
            bytes_accessed=8 * rows * length,
            transcendentals=0,
        ),
        name="column_transform",
    )(at, x, jnp.asarray(twiddle_table(length)), jnp.asarray(inner_table(inner)))


def clean_kernel(split, waits, steps, at_ref, *refs):
    refs, out_refs, slab = refs[: -1 - steps], refs[-1 - steps : -1], refs[-1]
    *x_refs, basis_ref, basis_t_ref, gain_ref, swap_ref, back_ref = refs[: len(refs) - waits]
    chans = slab.shape[0]
    pair = 2 * LANES
    rows_dev = slab.shape[1] // pair
    tall = swap_ref.shape[0]
    group = tall // rows_dev
    sources = len(x_refs) if split else x_refs[0].shape[0]
    own = chans // sources
    for source in range(sources):
        block = x_refs[source] if split else x_refs[0].at[source]
        begin = partner(at_ref[0], source, sources) * own if split else source * own
        for k in range(own // group):
            rows = slice(k * tall, (k + 1) * tall)
            turned = jnp.dot(
                swap_ref[...],
                jnp.concatenate([block[0, rows, :], block[1, rows, :]], axis=1),
                preferred_element_type=jnp.float32,
            ).astype(jnp.bfloat16)
            channels = pl.ds(pl.multiple_of(begin + k * group, group), group)
            for u in range(rows_dev):
                slab[channels, u * pair : (u + 1) * pair] = turned[u * group : (u + 1) * group]
    for u in range(rows_dev):
        lanes = slice(u * pair, (u + 1) * pair)
        line = slab[:, lanes]
        amps = jnp.dot(basis_t_ref[...], line, preferred_element_type=jnp.float32)
        amps = amps.astype(jnp.bfloat16).astype(jnp.float32)
        front = (gain_ref[:, u : u + 1] * amps).astype(jnp.bfloat16)
        drop = jnp.dot(basis_ref[...], front, preferred_element_type=jnp.float32)
        slab[:, lanes] = (line.astype(jnp.float32) - drop).astype(jnp.bfloat16)
    out_rows = out_refs[0].shape[3]
    tall = back_ref.shape[0]
    group = tall // rows_dev
    share = chans // steps
    for step, out_ref in enumerate(out_refs):
        start = lax.rem(at_ref[1] + step, steps) * share if steps > 1 else 0
        for b in range(share // group):
            channels = pl.ds(pl.multiple_of(start + b * group, group), group)
            tile = jnp.concatenate(
                [slab[channels, u * pair : (u + 1) * pair] for u in range(rows_dev)], axis=0
            )
            value = jnp.dot(back_ref[...], tile, preferred_element_type=jnp.float32)
            for part in range(2):
                half = value[:, part * LANES : (part + 1) * LANES]
                if out_rows % tall == 0:
                    target, row = divmod(b * tall, out_rows)
                    out_ref[target, 0, part, row : row + tall, :] = half.astype(jnp.bfloat16)
                else:
                    take = tall // out_rows
                    out_ref[b * take : (b + 1) * take, 0, part] = half.reshape(
                        take, out_rows, LANES
                    ).astype(jnp.bfloat16)


def clean(at, xs, basis, basis_t, gain, targets, rows_dev, slot, slots, before, steps=1):
    split = len(xs) > 1
    chans = basis.shape[0]
    sources = len(xs) if split else xs[0].shape[0]
    own = chans // sources
    swap = swap_table(min(256 // rows_dev, own), rows_dev)
    back = np.ascontiguousarray(swap_table(256 // rows_dev, rows_dev).T)
    vmem = pl.BlockSpec(memory_space=pltpu.VMEM)
    out_rows = chans * rows_dev // targets
    return pl.pallas_call(
        functools.partial(clean_kernel, split, len(before), steps),
        grid=(1,),
        in_specs=[pl.BlockSpec(memory_space=pltpu.SMEM)]
        + [vmem] * (len(xs) + 5)
        + [pl.BlockSpec(memory_space=pl.ANY)] * len(before),
        out_specs=[
            pl.BlockSpec((targets // steps, 1, 2, out_rows, LANES), lambda i: (0, slot, 0, 0, 0))
        ]
        * steps,
        out_shape=[
            jax.ShapeDtypeStruct((targets // steps, slots, 2, out_rows, LANES), jnp.bfloat16)
        ]
        * steps,
        input_output_aliases={6 + len(xs): 0} if slot else {},
        scratch_shapes=[pltpu.VMEM((chans, rows_dev * 2 * LANES), jnp.bfloat16)],
        compiler_params=params(),
        cost_estimate=pl.CostEstimate(
            flops=12 * chans * chans * rows_dev * LANES,
            bytes_accessed=8 * chans * rows_dev * LANES,
            transcendentals=0,
        ),
        name="clean",
    )(at, *xs, basis, basis_t, gain, jnp.asarray(swap), jnp.asarray(back), *before)


def image_kernel(scale, x_ref, table_ref, order_ref, *refs):
    out_ref = refs[-1]
    z, _, _, parts, rows, _ = x_ref.shape
    tiles = []
    for y_lo in range(RADIX):
        tile = x_ref[:, y_lo, 0]
        if rows % 16:
            tile = tile.astype(jnp.float32)
        tile = tile.reshape(z * parts * rows, LANES).astype(jnp.bfloat16)
        tiles.append(tile)
    value = jnp.dot(table_ref[...], jnp.concatenate(tiles, axis=1), preferred_element_type=jnp.float32)
    value = (value * scale).astype(jnp.bfloat16)
    value = jnp.dot(value, order_ref[...], preferred_element_type=jnp.float32)
    out_ref[...] = value.astype(jnp.bfloat16).reshape(out_ref.shape)


def image(x, slot, chunk, count, rows_dev, held):
    z, pieces, _, _, rows, _ = x.shape
    chans = rows // rows_dev
    total = z * rows_dev
    spread = pieces // RADIX
    wide = RADIX * LANES
    group = min(chans, max(1, 256 // (2 * total)))
    table = row_table(rows_dev, z, group)
    order = order_table()
    scale = 1.0 / math.sqrt(total * count * spread * wide)
    return pl.pallas_call(
        functools.partial(image_kernel, scale),
        grid=(chans // group, spread),
        in_specs=[
            pl.BlockSpec(
                (z, RADIX, 1, 2, group * rows_dev, LANES), lambda c, g: (0, g, slot, 0, c, 0)
            ),
            pl.BlockSpec(table.shape, lambda c, g: (0, 0)),
            pl.BlockSpec(order.shape, lambda c, g: (0, 0)),
        ]
        + [pl.BlockSpec(memory_space=pl.ANY)] * len(held),
        out_specs=pl.BlockSpec(
            (2, group, total, wide), lambda c, g: (0, c, 0, chunk * spread + g)
        ),
        out_shape=jax.ShapeDtypeStruct((2, chans, total, count * spread * wide), jnp.bfloat16),
        input_output_aliases={3: 0} if held else {},
        compiler_params=params(),
        cost_estimate=pl.CostEstimate(
            flops=4 * pieces * chans * total * LANES * wide,
            bytes_accessed=8 * pieces * chans * total * LANES,
            transcendentals=0,
        ),
        name="image",
    )(x, jnp.asarray(table), jnp.asarray(order), *held)


def row_kernel(scale, group, steps, at_ref, *refs):
    x_refs, table_ref, stage = refs[:steps], refs[steps], refs[-1]
    out_refs = refs[steps + 1 : -1]
    targets, _, chans, total, _ = stage.shape
    tall = x_refs[0].shape[3] // chans * group
    for target in range(targets):
        for c in range(chans // group):
            rows = slice(c * tall, (c + 1) * tall)
            tile = jnp.concatenate(
                [x_ref[target, 0, s, rows, :] for x_ref in x_refs for s in range(2)], axis=0
            )
            value = jnp.dot(table_ref[...], tile, preferred_element_type=jnp.float32) * scale
            stage[target, :, c * group : (c + 1) * group] = value.reshape(
                2, group, total, LANES
            ).astype(jnp.bfloat16)
    for step, out_ref in enumerate(out_refs):
        out_ref[...] = stage[partner(at_ref[0], step, targets)]


def row_transform(parts, at, chans, rows_dev, length):
    steps = len(parts)
    targets = parts[0].shape[0]
    total = steps * rows_dev
    group = min(chans, max(1, 256 // (2 * total)))
    tables = jnp.asarray(row_tables(rows_dev, steps, group))
    table = lax.dynamic_index_in_dim(tables, at[1], 0, keepdims=False)
    vmem = pl.BlockSpec(memory_space=pltpu.VMEM)
    return pl.pallas_call(
        functools.partial(row_kernel, 1.0 / math.sqrt(total * length), group, steps),
        in_specs=[pl.BlockSpec(memory_space=pltpu.SMEM)] + [vmem] * (steps + 1),
        out_specs=[vmem] * targets,
        out_shape=[jax.ShapeDtypeStruct((2, chans, total, LANES), jnp.bfloat16)] * targets,
        scratch_shapes=[pltpu.VMEM((targets, 2, chans, total, LANES), jnp.bfloat16)],
        compiler_params=params(),
        name="row_transform",
    )(at, *parts, table)


def place_kernel(count, at_ref, *refs):
    x_refs, order_ref, out_ref, stage = refs[:count], refs[count], refs[-2], refs[-1]
    for step, x_ref in enumerate(x_refs):
        stage[partner(at_ref[0], step, count)] = x_ref[...].reshape(stage.shape[1:])
    tile = jnp.concatenate([stage[y_lo] for y_lo in range(count)], axis=1)
    value = jnp.dot(tile, order_ref[...], preferred_element_type=jnp.float32)
    out_ref[...] = value.astype(jnp.bfloat16).reshape(out_ref.shape)


def place(xs, at, chunk, count, held):
    _, chans, total, _ = xs[0].shape
    order = order_table()
    wide = RADIX * LANES
    block = math.gcd(chans, 4)
    return pl.pallas_call(
        functools.partial(place_kernel, len(xs)),
        grid=(chans // block,),
        in_specs=[pl.BlockSpec(memory_space=pltpu.SMEM)]
        + [pl.BlockSpec((2, block, total, LANES), lambda c: (0, c, 0, 0))] * len(xs)
        + [pl.BlockSpec(order.shape, lambda c: (0, 0))]
        + [pl.BlockSpec(memory_space=pl.ANY)] * len(held),
        out_specs=pl.BlockSpec((2, block, total, wide), lambda c: (0, c, 0, chunk)),
        out_shape=jax.ShapeDtypeStruct((2, chans, total, count * wide), jnp.bfloat16),
        scratch_shapes=[pltpu.VMEM((len(xs), 2 * block * total, LANES), jnp.bfloat16)],
        input_output_aliases={2 + len(xs): 0} if held else {},
        compiler_params=params(),
        name="place",
    )(at, *xs, jnp.asarray(order), *held)


def hold_kernel(*refs):
    pass


def hold(x, after):
    untouched = pl.BlockSpec(memory_space=pl.ANY)
    return pl.pallas_call(
        hold_kernel,
        in_specs=[untouched] * (1 + len(after)),
        out_specs=untouched,
        out_shape=jax.ShapeDtypeStruct(x.shape, x.dtype),
        input_output_aliases={0: 0},
        name="hold",
    )(x, *after)


def spread_rows(parts):
    count = len(parts)
    out = list(parts)
    for step in sorted(range(1, count), key=lambda n: -min(n, count - n)):
        out[step] = lax.ppermute(parts[step], "uv", [(z, (z + step) % count) for z in range(count)])
    return out


def turn_kernel(basis_ref, out_ref):
    out_ref[...] = basis_ref[...].T


def turn(basis):
    vmem = pl.BlockSpec(memory_space=pltpu.VMEM)
    return pl.pallas_call(
        turn_kernel,
        in_specs=[vmem],
        out_specs=vmem,
        out_shape=jax.ShapeDtypeStruct(basis.shape[::-1], basis.dtype),
        compiler_params=params(),
        name="turn",
    )(basis)


def exchange(x, axes):
    return lax.all_to_all(x, axes, split_axis=0, concat_axis=0, tiled=True)


def scatter(pieces):
    count = len(pieces)
    return [pieces[0]] + [
        lax.ppermute(
            pieces[step], "chan", [(j, int(partner(np.int32(j), step, count))) for j in range(count)]
        )
        for step in range(1, count)
    ]


def shards(visibility, eigen_basis, eigenvalues, noise_power):
    uv_count = lax.axis_size("uv")
    chan_count = lax.axis_size("chan")
    _, chans, rows_dev, length = visibility.shape
    count = length // chan_count // LANES
    targets = uv_count * chan_count
    at = jnp.stack([lax.axis_index("chan"), lax.axis_index("uv")]).astype(jnp.int32)
    basis = exchange(jnp.broadcast_to(eigen_basis, (chan_count,) + eigen_basis.shape), "chan")
    basis = basis.reshape(chan_count * chans, -1)
    basis_t = turn(basis)
    gain = eigenvalues[:, None] / (eigenvalues[:, None] + noise_power[None, :])
    flat = visibility.reshape(2, chans * rows_dev, length)
    rows_first = count > 3 and chan_count == RADIX
    whole = 3 if rows_first else 2
    first = column_transform(flat, at, chan_count, [(0, False)])
    cells = [[exchange(first[0], "chan")]]
    sends = []
    if count > 1:
        sends = list(
            column_transform(flat, at, chan_count, [(k, k >= whole) for k in range(1, count)])
        )
        sends[0] = hold(sends[0], [basis_t])
        cells.append([exchange(sends[0], "chan")])

    def cleaned_chunk(k, slot, slots, before, steps=1):
        return clean(
            at, cells[k], basis, basis_t, gain, targets, rows_dev, slot, slots, before, steps
        )

    before, lines = sends[:1], []
    groups = [[0]] + [g for g in (list(range(1, count - 1)), [count - 1]) if g and count > 1]
    if rows_first:
        groups = groups[1:]
        parts = spread_rows(cleaned_chunk(0, 0, 1, before, uv_count))
        before = []
        cells.append([exchange(hold(sends[1], [parts[1]]), "chan")])
        sends = sends[1:]
        lines = scatter(row_transform(parts, at, chans // uv_count, rows_dev, length))
    sends = sends[1:]
    for k in range(len(cells), count):
        cells.append(scatter(sends[:chan_count]))
        sends = sends[chan_count:]
    held = []
    for chunks in groups:
        if lines and chunks[-1] == count - 1:
            held = [place(lines, at, 0, count, held)]
        for slot, k in enumerate(chunks):
            if rows_first and k == 2:
                before = before + [parts[uv_count // 2]]
            if rows_first and k == count - 1:
                before = before + lines[:1]
            (cleaned,) = cleaned_chunk(k, slot, len(chunks), before)
            before = [cleaned]
        planes = exchange(cleaned, ("uv", "chan"))
        planes = planes.reshape((uv_count, chan_count) + planes.shape[1:])
        for slot, k in enumerate(chunks):
            held = [image(planes, slot, k, count, rows_dev, held)]
    return held[0]


def solution(mesh):
    in_specs = (P(None, "chan", "uv", None), P("chan", None), P(), P("uv"))
    out_specs = P(None, ("uv", "chan"), None, None)
    return jax.shard_map(shards, mesh=mesh, in_specs=in_specs, out_specs=out_specs, check_vma=False)
```

```python
import functools
import math

import jax
import jax.numpy as jnp
import numpy as np
from jax import lax
from jax.experimental import pallas as pl
from jax.experimental.pallas import tpu as pltpu
from jax.sharding import PartitionSpec as P

LANES = 128
RADIX = 8
VMEM_BYTES = 56 * 1024 * 1024


def params():
    return pltpu.CompilerParams(vmem_limit_bytes=VMEM_BYTES)


def inner_table(size):
    position = np.arange(size)
    phase = 2.0 * np.pi * (np.outer(position, position) % size) / size
    cosine, sine = np.cos(phase), np.sin(phase)
    return np.block([[cosine, sine], [-sine, cosine]]).astype(jnp.bfloat16)


def twiddle_table(length):
    inner = length // RADIX
    phase = 2.0 * np.pi * np.outer(np.arange(RADIX), np.arange(inner)) / length
    return np.stack([np.cos(phase), np.sin(phase)], axis=1).astype(np.float32)


def order_table():
    table = np.zeros((RADIX, LANES, LANES, RADIX), np.float32)
    for y_lo in range(RADIX):
        for y_hi in range(LANES):
            table[y_lo, y_hi, y_hi, y_lo] = 1.0
    return table.reshape(RADIX * LANES, RADIX * LANES).astype(jnp.bfloat16)


def swap_table(major, minor):
    table = np.zeros((major * minor, major * minor), np.float32)
    for a in range(major):
        for b in range(minor):
            table[b * major + a, a * minor + b] = 1.0
    return table.astype(jnp.bfloat16)


def row_table(rows_dev, uv_count, group):
    total = rows_dev * uv_count
    position = np.arange(total)
    phase = 2.0 * np.pi * (np.outer(position, position) % total) / total
    cosine, sine = np.cos(phase), np.sin(phase)
    parts = np.array([[cosine, -sine], [sine, cosine]])
    parts = parts.reshape(2, 2, total, uv_count, rows_dev)
    size = 2 * group * total
    table = np.einsum("tsxzu,cd->tcxzsdu", parts, np.eye(group))
    return table.reshape(size, size).astype(jnp.bfloat16)


def row_tables(rows_dev, uv_count, group):
    total = rows_dev * uv_count
    position = np.arange(total)
    phase = 2.0 * np.pi * (np.outer(position, position) % total) / total
    cosine, sine = np.cos(phase), np.sin(phase)
    parts = np.array([[cosine, -sine], [sine, cosine]])
    parts = parts.reshape(2, 2, total, uv_count, rows_dev)
    eye = np.eye(group)
    size = 2 * group * total
    tables = []
    for at in range(uv_count):
        order = (at - np.arange(uv_count)) % uv_count
        table = np.einsum("tsxzu,cd->tcxzsdu", parts[:, :, :, order], eye)
        tables.append(table.reshape(size, size).astype(jnp.bfloat16))
    return np.stack(tables)


def butterfly8(re, im):
    def dft2(ar, ai, br, bi):
        return ar + br, ai + bi, ar - br, ai - bi

    def dft4(r, i):
        s0r, s0i, d0r, d0i = dft2(r[0], i[0], r[2], i[2])
        s1r, s1i, d1r, d1i = dft2(r[1], i[1], r[3], i[3])
        return (
            [s0r + s1r, d0r - d1i, s0r - s1r, d0r + d1i],
            [s0i + s1i, d0i + d1r, s0i - s1i, d0i - d1r],
        )

    er, ei = dft4(re[0::2], im[0::2])
    orr, oi = dft4(re[1::2], im[1::2])
    half = math.sqrt(0.5)
    turned_r = [orr[0], (orr[1] - oi[1]) * half, -oi[2], (-orr[3] - oi[3]) * half]
    turned_i = [oi[0], (orr[1] + oi[1]) * half, orr[2], (orr[3] - oi[3]) * half]
    out_r = [er[k] + turned_r[k] for k in range(4)] + [er[k] - turned_r[k] for k in range(4)]
    out_i = [ei[k] + turned_i[k] for k in range(4)] + [ei[k] - turned_i[k] for k in range(4)]
    return out_r, out_i


def column_kernel(chunks, spread, at_ref, x_ref, twiddle_ref, table_ref, *refs):
    *out_refs, mid, stage = refs
    pieces = spread * RADIX
    rows, length = x_ref.shape[1:]
    inner = length // RADIX
    step = 16
    for i in range(rows // step):
        at = slice(i * step, (i + 1) * step)
        for block in range(inner // LANES):
            re, im = [], []
            for a in range(RADIX):
                lanes = slice(a * inner + block * LANES, a * inner + (block + 1) * LANES)
                re.append(x_ref[0, at, lanes].astype(jnp.float32))
                im.append(x_ref[1, at, lanes].astype(jnp.float32))
            re, im = butterfly8(re, im)
            lanes = slice(block * LANES, (block + 1) * LANES)
            other = slice(inner + block * LANES, inner + (block + 1) * LANES)
            for y_lo in range(RADIX):
                if y_lo == 0:
                    tr, ti = re[0], im[0]
                else:
                    cosine = twiddle_ref[y_lo, 0:1, lanes]
                    sine = twiddle_ref[y_lo, 1:2, lanes]
                    tr = re[y_lo] * cosine - im[y_lo] * sine
                    ti = re[y_lo] * sine + im[y_lo] * cosine
                mid[y_lo, at, lanes] = tr.astype(jnp.bfloat16)
                mid[y_lo, at, other] = ti.astype(jnp.bfloat16)
    for chunk, split in chunks:
        outs = out_refs[: pieces if split else 1]
        out_refs = out_refs[len(outs) :]
        for group in range(spread):
            column = (chunk * spread + group) * LANES
            table = jnp.concatenate(
                [table_ref[:, at : at + LANES] for at in (column, inner + column)], axis=1
            )
            wide = jnp.dot(
                mid[...].reshape(RADIX * rows, 2 * inner), table, preferred_element_type=jnp.float32
            ).astype(jnp.bfloat16)
            for y_lo in range(RADIX):
                for part in range(2):
                    value = wide[y_lo * rows : (y_lo + 1) * rows, part * LANES : (part + 1) * LANES]
                    if split:
                        stage[group * RADIX + y_lo, part] = value
                    else:
                        outs[0][group * RADIX + y_lo, part] = value
        if split:
            for step, out_ref in enumerate(outs):
                out_ref[...] = stage[partner(at_ref[0], step, pieces)]


def partner(at, step, count):
    if count & (count - 1):
        return (count - at + step) % count
    if step:
        step = sorted(range(1, count), key=lambda n: (-bin(n // 2).count("1"), -n))[step - 1]
    return at ^ step


def column_transform(x, at, pieces, chunks):
    _, rows, length = x.shape
    inner = length // RADIX
    block = math.gcd(rows, 128)
    specs, shapes = [], []
    for _, split in chunks:
        if split:
            specs += [pl.BlockSpec((2, block, LANES), lambda i, at: (0, i, 0))] * pieces
            shapes += [jax.ShapeDtypeStruct((2, rows, LANES), jnp.bfloat16)] * pieces
        else:
            specs.append(pl.BlockSpec((pieces, 2, block, LANES), lambda i, at: (0, 0, i, 0)))
            shapes.append(jax.ShapeDtypeStruct((pieces, 2, rows, LANES), jnp.bfloat16))
    return pl.pallas_call(
        functools.partial(column_kernel, chunks, pieces // RADIX),
        grid_spec=pltpu.PrefetchScalarGridSpec(
            num_scalar_prefetch=1,
            grid=(rows // block,),
            in_specs=[
                pl.BlockSpec((2, block, length), lambda i, at: (0, i, 0)),
                pl.BlockSpec((RADIX, 2, inner), lambda i, at: (0, 0, 0)),
                pl.BlockSpec((2 * inner, 2 * inner), lambda i, at: (0, 0)),
            ],
            out_specs=specs,
            scratch_shapes=[
                pltpu.VMEM((RADIX, block, 2 * inner), jnp.bfloat16),
                pltpu.VMEM((pieces, 2, block, LANES), jnp.bfloat16),
            ],
        ),
        out_shape=shapes,
        compiler_params=params(),
        cost_estimate=pl.CostEstimate(
            flops=4 * rows * length * LANES * pieces * len(chunks),
            bytes_accessed=8 * rows * length,
            transcendentals=0,
        ),
        name="column_transform",
    )(at, x, jnp.asarray(twiddle_table(length)), jnp.asarray(inner_table(inner)))


def clean_kernel(split, waits, steps, at_ref, *refs):
    refs, out_refs, slab = refs[: -1 - steps], refs[-1 - steps : -1], refs[-1]
    *x_refs, basis_ref, basis_t_ref, gain_ref, swap_ref, back_ref = refs[: len(refs) - waits]
    chans = slab.shape[0]
    pair = 2 * LANES
    rows_dev = slab.shape[1] // pair
    tall = swap_ref.shape[0]
    group = tall // rows_dev
    sources = len(x_refs) if split else x_refs[0].shape[0]
    own = chans // sources
    for source in range(sources):
        block = x_refs[source] if split else x_refs[0].at[source]
        begin = partner(at_ref[0], source, sources) * own if split else source * own
        for k in range(own // group):
            rows = slice(k * tall, (k + 1) * tall)
            turned = jnp.dot(
                swap_ref[...],
                jnp.concatenate([block[0, rows, :], block[1, rows, :]], axis=1),
                preferred_element_type=jnp.float32,
            ).astype(jnp.bfloat16)
            channels = pl.ds(pl.multiple_of(begin + k * group, group), group)
            for u in range(rows_dev):
                slab[channels, u * pair : (u + 1) * pair] = turned[u * group : (u + 1) * group]
    for u in range(rows_dev):
        lanes = slice(u * pair, (u + 1) * pair)
        line = slab[:, lanes]
        amps = jnp.dot(basis_t_ref[...], line, preferred_element_type=jnp.float32)
        amps = amps.astype(jnp.bfloat16).astype(jnp.float32)
        front = (gain_ref[:, u : u + 1] * amps).astype(jnp.bfloat16)
        drop = jnp.dot(basis_ref[...], front, preferred_element_type=jnp.float32)
        slab[:, lanes] = (line.astype(jnp.float32) - drop).astype(jnp.bfloat16)
    out_rows = out_refs[0].shape[3]
    tall = back_ref.shape[0]
    group = tall // rows_dev
    share = chans // steps
    for step, out_ref in enumerate(out_refs):
        start = lax.rem(at_ref[1] + step, steps) * share if steps > 1 else 0
        for b in range(share // group):
            channels = pl.ds(pl.multiple_of(start + b * group, group), group)
            tile = jnp.concatenate(
                [slab[channels, u * pair : (u + 1) * pair] for u in range(rows_dev)], axis=0
            )
            value = jnp.dot(back_ref[...], tile, preferred_element_type=jnp.float32)
            for part in range(2):
                half = value[:, part * LANES : (part + 1) * LANES]
                if out_rows % tall == 0:
                    target, row = divmod(b * tall, out_rows)
                    out_ref[target, 0, part, row : row + tall, :] = half.astype(jnp.bfloat16)
                else:
                    take = tall // out_rows
                    out_ref[b * take : (b + 1) * take, 0, part] = half.reshape(
                        take, out_rows, LANES
                    ).astype(jnp.bfloat16)


def clean(at, xs, basis, basis_t, gain, targets, rows_dev, slot, slots, before, steps=1):
    split = len(xs) > 1
    chans = basis.shape[0]
    sources = len(xs) if split else xs[0].shape[0]
    own = chans // sources
    swap = swap_table(min(256 // rows_dev, own), rows_dev)
    back = np.ascontiguousarray(swap_table(256 // rows_dev, rows_dev).T)
    vmem = pl.BlockSpec(memory_space=pltpu.VMEM)
    out_rows = chans * rows_dev // targets
    return pl.pallas_call(
        functools.partial(clean_kernel, split, len(before), steps),
        grid=(1,),
        in_specs=[pl.BlockSpec(memory_space=pltpu.SMEM)]
        + [vmem] * (len(xs) + 5)
        + [pl.BlockSpec(memory_space=pl.ANY)] * len(before),
        out_specs=[
            pl.BlockSpec((targets // steps, 1, 2, out_rows, LANES), lambda i: (0, slot, 0, 0, 0))
        ]
        * steps,
        out_shape=[
            jax.ShapeDtypeStruct((targets // steps, slots, 2, out_rows, LANES), jnp.bfloat16)
        ]
        * steps,
        input_output_aliases={6 + len(xs): 0} if slot else {},
        scratch_shapes=[pltpu.VMEM((chans, rows_dev * 2 * LANES), jnp.bfloat16)],
        compiler_params=params(),
        cost_estimate=pl.CostEstimate(
            flops=12 * chans * chans * rows_dev * LANES,
            bytes_accessed=8 * chans * rows_dev * LANES,
            transcendentals=0,
        ),
        name="clean",
    )(at, *xs, basis, basis_t, gain, jnp.asarray(swap), jnp.asarray(back), *before)


def image_kernel(scale, x_ref, table_ref, order_ref, *refs):
    out_ref = refs[-1]
    z, _, _, parts, rows, _ = x_ref.shape
    _, chans, total, _ = out_ref.shape
    subs = 2 * chans * total // table_ref.shape[0]
    own = rows // subs
    values = []
    for sub in range(subs):
        tiles = []
        for y_lo in range(RADIX):
            tile = x_ref[:, y_lo, 0, :, sub * own : (sub + 1) * own, :]
            if own % 16:
                tile = tile.astype(jnp.float32)
            tiles.append(tile.reshape(z * parts * own, LANES).astype(jnp.bfloat16))
        tile = jnp.concatenate(tiles, axis=1)
        value = jnp.dot(table_ref[...], tile, preferred_element_type=jnp.float32)
        values.append((value * scale).astype(jnp.bfloat16))
    value = jnp.dot(
        jnp.concatenate(values, axis=0), order_ref[...], preferred_element_type=jnp.float32
    ).astype(jnp.bfloat16)
    size = table_ref.shape[0]
    group = chans // subs
    for sub in range(subs):
        out_ref[:, sub * group : (sub + 1) * group] = value[sub * size : (sub + 1) * size].reshape(
            2, group, total, RADIX * LANES
        )


def image(x, slot, chunk, count, rows_dev, held):
    z, pieces, _, _, rows, _ = x.shape
    chans = rows // rows_dev
    total = z * rows_dev
    spread = pieces // RADIX
    wide = RADIX * LANES
    group = min(chans, max(1, 256 // (2 * total)))
    table = row_table(rows_dev, z, group)
    order = order_table()
    scale = 1.0 / math.sqrt(total * count * spread * wide)
    block = group * math.gcd(chans // group, 2)
    return pl.pallas_call(
        functools.partial(image_kernel, scale),
        grid=(chans // block, spread),
        in_specs=[
            pl.BlockSpec(
                (z, RADIX, 1, 2, block * rows_dev, LANES), lambda c, g: (0, g, slot, 0, c, 0)
            ),
            pl.BlockSpec(table.shape, lambda c, g: (0, 0)),
            pl.BlockSpec(order.shape, lambda c, g: (0, 0)),
        ]
        + [pl.BlockSpec(memory_space=pl.ANY)] * len(held),
        out_specs=pl.BlockSpec(
            (2, block, total, wide), lambda c, g: (0, c, 0, chunk * spread + g)
        ),
        out_shape=jax.ShapeDtypeStruct((2, chans, total, count * spread * wide), jnp.bfloat16),
        input_output_aliases={3: 0} if held else {},
        compiler_params=params(),
        cost_estimate=pl.CostEstimate(
            flops=4 * pieces * chans * total * LANES * wide,
            bytes_accessed=8 * pieces * chans * total * LANES,
            transcendentals=0,
        ),
        name="image",
    )(x, jnp.asarray(table), jnp.asarray(order), *held)


def row_kernel(scale, group, steps, at_ref, *refs):
    x_refs, table_ref, stage = refs[:steps], refs[steps], refs[-1]
    out_refs = refs[steps + 1 : -1]
    targets, _, chans, total, _ = stage.shape
    tall = x_refs[0].shape[3] // chans * group
    for target in range(targets):
        for c in range(chans // group):
            rows = slice(c * tall, (c + 1) * tall)
            tile = jnp.concatenate(
                [x_ref[target, 0, s, rows, :] for x_ref in x_refs for s in range(2)], axis=0
            )
            value = jnp.dot(table_ref[...], tile, preferred_element_type=jnp.float32) * scale
            stage[target, :, c * group : (c + 1) * group] = value.reshape(
                2, group, total, LANES
            ).astype(jnp.bfloat16)
    for step, out_ref in enumerate(out_refs):
        out_ref[...] = stage[partner(at_ref[0], step, targets)]


def row_transform(parts, at, chans, rows_dev, length):
    steps = len(parts)
    targets = parts[0].shape[0]
    total = steps * rows_dev
    group = min(chans, max(1, 256 // (2 * total)))
    tables = jnp.asarray(row_tables(rows_dev, steps, group))
    table = lax.dynamic_index_in_dim(tables, at[1], 0, keepdims=False)
    vmem = pl.BlockSpec(memory_space=pltpu.VMEM)
    return pl.pallas_call(
        functools.partial(row_kernel, 1.0 / math.sqrt(total * length), group, steps),
        in_specs=[pl.BlockSpec(memory_space=pltpu.SMEM)] + [vmem] * (steps + 1),
        out_specs=[vmem] * targets,
        out_shape=[jax.ShapeDtypeStruct((2, chans, total, LANES), jnp.bfloat16)] * targets,
        scratch_shapes=[pltpu.VMEM((targets, 2, chans, total, LANES), jnp.bfloat16)],
        compiler_params=params(),
        name="row_transform",
    )(at, *parts, table)


def place_kernel(count, at_ref, *refs):
    x_refs, order_ref, out_ref, stage = refs[:count], refs[count], refs[-2], refs[-1]
    for step, x_ref in enumerate(x_refs):
        stage[partner(at_ref[0], step, count)] = x_ref[...].reshape(stage.shape[1:])
    tile = jnp.concatenate([stage[y_lo] for y_lo in range(count)], axis=1)
    value = jnp.dot(tile, order_ref[...], preferred_element_type=jnp.float32)
    out_ref[...] = value.astype(jnp.bfloat16).reshape(out_ref.shape)


def place(xs, at, chunk, count, held):
    _, chans, total, _ = xs[0].shape
    order = order_table()
    wide = RADIX * LANES
    block = math.gcd(chans, 4)
    return pl.pallas_call(
        functools.partial(place_kernel, len(xs)),
        grid=(chans // block,),
        in_specs=[pl.BlockSpec(memory_space=pltpu.SMEM)]
        + [pl.BlockSpec((2, block, total, LANES), lambda c: (0, c, 0, 0))] * len(xs)
        + [pl.BlockSpec(order.shape, lambda c: (0, 0))]
        + [pl.BlockSpec(memory_space=pl.ANY)] * len(held),
        out_specs=pl.BlockSpec((2, block, total, wide), lambda c: (0, c, 0, chunk)),
        out_shape=jax.ShapeDtypeStruct((2, chans, total, count * wide), jnp.bfloat16),
        scratch_shapes=[pltpu.VMEM((len(xs), 2 * block * total, LANES), jnp.bfloat16)],
        input_output_aliases={2 + len(xs): 0} if held else {},
        compiler_params=params(),
        name="place",
    )(at, *xs, jnp.asarray(order), *held)


def hold_kernel(*refs):
    pass


def hold(x, after):
    untouched = pl.BlockSpec(memory_space=pl.ANY)
    return pl.pallas_call(
        hold_kernel,
        in_specs=[untouched] * (1 + len(after)),
        out_specs=untouched,
        out_shape=jax.ShapeDtypeStruct(x.shape, x.dtype),
        input_output_aliases={0: 0},
        name="hold",
    )(x, *after)


def spread_rows(parts):
    count = len(parts)
    out = list(parts)
    for step in sorted(range(1, count), key=lambda n: -min(n, count - n)):
        out[step] = lax.ppermute(parts[step], "uv", [(z, (z + step) % count) for z in range(count)])
    return out


def turn_kernel(basis_ref, out_ref):
    out_ref[...] = basis_ref[...].T


def turn(basis):
    vmem = pl.BlockSpec(memory_space=pltpu.VMEM)
    return pl.pallas_call(
        turn_kernel,
        in_specs=[vmem],
        out_specs=vmem,
        out_shape=jax.ShapeDtypeStruct(basis.shape[::-1], basis.dtype),
        compiler_params=params(),
        name="turn",
    )(basis)


def exchange(x, axes):
    return lax.all_to_all(x, axes, split_axis=0, concat_axis=0, tiled=True)


def scatter(pieces):
    count = len(pieces)
    return [pieces[0]] + [
        lax.ppermute(
            pieces[step], "chan", [(j, int(partner(np.int32(j), step, count))) for j in range(count)]
        )
        for step in range(1, count)
    ]


def shards(visibility, eigen_basis, eigenvalues, noise_power):
    uv_count = lax.axis_size("uv")
    chan_count = lax.axis_size("chan")
    _, chans, rows_dev, length = visibility.shape
    count = length // chan_count // LANES
    targets = uv_count * chan_count
    at = jnp.stack([lax.axis_index("chan"), lax.axis_index("uv")]).astype(jnp.int32)
    basis = exchange(jnp.broadcast_to(eigen_basis, (chan_count,) + eigen_basis.shape), "chan")
    basis = basis.reshape(chan_count * chans, -1)
    basis_t = turn(basis)
    gain = eigenvalues[:, None] / (eigenvalues[:, None] + noise_power[None, :])
    flat = visibility.reshape(2, chans * rows_dev, length)
    rows_first = count > 3 and chan_count == RADIX
    whole = 3 if rows_first else 2
    first = column_transform(flat, at, chan_count, [(0, False)])
    cells = [[exchange(first[0], "chan")]]
    sends = []
    if count > 1:
        sends = list(
            column_transform(flat, at, chan_count, [(k, k >= whole) for k in range(1, count)])
        )
        sends[0] = hold(sends[0], [basis_t])
        cells.append([exchange(sends[0], "chan")])

    def cleaned_chunk(k, slot, slots, before, steps=1):
        return clean(
            at, cells[k], basis, basis_t, gain, targets, rows_dev, slot, slots, before, steps
        )

    before, lines = sends[:1], []
    groups = [[0]] + [g for g in (list(range(1, count - 1)), [count - 1]) if g and count > 1]
    if rows_first:
        groups = groups[1:]
        parts = spread_rows(cleaned_chunk(0, 0, 1, before, uv_count))
        before = []
        cells.append([exchange(hold(sends[1], [parts[uv_count // 2]]), "chan")])
        sends = sends[1:]
        lines = scatter(row_transform(parts, at, chans // uv_count, rows_dev, length))
    sends = sends[1:]
    for k in range(len(cells), count):
        cells.append(scatter(sends[:chan_count]))
        sends = sends[chan_count:]
    held = []
    for chunks in groups:
        if lines and chunks[-1] == count - 1:
            held = [place(lines, at, 0, count, held)]
        for slot, k in enumerate(chunks):
            if rows_first and k == 2:
                before = before + parts[1:]
            if rows_first and k == count - 1:
                before = before + lines[1:4]
            (cleaned,) = cleaned_chunk(k, slot, len(chunks), before)
            before = [cleaned]
        planes = exchange(cleaned, ("uv", "chan"))
        planes = planes.reshape((uv_count, chan_count) + planes.shape[1:])
        for slot, k in enumerate(chunks):
            held = [image(planes, slot, k, count, rows_dev, held)]
    return held[0]


def solution(mesh):
    in_specs = (P(None, "chan", "uv", None), P("chan", None), P(), P("uv"))
    out_specs = P(None, ("uv", "chan"), None, None)
    return jax.shard_map(shards, mesh=mesh, in_specs=in_specs, out_specs=out_specs, check_vma=False)
```

```python
import functools
import math

import jax
import jax.numpy as jnp
import numpy as np
from jax import lax
from jax.experimental import pallas as pl
from jax.experimental.pallas import tpu as pltpu
from jax.sharding import PartitionSpec as P

LANES = 128
RADIX = 8
VMEM_BYTES = 40 * 1024 * 1024


def params():
    return pltpu.CompilerParams(vmem_limit_bytes=VMEM_BYTES)


def inner_table(size):
    position = np.arange(size)
    phase = 2.0 * np.pi * (np.outer(position, position) % size) / size
    cosine, sine = np.cos(phase), np.sin(phase)
    return np.block([[cosine, sine], [-sine, cosine]]).astype(jnp.bfloat16)


def twiddle_table(length):
    inner = length // RADIX
    phase = 2.0 * np.pi * np.outer(np.arange(RADIX), np.arange(inner)) / length
    return np.stack([np.cos(phase), np.sin(phase)], axis=1).astype(np.float32)


def order_table():
    table = np.zeros((RADIX, LANES, LANES, RADIX), np.float32)
    for y_lo in range(RADIX):
        for y_hi in range(LANES):
            table[y_lo, y_hi, y_hi, y_lo] = 1.0
    return table.reshape(RADIX * LANES, RADIX * LANES).astype(jnp.bfloat16)


def swap_table(major, minor):
    table = np.zeros((major * minor, major * minor), np.float32)
    for a in range(major):
        for b in range(minor):
            table[b * major + a, a * minor + b] = 1.0
    return table.astype(jnp.bfloat16)


def row_table(rows_dev, uv_count, group):
    total = rows_dev * uv_count
    position = np.arange(total)
    phase = 2.0 * np.pi * (np.outer(position, position) % total) / total
    cosine, sine = np.cos(phase), np.sin(phase)
    parts = np.array([[cosine, -sine], [sine, cosine]])
    parts = parts.reshape(2, 2, total, uv_count, rows_dev)
    size = 2 * group * total
    table = np.einsum("tsxzu,cd->tcxzsdu", parts, np.eye(group))
    return table.reshape(size, size).astype(jnp.bfloat16)


def row_tables(rows_dev, uv_count, group):
    total = rows_dev * uv_count
    position = np.arange(total)
    phase = 2.0 * np.pi * (np.outer(position, position) % total) / total
    cosine, sine = np.cos(phase), np.sin(phase)
    parts = np.array([[cosine, -sine], [sine, cosine]])
    parts = parts.reshape(2, 2, total, uv_count, rows_dev)
    eye = np.eye(group)
    size = 2 * group * total
    tables = []
    for at in range(uv_count):
        order = (at - np.arange(uv_count)) % uv_count
        table = np.einsum("tsxzu,cd->tcxzsdu", parts[:, :, :, order], eye)
        tables.append(table.reshape(size, size).astype(jnp.bfloat16))
    return np.stack(tables)


def butterfly8(re, im):
    def dft2(ar, ai, br, bi):
        return ar + br, ai + bi, ar - br, ai - bi

    def dft4(r, i):
        s0r, s0i, d0r, d0i = dft2(r[0], i[0], r[2], i[2])
        s1r, s1i, d1r, d1i = dft2(r[1], i[1], r[3], i[3])
        return (
            [s0r + s1r, d0r - d1i, s0r - s1r, d0r + d1i],
            [s0i + s1i, d0i + d1r, s0i - s1i, d0i - d1r],
        )

    er, ei = dft4(re[0::2], im[0::2])
    orr, oi = dft4(re[1::2], im[1::2])
    half = math.sqrt(0.5)
    turned_r = [orr[0], (orr[1] - oi[1]) * half, -oi[2], (-orr[3] - oi[3]) * half]
    turned_i = [oi[0], (orr[1] + oi[1]) * half, orr[2], (orr[3] - oi[3]) * half]
    out_r = [er[k] + turned_r[k] for k in range(4)] + [er[k] - turned_r[k] for k in range(4)]
    out_i = [ei[k] + turned_i[k] for k in range(4)] + [ei[k] - turned_i[k] for k in range(4)]
    return out_r, out_i


def column_kernel(chunks, spread, at_ref, x_ref, twiddle_ref, table_ref, *refs):
    *out_refs, mid, stage = refs
    pieces = spread * RADIX
    rows, length = x_ref.shape[1:]
    inner = length // RADIX
    step = 16
    for i in range(rows // step):
        at = slice(i * step, (i + 1) * step)
        for block in range(inner // LANES):
            re, im = [], []
            for a in range(RADIX):
                lanes = slice(a * inner + block * LANES, a * inner + (block + 1) * LANES)
                re.append(x_ref[0, at, lanes].astype(jnp.float32))
                im.append(x_ref[1, at, lanes].astype(jnp.float32))
            re, im = butterfly8(re, im)
            lanes = slice(block * LANES, (block + 1) * LANES)
            other = slice(inner + block * LANES, inner + (block + 1) * LANES)
            for y_lo in range(RADIX):
                if y_lo == 0:
                    tr, ti = re[0], im[0]
                else:
                    cosine = twiddle_ref[y_lo, 0:1, lanes]
                    sine = twiddle_ref[y_lo, 1:2, lanes]
                    tr = re[y_lo] * cosine - im[y_lo] * sine
                    ti = re[y_lo] * sine + im[y_lo] * cosine
                mid[y_lo, at, lanes] = tr.astype(jnp.bfloat16)
                mid[y_lo, at, other] = ti.astype(jnp.bfloat16)
    for chunk, split in chunks:
        outs = out_refs[: pieces if split else 1]
        out_refs = out_refs[len(outs) :]
        for group in range(spread):
            column = (chunk * spread + group) * LANES
            table = jnp.concatenate(
                [table_ref[:, at : at + LANES] for at in (column, inner + column)], axis=1
            )
            wide = jnp.dot(
                mid[...].reshape(RADIX * rows, 2 * inner), table, preferred_element_type=jnp.float32
            ).astype(jnp.bfloat16)
            for y_lo in range(RADIX):
                for part in range(2):
                    value = wide[y_lo * rows : (y_lo + 1) * rows, part * LANES : (part + 1) * LANES]
                    if split:
                        stage[group * RADIX + y_lo, part] = value
                    else:
                        outs[0][group * RADIX + y_lo, part] = value
        if split:
            for step, out_ref in enumerate(outs):
                out_ref[...] = stage[partner(at_ref[0], step, pieces)]


def partner(at, step, count):
    if count & (count - 1):
        return (count - at + step) % count
    if step:
        step = sorted(range(1, count), key=lambda n: (-bin(n // 2).count("1"), -n))[step - 1]
    return at ^ step


def column_transform(x, at, pieces, chunks):
    _, rows, length = x.shape
    inner = length // RADIX
    block = math.gcd(rows, 128)
    specs, shapes = [], []
    for _, split in chunks:
        if split:
            specs += [pl.BlockSpec((2, block, LANES), lambda i, at: (0, i, 0))] * pieces
            shapes += [jax.ShapeDtypeStruct((2, rows, LANES), jnp.bfloat16)] * pieces
        else:
            specs.append(pl.BlockSpec((pieces, 2, block, LANES), lambda i, at: (0, 0, i, 0)))
            shapes.append(jax.ShapeDtypeStruct((pieces, 2, rows, LANES), jnp.bfloat16))
    return pl.pallas_call(
        functools.partial(column_kernel, chunks, pieces // RADIX),
        grid_spec=pltpu.PrefetchScalarGridSpec(
            num_scalar_prefetch=1,
            grid=(rows // block,),
            in_specs=[
                pl.BlockSpec((2, block, length), lambda i, at: (0, i, 0)),
                pl.BlockSpec((RADIX, 2, inner), lambda i, at: (0, 0, 0)),
                pl.BlockSpec((2 * inner, 2 * inner), lambda i, at: (0, 0)),
            ],
            out_specs=specs,
            scratch_shapes=[
                pltpu.VMEM((RADIX, block, 2 * inner), jnp.bfloat16),
                pltpu.VMEM((pieces, 2, block, LANES), jnp.bfloat16),
            ],
        ),
        out_shape=shapes,
        compiler_params=params(),
        cost_estimate=pl.CostEstimate(
            flops=4 * rows * length * LANES * pieces * len(chunks),
            bytes_accessed=8 * rows * length,
            transcendentals=0,
        ),
        name="column_transform",
    )(at, x, jnp.asarray(twiddle_table(length)), jnp.asarray(inner_table(inner)))


def clean_kernel(split, waits, steps, at_ref, *refs):
    refs, out_refs, slab = refs[: -1 - steps], refs[-1 - steps : -1], refs[-1]
    *x_refs, basis_ref, basis_t_ref, gain_ref, swap_ref, back_ref = refs[: len(refs) - waits]
    chans = slab.shape[0]
    pair = 2 * LANES
    rows_dev = slab.shape[1] // pair
    tall = swap_ref.shape[0]
    group = tall // rows_dev
    sources = len(x_refs) if split else x_refs[0].shape[0]
    own = chans // sources
    for source in range(sources):
        block = x_refs[source] if split else x_refs[0].at[source]
        begin = partner(at_ref[0], source, sources) * own if split else source * own
        for k in range(own // group):
            rows = slice(k * tall, (k + 1) * tall)
            turned = jnp.dot(
                swap_ref[...],
                jnp.concatenate([block[0, rows, :], block[1, rows, :]], axis=1),
                preferred_element_type=jnp.float32,
            ).astype(jnp.bfloat16)
            channels = pl.ds(pl.multiple_of(begin + k * group, group), group)
            for u in range(rows_dev):
                slab[channels, u * pair : (u + 1) * pair] = turned[u * group : (u + 1) * group]
    for u in range(rows_dev):
        lanes = slice(u * pair, (u + 1) * pair)
        line = slab[:, lanes]
        amps = jnp.dot(basis_t_ref[...], line, preferred_element_type=jnp.float32)
        amps = amps.astype(jnp.bfloat16).astype(jnp.float32)
        front = (gain_ref[:, u : u + 1] * amps).astype(jnp.bfloat16)
        drop = jnp.dot(basis_ref[...], front, preferred_element_type=jnp.float32)
        slab[:, lanes] = (line.astype(jnp.float32) - drop).astype(jnp.bfloat16)
    out_rows = out_refs[0].shape[3]
    tall = back_ref.shape[0]
    group = tall // rows_dev
    share = chans // steps
    for step, out_ref in enumerate(out_refs):
        start = lax.rem(at_ref[1] + step, steps) * share if steps > 1 else 0
        for b in range(share // group):
            channels = pl.ds(pl.multiple_of(start + b * group, group), group)
            tile = jnp.concatenate(
                [slab[channels, u * pair : (u + 1) * pair] for u in range(rows_dev)], axis=0
            )
            value = jnp.dot(back_ref[...], tile, preferred_element_type=jnp.float32)
            for part in range(2):
                half = value[:, part * LANES : (part + 1) * LANES]
                if out_rows % tall == 0:
                    target, row = divmod(b * tall, out_rows)
                    out_ref[target, 0, part, row : row + tall, :] = half.astype(jnp.bfloat16)
                else:
                    take = tall // out_rows
                    out_ref[b * take : (b + 1) * take, 0, part] = half.reshape(
                        take, out_rows, LANES
                    ).astype(jnp.bfloat16)


def clean(at, xs, basis, basis_t, gain, targets, rows_dev, slot, slots, before, steps=1):
    split = len(xs) > 1
    chans = basis.shape[0]
    sources = len(xs) if split else xs[0].shape[0]
    own = chans // sources
    swap = swap_table(min(256 // rows_dev, own), rows_dev)
    back = np.ascontiguousarray(swap_table(256 // rows_dev, rows_dev).T)
    vmem = pl.BlockSpec(memory_space=pltpu.VMEM)
    out_rows = chans * rows_dev // targets
    return pl.pallas_call(
        functools.partial(clean_kernel, split, len(before), steps),
        grid=(1,),
        in_specs=[pl.BlockSpec(memory_space=pltpu.SMEM)]
        + [vmem] * (len(xs) + 5)
        + [pl.BlockSpec(memory_space=pl.ANY)] * len(before),
        out_specs=[
            pl.BlockSpec((targets // steps, 1, 2, out_rows, LANES), lambda i: (0, slot, 0, 0, 0))
        ]
        * steps,
        out_shape=[
            jax.ShapeDtypeStruct((targets // steps, slots, 2, out_rows, LANES), jnp.bfloat16)
        ]
        * steps,
        input_output_aliases={6 + len(xs): 0} if slot else {},
        scratch_shapes=[pltpu.VMEM((chans, rows_dev * 2 * LANES), jnp.bfloat16)],
        compiler_params=params(),
        cost_estimate=pl.CostEstimate(
            flops=12 * chans * chans * rows_dev * LANES,
            bytes_accessed=8 * chans * rows_dev * LANES,
            transcendentals=0,
        ),
        name="clean",
    )(at, *xs, basis, basis_t, gain, jnp.asarray(swap), jnp.asarray(back), *before)


def image_kernel(scale, x_ref, table_ref, order_ref, *refs):
    out_ref = refs[-1]
    z, _, _, parts, rows, _ = x_ref.shape
    _, chans, total, _ = out_ref.shape
    subs = 2 * chans * total // table_ref.shape[0]
    own = rows // subs
    values = []
    for sub in range(subs):
        tiles = []
        for y_lo in range(RADIX):
            tile = x_ref[:, y_lo, 0, :, sub * own : (sub + 1) * own, :]
            if own % 16:
                tile = tile.astype(jnp.float32)
            tiles.append(tile.reshape(z * parts * own, LANES).astype(jnp.bfloat16))
        tile = jnp.concatenate(tiles, axis=1)
        value = jnp.dot(table_ref[...], tile, preferred_element_type=jnp.float32)
        values.append((value * scale).astype(jnp.bfloat16))
    value = jnp.dot(
        jnp.concatenate(values, axis=0), order_ref[...], preferred_element_type=jnp.float32
    ).astype(jnp.bfloat16)
    size = table_ref.shape[0]
    group = chans // subs
    for sub in range(subs):
        out_ref[:, sub * group : (sub + 1) * group] = value[sub * size : (sub + 1) * size].reshape(
            2, group, total, RADIX * LANES
        )


def image(x, slot, chunk, count, rows_dev, held):
    z, pieces, _, _, rows, _ = x.shape
    chans = rows // rows_dev
    total = z * rows_dev
    spread = pieces // RADIX
    wide = RADIX * LANES
    group = min(chans, max(1, 256 // (2 * total)))
    table = row_table(rows_dev, z, group)
    order = order_table()
    scale = 1.0 / math.sqrt(total * count * spread * wide)
    block = group * math.gcd(chans // group, 2)
    return pl.pallas_call(
        functools.partial(image_kernel, scale),
        grid=(chans // block, spread),
        in_specs=[
            pl.BlockSpec(
                (z, RADIX, 1, 2, block * rows_dev, LANES), lambda c, g: (0, g, slot, 0, c, 0)
            ),
            pl.BlockSpec(table.shape, lambda c, g: (0, 0)),
            pl.BlockSpec(order.shape, lambda c, g: (0, 0)),
        ]
        + [pl.BlockSpec(memory_space=pl.ANY)] * len(held),
        out_specs=pl.BlockSpec(
            (2, block, total, wide), lambda c, g: (0, c, 0, chunk * spread + g)
        ),
        out_shape=jax.ShapeDtypeStruct((2, chans, total, count * spread * wide), jnp.bfloat16),
        input_output_aliases={3: 0} if held else {},
        compiler_params=params(),
        cost_estimate=pl.CostEstimate(
            flops=4 * pieces * chans * total * LANES * wide,
            bytes_accessed=8 * pieces * chans * total * LANES,
            transcendentals=0,
        ),
        name="image",
    )(x, jnp.asarray(table), jnp.asarray(order), *held)


def row_kernel(scale, group, steps, at_ref, *refs):
    x_refs, table_ref, stage = refs[:steps], refs[steps], refs[-1]
    out_refs = refs[steps + 1 : -1]
    targets, _, chans, total, _ = stage.shape
    tall = x_refs[0].shape[3] // chans * group
    for target in range(targets):
        for c in range(chans // group):
            rows = slice(c * tall, (c + 1) * tall)
            tile = jnp.concatenate(
                [x_ref[target, 0, s, rows, :] for x_ref in x_refs for s in range(2)], axis=0
            )
            value = jnp.dot(table_ref[...], tile, preferred_element_type=jnp.float32) * scale
            stage[target, :, c * group : (c + 1) * group] = value.reshape(
                2, group, total, LANES
            ).astype(jnp.bfloat16)
    for step, out_ref in enumerate(out_refs):
        out_ref[...] = stage[partner(at_ref[0], step, targets)]


def row_transform(parts, at, chans, rows_dev, length):
    steps = len(parts)
    targets = parts[0].shape[0]
    total = steps * rows_dev
    group = min(chans, max(1, 256 // (2 * total)))
    tables = jnp.asarray(row_tables(rows_dev, steps, group))
    table = lax.dynamic_index_in_dim(tables, at[1], 0, keepdims=False)
    vmem = pl.BlockSpec(memory_space=pltpu.VMEM)
    return pl.pallas_call(
        functools.partial(row_kernel, 1.0 / math.sqrt(total * length), group, steps),
        in_specs=[pl.BlockSpec(memory_space=pltpu.SMEM)] + [vmem] * (steps + 1),
        out_specs=[vmem] * targets,
        out_shape=[jax.ShapeDtypeStruct((2, chans, total, LANES), jnp.bfloat16)] * targets,
        scratch_shapes=[pltpu.VMEM((targets, 2, chans, total, LANES), jnp.bfloat16)],
        compiler_params=params(),
        name="row_transform",
    )(at, *parts, table)


def place_kernel(count, at_ref, *refs):
    x_refs, order_ref, out_ref, stage = refs[:count], refs[count], refs[-2], refs[-1]
    for step, x_ref in enumerate(x_refs):
        stage[partner(at_ref[0], step, count)] = x_ref[...].reshape(stage.shape[1:])
    tile = jnp.concatenate([stage[y_lo] for y_lo in range(count)], axis=1)
    value = jnp.dot(tile, order_ref[...], preferred_element_type=jnp.float32)
    out_ref[...] = value.astype(jnp.bfloat16).reshape(out_ref.shape)


def place(xs, at, chunk, count, held):
    _, chans, total, _ = xs[0].shape
    order = order_table()
    wide = RADIX * LANES
    block = math.gcd(chans, 4)
    return pl.pallas_call(
        functools.partial(place_kernel, len(xs)),
        grid=(chans // block,),
        in_specs=[pl.BlockSpec(memory_space=pltpu.SMEM)]
        + [pl.BlockSpec((2, block, total, LANES), lambda c: (0, c, 0, 0))] * len(xs)
        + [pl.BlockSpec(order.shape, lambda c: (0, 0))]
        + [pl.BlockSpec(memory_space=pl.ANY)] * len(held),
        out_specs=pl.BlockSpec((2, block, total, wide), lambda c: (0, c, 0, chunk)),
        out_shape=jax.ShapeDtypeStruct((2, chans, total, count * wide), jnp.bfloat16),
        scratch_shapes=[pltpu.VMEM((len(xs), 2 * block * total, LANES), jnp.bfloat16)],
        input_output_aliases={2 + len(xs): 0} if held else {},
        compiler_params=params(),
        name="place",
    )(at, *xs, jnp.asarray(order), *held)


def hold_kernel(*refs):
    pass


def hold(x, after):
    untouched = pl.BlockSpec(memory_space=pl.ANY)
    return pl.pallas_call(
        hold_kernel,
        in_specs=[untouched] * (1 + len(after)),
        out_specs=untouched,
        out_shape=jax.ShapeDtypeStruct(x.shape, x.dtype),
        input_output_aliases={0: 0},
        name="hold",
    )(x, *after)


def spread_rows(parts):
    count = len(parts)
    out = list(parts)
    for step in sorted(range(1, count), key=lambda n: -min(n, count - n)):
        out[step] = lax.ppermute(parts[step], "uv", [(z, (z + step) % count) for z in range(count)])
    return out


def turn_kernel(basis_ref, out_ref):
    out_ref[...] = basis_ref[...].T


def turn(basis):
    vmem = pl.BlockSpec(memory_space=pltpu.VMEM)
    return pl.pallas_call(
        turn_kernel,
        in_specs=[vmem],
        out_specs=vmem,
        out_shape=jax.ShapeDtypeStruct(basis.shape[::-1], basis.dtype),
        compiler_params=params(),
        name="turn",
    )(basis)


def exchange(x, axes):
    return lax.all_to_all(x, axes, split_axis=0, concat_axis=0, tiled=True)


def scatter(pieces):
    count = len(pieces)
    return [pieces[0]] + [
        lax.ppermute(
            pieces[step], "chan", [(j, int(partner(np.int32(j), step, count))) for j in range(count)]
        )
        for step in range(1, count)
    ]


def shards(visibility, eigen_basis, eigenvalues, noise_power):
    uv_count = lax.axis_size("uv")
    chan_count = lax.axis_size("chan")
    _, chans, rows_dev, length = visibility.shape
    count = length // chan_count // LANES
    targets = uv_count * chan_count
    at = jnp.stack([lax.axis_index("chan"), lax.axis_index("uv")]).astype(jnp.int32)
    basis = exchange(jnp.broadcast_to(eigen_basis, (chan_count,) + eigen_basis.shape), "chan")
    basis = basis.reshape(chan_count * chans, -1)
    basis_t = turn(basis)
    gain = eigenvalues[:, None] / (eigenvalues[:, None] + noise_power[None, :])
    flat = visibility.reshape(2, chans * rows_dev, length)
    rows_first = count > 3 and chan_count == RADIX
    whole = 3 if rows_first else 2
    first = column_transform(flat, at, chan_count, [(0, False)])
    cells = [[exchange(first[0], "chan")]]
    sends = []
    if count > 1:
        sends = list(
            column_transform(flat, at, chan_count, [(k, k >= whole) for k in range(1, count)])
        )
        sends[0] = hold(sends[0], [basis_t])
        cells.append([exchange(sends[0], "chan")])

    def cleaned_chunk(k, slot, slots, before, steps=1):
        return clean(
            at, cells[k], basis, basis_t, gain, targets, rows_dev, slot, slots, before, steps
        )

    before, lines = sends[:1], []
    groups = [[0]] + [g for g in (list(range(1, count - 1)), [count - 1]) if g and count > 1]
    if rows_first:
        groups = groups[1:]
        parts = spread_rows(cleaned_chunk(0, 0, 1, before, uv_count))
        before = []
        cells.append([exchange(hold(sends[1], [parts[uv_count // 2]]), "chan")])
        sends = sends[1:]
        lines = scatter(row_transform(parts, at, chans // uv_count, rows_dev, length))
    sends = sends[1:]
    for k in range(len(cells), count):
        cells.append(scatter(sends[:chan_count]))
        sends = sends[chan_count:]
    held = []
    for chunks in groups:
        if lines and chunks[-1] == count - 1:
            held = [place(lines, at, 0, count, held)]
        for slot, k in enumerate(chunks):
            if rows_first and k == 2:
                before = before + parts[1:]
            if rows_first and k == count - 1:
                before = before + lines[1:3]
            (cleaned,) = cleaned_chunk(k, slot, len(chunks), before)
            before = [cleaned]
        planes = exchange(cleaned, ("uv", "chan"))
        planes = planes.reshape((uv_count, chan_count) + planes.shape[1:])
        for slot, k in enumerate(chunks):
            held = [image(planes, slot, k, count, rows_dev, held)]
    return held[0]


def solution(mesh):
    in_specs = (P(None, "chan", "uv", None), P("chan", None), P(), P("uv"))
    out_specs = P(None, ("uv", "chan"), None, None)
    return jax.shard_map(shards, mesh=mesh, in_specs=in_specs, out_specs=out_specs, check_vma=False)
```

```python
import functools
import math

import jax
import jax.numpy as jnp
import numpy as np
from jax import lax
from jax.experimental import pallas as pl
from jax.experimental.pallas import tpu as pltpu
from jax.sharding import PartitionSpec as P

LANES = 128
RADIX = 8
VMEM_BYTES = 56 * 1024 * 1024


def params():
    return pltpu.CompilerParams(vmem_limit_bytes=VMEM_BYTES)


def inner_table(size):
    position = np.arange(size)
    phase = 2.0 * np.pi * (np.outer(position, position) % size) / size
    cosine, sine = np.cos(phase), np.sin(phase)
    return np.block([[cosine, sine], [-sine, cosine]]).astype(jnp.bfloat16)


def twiddle_table(length):
    inner = length // RADIX
    phase = 2.0 * np.pi * np.outer(np.arange(RADIX), np.arange(inner)) / length
    return np.stack([np.cos(phase), np.sin(phase)], axis=1).astype(np.float32)


def order_table():
    table = np.zeros((RADIX, LANES, LANES, RADIX), np.float32)
    for y_lo in range(RADIX):
        for y_hi in range(LANES):
            table[y_lo, y_hi, y_hi, y_lo] = 1.0
    return table.reshape(RADIX * LANES, RADIX * LANES).astype(jnp.bfloat16)


def swap_table(major, minor):
    table = np.zeros((major * minor, major * minor), np.float32)
    for a in range(major):
        for b in range(minor):
            table[b * major + a, a * minor + b] = 1.0
    return table.astype(jnp.bfloat16)


def row_table(rows_dev, uv_count, group):
    total = rows_dev * uv_count
    position = np.arange(total)
    phase = 2.0 * np.pi * (np.outer(position, position) % total) / total
    cosine, sine = np.cos(phase), np.sin(phase)
    parts = np.array([[cosine, -sine], [sine, cosine]])
    parts = parts.reshape(2, 2, total, uv_count, rows_dev)
    size = 2 * group * total
    table = np.einsum("tsxzu,cd->tcxzsdu", parts, np.eye(group))
    return table.reshape(size, size).astype(jnp.bfloat16)


def row_tables(rows_dev, uv_count, group):
    total = rows_dev * uv_count
    position = np.arange(total)
    phase = 2.0 * np.pi * (np.outer(position, position) % total) / total
    cosine, sine = np.cos(phase), np.sin(phase)
    parts = np.array([[cosine, -sine], [sine, cosine]])
    parts = parts.reshape(2, 2, total, uv_count, rows_dev)
    eye = np.eye(group)
    size = 2 * group * total
    tables = []
    for at in range(uv_count):
        order = (at - np.arange(uv_count)) % uv_count
        table = np.einsum("tsxzu,cd->tcxzsdu", parts[:, :, :, order], eye)
        tables.append(table.reshape(size, size).astype(jnp.bfloat16))
    return np.stack(tables)


def butterfly8(re, im):
    def dft2(ar, ai, br, bi):
        return ar + br, ai + bi, ar - br, ai - bi

    def dft4(r, i):
        s0r, s0i, d0r, d0i = dft2(r[0], i[0], r[2], i[2])
        s1r, s1i, d1r, d1i = dft2(r[1], i[1], r[3], i[3])
        return (
            [s0r + s1r, d0r - d1i, s0r - s1r, d0r + d1i],
            [s0i + s1i, d0i + d1r, s0i - s1i, d0i - d1r],
        )

    er, ei = dft4(re[0::2], im[0::2])
    orr, oi = dft4(re[1::2], im[1::2])
    half = math.sqrt(0.5)
    turned_r = [orr[0], (orr[1] - oi[1]) * half, -oi[2], (-orr[3] - oi[3]) * half]
    turned_i = [oi[0], (orr[1] + oi[1]) * half, orr[2], (orr[3] - oi[3]) * half]
    out_r = [er[k] + turned_r[k] for k in range(4)] + [er[k] - turned_r[k] for k in range(4)]
    out_i = [ei[k] + turned_i[k] for k in range(4)] + [ei[k] - turned_i[k] for k in range(4)]
    return out_r, out_i


def column_kernel(chunks, spread, at_ref, x_ref, twiddle_ref, table_ref, *refs):
    *out_refs, mid, stage = refs
    pieces = spread * RADIX
    rows, length = x_ref.shape[1:]
    inner = length // RADIX
    step = 16
    for i in range(rows // step):
        at = slice(i * step, (i + 1) * step)
        for block in range(inner // LANES):
            re, im = [], []
            for a in range(RADIX):
                lanes = slice(a * inner + block * LANES, a * inner + (block + 1) * LANES)
                re.append(x_ref[0, at, lanes].astype(jnp.float32))
                im.append(x_ref[1, at, lanes].astype(jnp.float32))
            re, im = butterfly8(re, im)
            lanes = slice(block * LANES, (block + 1) * LANES)
            other = slice(inner + block * LANES, inner + (block + 1) * LANES)
            for y_lo in range(RADIX):
                if y_lo == 0:
                    tr, ti = re[0], im[0]
                else:
                    cosine = twiddle_ref[y_lo, 0:1, lanes]
                    sine = twiddle_ref[y_lo, 1:2, lanes]
                    tr = re[y_lo] * cosine - im[y_lo] * sine
                    ti = re[y_lo] * sine + im[y_lo] * cosine
                mid[y_lo, at, lanes] = tr.astype(jnp.bfloat16)
                mid[y_lo, at, other] = ti.astype(jnp.bfloat16)
    for chunk, split in chunks:
        outs = out_refs[: pieces if split else 1]
        out_refs = out_refs[len(outs) :]
        for group in range(spread):
            column = (chunk * spread + group) * LANES
            table = jnp.concatenate(
                [table_ref[:, at : at + LANES] for at in (column, inner + column)], axis=1
            )
            wide = jnp.dot(
                mid[...].reshape(RADIX * rows, 2 * inner), table, preferred_element_type=jnp.float32
            ).astype(jnp.bfloat16)
            for y_lo in range(RADIX):
                for part in range(2):
                    value = wide[y_lo * rows : (y_lo + 1) * rows, part * LANES : (part + 1) * LANES]
                    if split:
                        stage[group * RADIX + y_lo, part] = value
                    else:
                        outs[0][group * RADIX + y_lo, part] = value
        if split:
            for step, out_ref in enumerate(outs):
                out_ref[...] = stage[partner(at_ref[0], step, pieces)]


def partner(at, step, count):
    if count & (count - 1):
        return (count - at + step) % count
    if step:
        step = sorted(range(1, count), key=lambda n: (-bin(n // 2).count("1"), -n))[step - 1]
    return at ^ step


def column_transform(x, at, pieces, chunks):
    _, rows, length = x.shape
    inner = length // RADIX
    block = math.gcd(rows, 128)
    specs, shapes = [], []
    for _, split in chunks:
        if split:
            specs += [pl.BlockSpec((2, block, LANES), lambda i, at: (0, i, 0))] * pieces
            shapes += [jax.ShapeDtypeStruct((2, rows, LANES), jnp.bfloat16)] * pieces
        else:
            specs.append(pl.BlockSpec((pieces, 2, block, LANES), lambda i, at: (0, 0, i, 0)))
            shapes.append(jax.ShapeDtypeStruct((pieces, 2, rows, LANES), jnp.bfloat16))
    return pl.pallas_call(
        functools.partial(column_kernel, chunks, pieces // RADIX),
        grid_spec=pltpu.PrefetchScalarGridSpec(
            num_scalar_prefetch=1,
            grid=(rows // block,),
            in_specs=[
                pl.BlockSpec((2, block, length), lambda i, at: (0, i, 0)),
                pl.BlockSpec((RADIX, 2, inner), lambda i, at: (0, 0, 0)),
                pl.BlockSpec((2 * inner, 2 * inner), lambda i, at: (0, 0)),
            ],
            out_specs=specs,
            scratch_shapes=[
                pltpu.VMEM((RADIX, block, 2 * inner), jnp.bfloat16),
                pltpu.VMEM((pieces, 2, block, LANES), jnp.bfloat16),
            ],
        ),
        out_shape=shapes,
        compiler_params=params(),
        cost_estimate=pl.CostEstimate(
            flops=4 * rows * length * LANES * pieces * len(chunks),
            bytes_accessed=8 * rows * length,
            transcendentals=0,
        ),
        name="column_transform",
    )(at, x, jnp.asarray(twiddle_table(length)), jnp.asarray(inner_table(inner)))


def clean_kernel(split, waits, steps, at_ref, *refs):
    refs, out_refs, slab = refs[: -1 - steps], refs[-1 - steps : -1], refs[-1]
    *x_refs, basis_ref, basis_t_ref, gain_ref, swap_ref, back_ref = refs[: len(refs) - waits]
    chans = slab.shape[0]
    pair = 2 * LANES
    rows_dev = slab.shape[1] // pair
    tall = swap_ref.shape[0]
    group = tall // rows_dev
    sources = len(x_refs) if split else x_refs[0].shape[0]
    own = chans // sources
    for source in range(sources):
        block = x_refs[source] if split else x_refs[0].at[source]
        begin = partner(at_ref[0], source, sources) * own if split else source * own
        for k in range(own // group):
            rows = slice(k * tall, (k + 1) * tall)
            turned = jnp.dot(
                swap_ref[...],
                jnp.concatenate([block[0, rows, :], block[1, rows, :]], axis=1),
                preferred_element_type=jnp.float32,
            ).astype(jnp.bfloat16)
            channels = pl.ds(pl.multiple_of(begin + k * group, group), group)
            for u in range(rows_dev):
                slab[channels, u * pair : (u + 1) * pair] = turned[u * group : (u + 1) * group]
    for u in range(rows_dev):
        lanes = slice(u * pair, (u + 1) * pair)
        line = slab[:, lanes]
        amps = jnp.dot(basis_t_ref[...], line, preferred_element_type=jnp.float32)
        amps = amps.astype(jnp.bfloat16).astype(jnp.float32)
        front = (gain_ref[:, u : u + 1] * amps).astype(jnp.bfloat16)
        drop = jnp.dot(basis_ref[...], front, preferred_element_type=jnp.float32)
        slab[:, lanes] = (line.astype(jnp.float32) - drop).astype(jnp.bfloat16)
    out_rows = out_refs[0].shape[3]
    tall = back_ref.shape[0]
    group = tall // rows_dev
    share = chans // steps
    for step, out_ref in enumerate(out_refs):
        start = lax.rem(at_ref[1] + step, steps) * share if steps > 1 else 0
        for b in range(share // group):
            channels = pl.ds(pl.multiple_of(start + b * group, group), group)
            tile = jnp.concatenate(
                [slab[channels, u * pair : (u + 1) * pair] for u in range(rows_dev)], axis=0
            )
            value = jnp.dot(back_ref[...], tile, preferred_element_type=jnp.float32)
            for part in range(2):
                half = value[:, part * LANES : (part + 1) * LANES]
                if out_rows % tall == 0:
                    target, row = divmod(b * tall, out_rows)
                    out_ref[target, 0, part, row : row + tall, :] = half.astype(jnp.bfloat16)
                else:
                    take = tall // out_rows
                    out_ref[b * take : (b + 1) * take, 0, part] = half.reshape(
                        take, out_rows, LANES
                    ).astype(jnp.bfloat16)


def clean(at, xs, basis, basis_t, gain, targets, rows_dev, slot, slots, before, steps=1):
    split = len(xs) > 1
    chans = basis.shape[0]
    sources = len(xs) if split else xs[0].shape[0]
    own = chans // sources
    swap = swap_table(min(256 // rows_dev, own), rows_dev)
    back = np.ascontiguousarray(swap_table(256 // rows_dev, rows_dev).T)
    vmem = pl.BlockSpec(memory_space=pltpu.VMEM)
    out_rows = chans * rows_dev // targets
    return pl.pallas_call(
        functools.partial(clean_kernel, split, len(before), steps),
        grid=(1,),
        in_specs=[pl.BlockSpec(memory_space=pltpu.SMEM)]
        + [vmem] * (len(xs) + 5)
        + [pl.BlockSpec(memory_space=pl.ANY)] * len(before),
        out_specs=[
            pl.BlockSpec((targets // steps, 1, 2, out_rows, LANES), lambda i: (0, slot, 0, 0, 0))
        ]
        * steps,
        out_shape=[
            jax.ShapeDtypeStruct((targets // steps, slots, 2, out_rows, LANES), jnp.bfloat16)
        ]
        * steps,
        input_output_aliases={6 + len(xs): 0} if slot else {},
        scratch_shapes=[pltpu.VMEM((chans, rows_dev * 2 * LANES), jnp.bfloat16)],
        compiler_params=params(),
        cost_estimate=pl.CostEstimate(
            flops=12 * chans * chans * rows_dev * LANES,
            bytes_accessed=8 * chans * rows_dev * LANES,
            transcendentals=0,
        ),
        name="clean",
    )(at, *xs, basis, basis_t, gain, jnp.asarray(swap), jnp.asarray(back), *before)


def image_kernel(scale, x_ref, table_ref, order_ref, *refs):
    out_ref = refs[-1]
    z, _, _, parts, rows, _ = x_ref.shape
    _, chans, total, _ = out_ref.shape
    subs = 2 * chans * total // table_ref.shape[0]
    own = rows // subs
    values = []
    for sub in range(subs):
        tiles = []
        for y_lo in range(RADIX):
            tile = x_ref[:, y_lo, 0, :, sub * own : (sub + 1) * own, :]
            if own % 16:
                tile = tile.astype(jnp.float32)
            tiles.append(tile.reshape(z * parts * own, LANES).astype(jnp.bfloat16))
        tile = jnp.concatenate(tiles, axis=1)
        value = jnp.dot(table_ref[...], tile, preferred_element_type=jnp.float32)
        values.append((value * scale).astype(jnp.bfloat16))
    value = jnp.dot(
        jnp.concatenate(values, axis=0), order_ref[...], preferred_element_type=jnp.float32
    ).astype(jnp.bfloat16)
    size = table_ref.shape[0]
    group = chans // subs
    for sub in range(subs):
        out_ref[:, sub * group : (sub + 1) * group] = value[sub * size : (sub + 1) * size].reshape(
            2, group, total, RADIX * LANES
        )


def image(x, slot, chunk, count, rows_dev, held):
    z, pieces, _, _, rows, _ = x.shape
    chans = rows // rows_dev
    total = z * rows_dev
    spread = pieces // RADIX
    wide = RADIX * LANES
    group = min(chans, max(1, 256 // (2 * total)))
    table = row_table(rows_dev, z, group)
    order = order_table()
    scale = 1.0 / math.sqrt(total * count * spread * wide)
    block = group * math.gcd(chans // group, 2)
    return pl.pallas_call(
        functools.partial(image_kernel, scale),
        grid=(chans // block, spread),
        in_specs=[
            pl.BlockSpec(
                (z, RADIX, 1, 2, block * rows_dev, LANES), lambda c, g: (0, g, slot, 0, c, 0)
            ),
            pl.BlockSpec(table.shape, lambda c, g: (0, 0)),
            pl.BlockSpec(order.shape, lambda c, g: (0, 0)),
        ]
        + [pl.BlockSpec(memory_space=pl.ANY)] * len(held),
        out_specs=pl.BlockSpec(
            (2, block, total, wide), lambda c, g: (0, c, 0, chunk * spread + g)
        ),
        out_shape=jax.ShapeDtypeStruct((2, chans, total, count * spread * wide), jnp.bfloat16),
        input_output_aliases={3: 0} if held else {},
        compiler_params=params(),
        cost_estimate=pl.CostEstimate(
            flops=4 * pieces * chans * total * LANES * wide,
            bytes_accessed=8 * pieces * chans * total * LANES,
            transcendentals=0,
        ),
        name="image",
    )(x, jnp.asarray(table), jnp.asarray(order), *held)


def row_kernel(scale, group, steps, at_ref, *refs):
    x_refs, table_ref, stage = refs[:steps], refs[steps], refs[-1]
    out_refs = refs[steps + 1 : -1]
    targets, _, chans, total, _ = stage.shape
    tall = x_refs[0].shape[3] // chans * group
    for target in range(targets):
        for c in range(chans // group):
            rows = slice(c * tall, (c + 1) * tall)
            tile = jnp.concatenate(
                [x_ref[target, 0, s, rows, :] for x_ref in x_refs for s in range(2)], axis=0
            )
            value = jnp.dot(table_ref[...], tile, preferred_element_type=jnp.float32) * scale
            stage[target, :, c * group : (c + 1) * group] = value.reshape(
                2, group, total, LANES
            ).astype(jnp.bfloat16)
    for step, out_ref in enumerate(out_refs):
        out_ref[...] = stage[partner(at_ref[0], step, targets)]


def row_transform(parts, at, chans, rows_dev, length):
    steps = len(parts)
    targets = parts[0].shape[0]
    total = steps * rows_dev
    group = min(chans, max(1, 256 // (2 * total)))
    tables = jnp.asarray(row_tables(rows_dev, steps, group))
    table = lax.dynamic_index_in_dim(tables, at[1], 0, keepdims=False)
    vmem = pl.BlockSpec(memory_space=pltpu.VMEM)
    return pl.pallas_call(
        functools.partial(row_kernel, 1.0 / math.sqrt(total * length), group, steps),
        in_specs=[pl.BlockSpec(memory_space=pltpu.SMEM)] + [vmem] * (steps + 1),
        out_specs=[vmem] * targets,
        out_shape=[jax.ShapeDtypeStruct((2, chans, total, LANES), jnp.bfloat16)] * targets,
        scratch_shapes=[pltpu.VMEM((targets, 2, chans, total, LANES), jnp.bfloat16)],
        compiler_params=params(),
        name="row_transform",
    )(at, *parts, table)


def place_kernel(count, at_ref, *refs):
    x_refs, order_ref, out_ref, stage = refs[:count], refs[count], refs[-2], refs[-1]
    for step, x_ref in enumerate(x_refs):
        stage[partner(at_ref[0], step, count)] = x_ref[...].reshape(stage.shape[1:])
    tile = jnp.concatenate([stage[y_lo] for y_lo in range(count)], axis=1)
    value = jnp.dot(tile, order_ref[...], preferred_element_type=jnp.float32)
    out_ref[...] = value.astype(jnp.bfloat16).reshape(out_ref.shape)


def place(xs, at, chunk, count, held):
    _, chans, total, _ = xs[0].shape
    order = order_table()
    wide = RADIX * LANES
    block = math.gcd(chans, 4)
    return pl.pallas_call(
        functools.partial(place_kernel, len(xs)),
        grid=(chans // block,),
        in_specs=[pl.BlockSpec(memory_space=pltpu.SMEM)]
        + [pl.BlockSpec((2, block, total, LANES), lambda c: (0, c, 0, 0))] * len(xs)
        + [pl.BlockSpec(order.shape, lambda c: (0, 0))]
        + [pl.BlockSpec(memory_space=pl.ANY)] * len(held),
        out_specs=pl.BlockSpec((2, block, total, wide), lambda c: (0, c, 0, chunk)),
        out_shape=jax.ShapeDtypeStruct((2, chans, total, count * wide), jnp.bfloat16),
        scratch_shapes=[pltpu.VMEM((len(xs), 2 * block * total, LANES), jnp.bfloat16)],
        input_output_aliases={2 + len(xs): 0} if held else {},
        compiler_params=params(),
        name="place",
    )(at, *xs, jnp.asarray(order), *held)


def hold_kernel(*refs):
    pass


def hold(x, after):
    untouched = pl.BlockSpec(memory_space=pl.ANY)
    return pl.pallas_call(
        hold_kernel,
        in_specs=[untouched] * (1 + len(after)),
        out_specs=untouched,
        out_shape=jax.ShapeDtypeStruct(x.shape, x.dtype),
        input_output_aliases={0: 0},
        name="hold",
    )(x, *after)


def spread_rows(parts):
    count = len(parts)
    out = list(parts)
    for step in sorted(range(1, count), key=lambda n: -min(n, count - n)):
        out[step] = lax.ppermute(parts[step], "uv", [(z, (z + step) % count) for z in range(count)])
    return out


def turn_kernel(basis_ref, out_ref):
    out_ref[...] = basis_ref[...].T


def turn(basis):
    vmem = pl.BlockSpec(memory_space=pltpu.VMEM)
    return pl.pallas_call(
        turn_kernel,
        in_specs=[vmem],
        out_specs=vmem,
        out_shape=jax.ShapeDtypeStruct(basis.shape[::-1], basis.dtype),
        compiler_params=params(),
        name="turn",
    )(basis)


def exchange(x, axes):
    return lax.all_to_all(x, axes, split_axis=0, concat_axis=0, tiled=True)


def scatter(pieces):
    count = len(pieces)
    return [pieces[0]] + [
        lax.ppermute(
            pieces[step], "chan", [(j, int(partner(np.int32(j), step, count))) for j in range(count)]
        )
        for step in range(1, count)
    ]


def shards(visibility, eigen_basis, eigenvalues, noise_power):
    uv_count = lax.axis_size("uv")
    chan_count = lax.axis_size("chan")
    _, chans, rows_dev, length = visibility.shape
    count = length // chan_count // LANES
    targets = uv_count * chan_count
    at = jnp.stack([lax.axis_index("chan"), lax.axis_index("uv")]).astype(jnp.int32)
    basis = exchange(jnp.broadcast_to(eigen_basis, (chan_count,) + eigen_basis.shape), "chan")
    basis = basis.reshape(chan_count * chans, -1)
    basis_t = turn(basis)
    gain = eigenvalues[:, None] / (eigenvalues[:, None] + noise_power[None, :])
    flat = visibility.reshape(2, chans * rows_dev, length)
    rows_first = count > 3 and chan_count == RADIX
    whole = 3 if rows_first else 2
    first = column_transform(flat, at, chan_count, [(0, False)])
    cells = [[exchange(first[0], "chan")]]
    sends = []
    if count > 1:
        sends = list(
            column_transform(flat, at, chan_count, [(k, k >= whole) for k in range(1, count)])
        )
        sends[0] = hold(sends[0], [basis_t])
        cells.append([exchange(sends[0], "chan")])

    def cleaned_chunk(k, slot, slots, before, steps=1):
        return clean(
            at, cells[k], basis, basis_t, gain, targets, rows_dev, slot, slots, before, steps
        )

    before, lines = sends[:1], []
    groups = [[0]] + [g for g in (list(range(1, count - 1)), [count - 1]) if g and count > 1]
    if rows_first:
        groups = groups[1:]
        parts = spread_rows(cleaned_chunk(0, 0, 1, before, uv_count))
        before = []
        cells.append([exchange(hold(sends[1], [parts[uv_count // 2]]), "chan")])
        sends = sends[1:]
        lines = scatter(row_transform(parts, at, chans // uv_count, rows_dev, length))
    sends = sends[1:]
    for k in range(len(cells), count):
        cells.append(scatter(sends[:chan_count]))
        sends = sends[chan_count:]
    held = []
    for chunks in groups:
        if lines and chunks[-1] == count - 1:
            held = [place(lines, at, 0, count, held)]
        for slot, k in enumerate(chunks):
            if rows_first and k == 2:
                before = before + parts[1:]
            if rows_first and k == count - 1:
                before = before + lines[1:3]
            (cleaned,) = cleaned_chunk(k, slot, len(chunks), before)
            before = [cleaned]
        planes = exchange(cleaned, ("uv", "chan"))
        planes = planes.reshape((uv_count, chan_count) + planes.shape[1:])
        for slot, k in enumerate(chunks):
            held = [image(planes, slot, k, count, rows_dev, held)]
    return held[0]


def solution(mesh):
    in_specs = (P(None, "chan", "uv", None), P("chan", None), P(), P("uv"))
    out_specs = P(None, ("uv", "chan"), None, None)
    return jax.shard_map(shards, mesh=mesh, in_specs=in_specs, out_specs=out_specs, check_vma=False)
```
